32 devices in a mesh: node: 16 (over z, y, x), freq: 2 (over core).
Axes of the slice: x: 2, y: 2, z: 4, core: 2. Of those that a mesh axis runs over, the one named last changes fastest.
Arguments:
- excitation: float32 [2, 8, 16384], P(None, 'freq', 'node')
- g_blocks: float32 [128, 8, 128, 128], P('node', 'freq')
- c_blocks: float32 [128, 8, 128, 128], P('node', 'freq')
- pattern: int32 [128, 8], P('node'), may hold values from 0 to 127, as said below
- counts: int32 [128], P('node'), may hold values from 1 to 8, as said below
- freq_ids: int32 [8], P('freq'), may hold values from 0 to 999
Outputs:
- solution: float32 [2, 8, 16384], P(None, 'freq', 'node')
- residual_norm: float32 [8], P('freq')
The draws below stay inside these ranges and needn't reach their ends.
Inputs may be any that keep to these rules, and one draw needn't show every extreme that they name: `pattern`: slot 0 of row block b names b itself; the other slots name any row block, repeats allowed. `counts`: slots at or past a row block's count are padding and add nothing.
All inputs are finite; a program needn't handle non-finite values.
Results may differ from the reference program's by a relative error of at most 0.0001.
Values sent between devices are 32-bit elements; how exact they have to be, the bound alone decides.
No kernel may reach another device: no remote copies, remote signals or barrier semaphores. Data moves between devices by JAX's collectives and lax.ppermute only.
A program may use at most 64 MiB of HBM per device.

```python
import math
import jax
import jax.numpy as jnp
from jax import lax

BS = 128
KMAX = 8
ITERS = 3
NB = 128
N = 16384
NFREQ = 8


def draw_excitation(key, part):
    ramp = jnp.arange(N, dtype=jnp.float32) / max(N - 1, 1)
    values = jax.random.normal(key, (2, NFREQ, N), jnp.float32)
    return (values * (1.0 + 2.0 * ramp)).astype(jnp.float32)


def block_draw(key, diag_lo, diag_hi):
    spread = 0.8 / math.sqrt(BS * KMAX)
    values = jax.random.normal(jax.random.fold_in(key, 1), (NB, KMAX, BS, BS), jnp.float32)
    values = values * spread
    diagonal = jax.random.uniform(jax.random.fold_in(key, 2), (NB, BS), jnp.float32, diag_lo, diag_hi)
    identity = jnp.eye(BS, dtype=jnp.float32)
    return values.at[:, 0].add(diagonal[:, :, None] * identity[None, :, :])


def draw_g_blocks(key, part):
    return block_draw(jax.random.fold_in(key, 11), 1.5, 3.0)


def draw_c_blocks(key, part):
    return block_draw(jax.random.fold_in(key, 13), 0.5, 1.5)


def draw_pattern(key, part):
    chosen = jax.random.randint(jax.random.fold_in(key, 17), (NB, KMAX), 0, NB)
    return chosen.at[:, 0].set(jnp.arange(NB, dtype=jnp.int32)).astype(jnp.int32)


def draw_counts(key, part):
    chosen = jax.random.randint(jax.random.fold_in(key, 19), (NB,), 1, KMAX + 1)
    return chosen.at[0].set(KMAX).astype(jnp.int32)


def with_ends(drawn, rng, smallest, high):
    spot = [jax.random.randint(jax.random.fold_in(rng, axis), (), 0, length) for axis, length in enumerate(drawn.shape)]
    widest = drawn.shape.index(max(drawn.shape))
    next_to = spot[:widest] + [(spot[widest] + 1) % drawn.shape[widest]] + spot[widest + 1:]
    return drawn.at[tuple(spot)].set(smallest).at[tuple(next_to)].set(high)


def setup_inputs(seed: int = 0) -> dict:
    key_of = jax.random.split(jax.random.key(seed), 7)
    excitation = draw_excitation(jax.random.fold_in(key_of[6], 71), 0)
    g_blocks = draw_g_blocks(jax.random.fold_in(key_of[6], 71), 0)
    c_blocks = draw_c_blocks(jax.random.fold_in(key_of[6], 71), 0)
    pattern = draw_pattern(jax.random.fold_in(key_of[6], 71), 0)
    counts = draw_counts(jax.random.fold_in(key_of[6], 71), 0)
    freq_ids = with_ends(jax.random.randint(key_of[5], (NFREQ,), 0, 1000), jax.random.fold_in(key_of[5], 1), 0, 999).astype(jnp.int32)
    return dict(excitation=excitation, g_blocks=g_blocks, c_blocks=c_blocks, pattern=pattern, counts=counts, freq_ids=freq_ids)


def apply_operator(field, g_blocks, c_blocks, pattern, in_use, angular):
    blocks_view = field.reshape(2, NFREQ, NB, BS)
    picked = blocks_view[:, :, pattern, :] * in_use[None, None, :, :, None]
    gsum = jnp.einsum('bkij,cfbkj->cfbi', g_blocks, picked, precision=lax.Precision.HIGHEST).reshape(2, NFREQ, N)
    csum = jnp.einsum('bkij,cfbkj->cfbi', c_blocks, picked, precision=lax.Precision.HIGHEST).reshape(2, NFREQ, N)
    scaled = angular[:, None]
    return jnp.stack([gsum[0] - scaled * csum[1], gsum[1] + scaled * csum[0]])

def projected(first_vec, second_vec):
    return lax.optimization_barrier(jnp.sum(first_vec * second_vec, axis=(0, 2)))

def reference(excitation, g_blocks, c_blocks, pattern, counts, freq_ids):
    angular = 0.2 * jnp.exp(freq_ids.astype(jnp.float32) * (math.log(8.0) / 1000.0))
    in_use = (jnp.arange(KMAX)[None, :] < counts[:, None]).astype(jnp.float32)
    initial_norm = jnp.sqrt(projected(excitation, excitation))
    krylov = [excitation / initial_norm[None, :, None]]
    columns = []
    for iteration in range(ITERS):
        applied = apply_operator(krylov[iteration], g_blocks, c_blocks, pattern, in_use, angular)
        coeffs = [projected(vector, applied) for vector in krylov]
        for vector, weight in zip(krylov, coeffs):
            applied = applied - weight[None, :, None] * vector
        height = jnp.sqrt(projected(applied, applied))
        entries = coeffs + [height] + [jnp.zeros_like(height)] * (ITERS - 1 - iteration)
        columns.append(jnp.stack(entries, axis=1))
        if iteration + 1 < ITERS:
            krylov.append(applied / height[None, :, None])
    hessen = jnp.stack(columns, axis=2)
    normal = jnp.einsum('fim,fin->fmn', hessen, hessen, precision=lax.Precision.HIGHEST)
    right_side = initial_norm[:, None] * hessen[:, 0, :]
    factor = jnp.linalg.cholesky(normal)
    middle = jax.scipy.linalg.solve_triangular(factor, right_side[:, :, None], lower=True)
    coef_y = jax.scipy.linalg.solve_triangular(factor, middle, lower=True, trans=1)[:, :, 0]
    target = jnp.zeros((NFREQ, ITERS + 1), jnp.float32).at[:, 0].set(initial_norm)
    misfit = target - jnp.einsum('fim,fm->fi', hessen, coef_y, precision=lax.Precision.HIGHEST)
    residual_norm = jnp.sqrt(lax.optimization_barrier(jnp.sum(misfit * misfit, axis=1)))
    solution = jnp.zeros_like(excitation)
    for iteration in range(ITERS):
        solution = solution + coef_y[:, iteration][None, :, None] * krylov[iteration]
    return (solution, residual_norm)
```

```python
import math

import jax
import jax.numpy as jnp
from jax import lax
from jax.sharding import PartitionSpec as P

ITERS = 3
HIGHEST = lax.Precision.HIGHEST


def gather_rows(rows, nodes):
    return lax.all_to_all(jnp.broadcast_to(rows[None], (nodes,) + rows.shape), "node", 0, 0)


def dots(first_vec, second_vec):
    return jnp.sum(first_vec * second_vec, axis=(0, 1, 3))


def swap_slots(blocks, freqs):
    return [blocks] + [
        lax.ppermute(blocks, "freq", [(i, (i + d) % freqs) for i in range(freqs)])
        for d in range(1, freqs)
    ]


def make_shards(nodes, freqs):
    def shards(excitation, g_blocks, c_blocks, pattern, counts, freq_ids):
        angular = 0.2 * jnp.exp(freq_ids.astype(jnp.float32) * (math.log(8.0) / 1000.0))
        row_blocks, slots = pattern.shape
        block_rows = g_blocks.shape[2]
        own_slots = g_blocks.shape[1]
        freq_count = excitation.shape[1]
        g_parts = swap_slots(g_blocks, freqs)
        c_parts = swap_slots(c_blocks, freqs)
        node = lax.axis_index("node")
        freq = lax.axis_index("freq")
        in_use = jnp.arange(slots)[None, :] < counts[:, None]
        portion_blocks = nodes * row_blocks
        block_ids = jnp.arange(portion_blocks, dtype=jnp.int32)
        select = ((pattern[:, :, None] == block_ids[None, None, :]) & in_use[:, :, None]).astype(
            jnp.float32
        )
        selects = [
            lax.dynamic_slice_in_dim(select, lax.rem(freq - d + freqs, freqs) * own_slots, own_slots, 1)
            for d in range(freqs)
        ]

        def apply(full):
            blocks = full.reshape(nodes, 2, freq_count, row_blocks, block_rows)
            blocks = blocks.transpose(0, 3, 1, 2, 4).reshape(portion_blocks, 2, freq_count, block_rows)
            gsum = csum = 0.0
            for chosen, g_part, c_part in zip(selects, g_parts, c_parts):
                picked = jnp.einsum("bkp,pcfj->bkcfj", chosen, blocks, precision=HIGHEST)
                gsum += jnp.einsum("bkij,bkcfj->cfbi", g_part, picked, precision=HIGHEST)
                csum += jnp.einsum("bkij,bkcfj->cfbi", c_part, picked, precision=HIGHEST)
            gsum = gsum.reshape(2, freq_count, row_blocks * block_rows)
            csum = csum.reshape(2, freq_count, row_blocks * block_rows)
            scaled = angular[:, None]
            return jnp.stack([gsum[0] - scaled * csum[1], gsum[1] + scaled * csum[0]])

        whole = gather_rows(excitation, nodes)
        initial_norm = jnp.sqrt(dots(whole, whole))
        whole = whole / initial_norm[:, None]
        krylov_full = [whole]
        krylov = [excitation / initial_norm[:, None]]
        columns = []
        zero = jnp.zeros_like(initial_norm)
        for iteration in range(ITERS - 1):
            local = apply(krylov_full[-1])
            full = gather_rows(local, nodes)
            coeffs = [dots(vector, full) for vector in krylov_full]
            for vector, mine, weight in zip(krylov_full, krylov, coeffs):
                full = full - weight[:, None] * vector
                local = local - weight[:, None] * mine
            height = jnp.sqrt(dots(full, full))
            krylov_full.append(full / height[:, None])
            krylov.append(local / height[:, None])
            columns.append(jnp.stack(coeffs + [height] + [zero] * (ITERS - 1 - iteration), axis=1))
        local = apply(krylov_full[-1])
        partial = jnp.stack([jnp.sum(v * local, axis=(0, 2)) for v in krylov + [local]])
        mine = (jnp.arange(freqs) == freq).astype(jnp.float32)
        sums = lax.psum(mine[:, None, None] * partial[None], ("node", "freq"))
        sums = lax.dynamic_index_in_dim(sums, freq, 0, keepdims=False)
        square = sums[ITERS] - jnp.sum(sums[:ITERS] ** 2, axis=0)
        height = jnp.sqrt(jnp.maximum(square, 0.0))
        columns.append(jnp.stack([sums[i] for i in range(ITERS)] + [height], axis=1))
        hessen = jnp.stack(columns, axis=2)
        normal = [
            [jnp.sum(hessen[:, :, m] * hessen[:, :, n], axis=1) for n in range(ITERS)]
            for m in range(ITERS)
        ]
        right_side = [initial_norm * hessen[:, 0, m] for m in range(ITERS)]
        low = [[None] * ITERS for _ in range(ITERS)]
        middle = []
        for m in range(ITERS):
            for n in range(m):
                rest = normal[m][n] - sum(low[m][k] * low[n][k] for k in range(n))
                low[m][n] = rest / low[n][n]
            low[m][m] = jnp.sqrt(normal[m][m] - sum(low[m][k] * low[m][k] for k in range(m)))
            middle.append((right_side[m] - sum(low[m][k] * middle[k] for k in range(m))) / low[m][m])
        coef_y = [None] * ITERS
        for m in reversed(range(ITERS)):
            rest = middle[m] - sum(low[k][m] * coef_y[k] for k in range(m + 1, ITERS))
            coef_y[m] = rest / low[m][m]
        misfit = [
            (initial_norm if i == 0 else 0.0) - sum(hessen[:, i, m] * coef_y[m] for m in range(ITERS))
            for i in range(ITERS + 1)
        ]
        residual_norm = jnp.sqrt(sum(m * m for m in misfit))
        solution = sum(y[:, None] * v for y, v in zip(coef_y, krylov))
        return (solution, residual_norm)

    return shards


def solution(mesh):
    in_specs = (
        P(None, "freq", "node"),
        P("node", "freq", None, None),
        P("node", "freq", None, None),
        P("node", None),
        P("node"),
        P("freq"),
    )
    out_specs = (P(None, "freq", "node"), P("freq"))
    shards = make_shards(mesh.shape["node"], mesh.shape["freq"])
    return jax.shard_map(shards, mesh=mesh, in_specs=in_specs, out_specs=out_specs, check_vma=False)
```

```python
import math

import jax
import jax.numpy as jnp
from jax import lax
from jax.sharding import PartitionSpec as P

ITERS = 3
HIGHEST = lax.Precision.HIGHEST


def split_nodes(nodes):
    plane = 4 if nodes % 4 == 0 else 1
    return nodes // plane, plane


def gather_rows(rows, nodes):
    line, plane = split_nodes(nodes)
    held = [rows]
    for d in range(1, line):
        perm = [(i, (i + d * plane) % nodes) for i in range(nodes)]
        held.append(lax.ppermute(rows, "node", perm))
    whole_line = jnp.stack(held)
    held = [whole_line]
    for d in range(1, plane):
        perm = [(i, (i // plane) * plane + ((i % plane) ^ d)) for i in range(nodes)]
        held.append(lax.ppermute(whole_line, "node", perm))
    return jnp.stack(held)


def gathered_place(owner, node, nodes):
    line, plane = split_nodes(nodes)
    far = lax.rem(node // plane - owner // plane + line, line)
    return ((node % plane) ^ (owner % plane)) * line + far


def dots(first_vec, second_vec):
    return both_parts(jnp.sum(first_vec * second_vec, axis=(0, 1, 3)))


def both_parts(sums):
    half = sums.shape[-1] // 2
    total = sums[..., :half] + sums[..., half:]
    return jnp.concatenate([total, total], axis=-1)


def swap_slots(blocks, freqs):
    return [blocks] + [
        lax.ppermute(blocks, "freq", [(i, (i + d) % freqs) for i in range(freqs)])
        for d in range(1, freqs)
    ]


def make_shards(nodes, freqs):
    def shards(excitation, g_blocks, c_blocks, pattern, counts, freq_ids):
        angular = 0.2 * jnp.exp(freq_ids.astype(jnp.float32) * (math.log(8.0) / 1000.0))
        row_blocks, slots = pattern.shape
        block_rows = g_blocks.shape[2]
        own_slots = g_blocks.shape[1]
        freq_count = excitation.shape[1]
        g_parts = swap_slots(g_blocks, freqs)
        c_parts = swap_slots(c_blocks, freqs)
        node = lax.axis_index("node")
        freq = lax.axis_index("freq")
        in_use = jnp.arange(slots)[None, :] < counts[:, None]
        portion_blocks = nodes * row_blocks
        block_ids = jnp.arange(portion_blocks, dtype=jnp.int32)
        owner = pattern // row_blocks
        place = gathered_place(owner, node, nodes) * row_blocks + pattern % row_blocks
        select = ((place[:, :, None] == block_ids[None, None, :]) & in_use[:, :, None]).astype(
            jnp.float32
        )
        selects = [
            lax.dynamic_slice_in_dim(select, lax.rem(freq - d + freqs, freqs) * own_slots, own_slots, 1)
            for d in range(freqs)
        ]
        rows = excitation.reshape(2 * freq_count, row_blocks * block_rows)
        turn = jnp.concatenate([-angular, angular])[:, None]

        def apply(full):
            blocks = full.reshape(nodes, 2 * freq_count, row_blocks, block_rows)
            blocks = blocks.transpose(0, 2, 1, 3).reshape(portion_blocks, 2 * freq_count, block_rows)
            gsum = csum = 0.0
            for chosen, g_part, c_part in zip(selects, g_parts, c_parts):
                picked = jnp.einsum("bkp,pfj->bkfj", chosen, blocks, precision=HIGHEST)
                gsum += jnp.einsum("bkij,bkfj->fbi", g_part, picked, precision=HIGHEST)
                csum += jnp.einsum("bkij,bkfj->fbi", c_part, picked, precision=HIGHEST)
            gsum = gsum.reshape(rows.shape)
            csum = csum.reshape(rows.shape)
            other = jnp.concatenate([csum[freq_count:], csum[:freq_count]])
            return gsum + turn * other

        whole = gather_rows(rows, nodes)
        initial_norm = jnp.sqrt(dots(whole, whole))
        whole = whole / initial_norm[:, None]
        krylov_full = [whole]
        krylov = [rows / initial_norm[:, None]]
        columns = []
        zero = jnp.zeros_like(initial_norm)
        for iteration in range(ITERS - 1):
            local = apply(krylov_full[-1])
            full = gather_rows(local, nodes)
            coeffs = [dots(vector, full) for vector in krylov_full]
            for vector, mine, weight in zip(krylov_full, krylov, coeffs):
                full = full - weight[:, None] * vector
                local = local - weight[:, None] * mine
            height = jnp.sqrt(dots(full, full))
            krylov_full.append(full / height[:, None])
            krylov.append(local / height[:, None])
            columns.append(jnp.stack(coeffs + [height] + [zero] * (ITERS - 1 - iteration), axis=1))
        local = apply(krylov_full[-1])
        partial = jnp.stack([jnp.sum(v * local, axis=1) for v in krylov + [local]])
        copies = jnp.broadcast_to(partial[None], (nodes,) + partial.shape)
        sums = both_parts(jnp.sum(lax.all_to_all(copies, "node", 0, 0), axis=0))
        square = sums[ITERS] - jnp.sum(sums[:ITERS] ** 2, axis=0)
        height = jnp.sqrt(jnp.maximum(square, 0.0))
        columns.append(jnp.stack([sums[i] for i in range(ITERS)] + [height], axis=1))
        hessen = jnp.stack(columns, axis=2)
        normal = [
            [jnp.sum(hessen[:, :, m] * hessen[:, :, n], axis=1) for n in range(ITERS)]
            for m in range(ITERS)
        ]
        right_side = [initial_norm * hessen[:, 0, m] for m in range(ITERS)]
        low = [[None] * ITERS for _ in range(ITERS)]
        middle = []
        for m in range(ITERS):
            for n in range(m):
                rest = normal[m][n] - sum(low[m][k] * low[n][k] for k in range(n))
                low[m][n] = rest / low[n][n]
            low[m][m] = jnp.sqrt(normal[m][m] - sum(low[m][k] * low[m][k] for k in range(m)))
            middle.append((right_side[m] - sum(low[m][k] * middle[k] for k in range(m))) / low[m][m])
        coef_y = [None] * ITERS
        for m in reversed(range(ITERS)):
            rest = middle[m] - sum(low[k][m] * coef_y[k] for k in range(m + 1, ITERS))
            coef_y[m] = rest / low[m][m]
        misfit = [
            (initial_norm if i == 0 else 0.0) - sum(hessen[:, i, m] * coef_y[m] for m in range(ITERS))
            for i in range(ITERS + 1)
        ]
        residual_norm = jnp.sqrt(sum(m * m for m in misfit))
        solution = sum(y[:, None] * v for y, v in zip(coef_y, krylov))
        return (solution.reshape(excitation.shape), residual_norm[:freq_count])

    return shards


def solution(mesh):
    in_specs = (
        P(None, "freq", "node"),
        P("node", "freq", None, None),
        P("node", "freq", None, None),
        P("node", None),
        P("node"),
        P("freq"),
    )
    out_specs = (P(None, "freq", "node"), P("freq"))
    shards = make_shards(mesh.shape["node"], mesh.shape["freq"])
    return jax.shard_map(shards, mesh=mesh, in_specs=in_specs, out_specs=out_specs, check_vma=False)
```

```python
import functools
import math

import jax
import jax.numpy as jnp
from jax import lax
from jax.experimental import pallas as pl
from jax.experimental.pallas import tpu as pltpu
from jax.sharding import PartitionSpec as P

ITERS = 3
LANES = 128
GROUP = 8
VMEM_LIMIT = 40 * 1024 * 1024
SIDE = 2


def split_nodes(nodes):
    plane = 4 if nodes % 4 == 0 else 1
    return nodes // plane, plane


def gather_rows(rows, nodes, parts):
    line, plane = split_nodes(nodes)
    held = [rows]
    for d in range(1, line):
        perm = [(i, (i + d * plane) % nodes) for i in range(nodes)]
        held.append(lax.ppermute(rows, "node", perm))
    whole_line = jnp.stack(held).reshape(line, parts, rows.shape[-1])
    held = [whole_line]
    for d in range(1, plane):
        perm = [(i, (i // plane) * plane + ((i % plane) ^ d)) for i in range(nodes)]
        held.append(lax.ppermute(whole_line, "node", perm))
    return held


def gathered_place(owner, node, nodes):
    line, plane = split_nodes(nodes)
    far = lax.rem(node // plane - owner // plane + line, line)
    return ((node % plane) ^ (owner % plane)) * line + far


def work_list(pattern, counts, node, freq, nodes, freqs):
    row_blocks, slots = pattern.shape
    own_slots = slots // freqs
    total = row_blocks * slots
    place = gathered_place(pattern // row_blocks, node, nodes) * row_blocks + pattern % row_blocks
    b = lax.broadcasted_iota(jnp.int32, (row_blocks, slots), 0)
    k = lax.broadcasted_iota(jnp.int32, (row_blocks, slots), 1)
    away = lax.rem(freq - k // own_slots + freqs, freqs)
    stored = (away * row_blocks + b) * own_slots + k % own_slots
    counts = jnp.clip(counts, 0, slots)
    before = jnp.sum(
        jnp.where(jnp.arange(row_blocks)[None, :] < jnp.arange(row_blocks)[:, None], counts[None, :], 0), axis=1
    )
    spot = jnp.where(k < counts[:, None], before[:, None] + k, total).reshape(-1)
    used = jnp.sum(counts)
    order = jnp.arange(total)
    values = jnp.stack([place, stored, b]).reshape(3, total)
    hit = spot[None, None, :] == order[None, :, None]
    packed = jnp.sum(jnp.where(hit, values[:, None, :], 0), axis=2)
    empty = jnp.where(order >= used, nodes * row_blocks, 0)
    groups = jnp.full((1, total), (used + GROUP - 1) // GROUP, jnp.int32)
    return jnp.concatenate([packed.at[0].add(empty), groups]).astype(jnp.int32)


def prepare_kernel(g_ref, c_ref, *rest):
    out_ref = rest[-1]
    size = g_ref.shape[-1]
    for slot in range(g_ref.shape[1]):
        for m, ref in enumerate((g_ref, c_ref)):
            x = ref[0, slot]
            high = x.astype(jnp.bfloat16)
            low = (x - high.astype(jnp.float32)).astype(jnp.bfloat16)
            out_ref[0, 0, slot, m * size : (m + 1) * size, :size] = high
            out_ref[0, 0, slot, m * size : (m + 1) * size, size:] = low


def prepare(g_part, c_part, away, freqs, into):
    row_blocks, own_slots, size, _ = g_part.shape
    shape = (freqs, row_blocks, own_slots, 2 * size, SIDE * size)
    block = pl.BlockSpec((1, own_slots, size, size), lambda b: (b, 0, 0, 0))
    operands, in_specs, aliases = [g_part, c_part], [block, block], {}
    if into is not None:
        operands.append(into)
        in_specs.append(pl.BlockSpec(memory_space=pl.ANY))
        aliases = {2: 0}
    return pl.pallas_call(
        prepare_kernel,
        grid=(row_blocks,),
        in_specs=in_specs,
        out_specs=pl.BlockSpec((1, 1) + shape[2:], lambda b: (away, b, 0, 0, 0)),
        out_shape=jax.ShapeDtypeStruct(shape, jnp.bfloat16),
        input_output_aliases=aliases,
        cost_estimate=pl.CostEstimate(
            flops=8 * g_part.size, bytes_accessed=16 * g_part.size, transcendentals=0
        ),
        name=f"prepare_{away}",
    )(*operands)


def lane_sum(x):
    return jnp.sum(x, axis=1, keepdims=True)


def with_other_part(column):
    wide = jnp.broadcast_to(column, (column.shape[0], LANES))
    return wide + pltpu.roll(wide, column.shape[0] // 2, 0)


def put_lane(tile, lane, column):
    at = lax.broadcasted_iota(jnp.int32, tile.shape, 1) == lane
    return jnp.where(at, column, tile)


def step_kernel(step, plane, line, items_ref, turn_ref, info_in_ref, *refs):
    lines = refs[:plane]
    prev = refs[plane : plane + step]
    w_ref, z_ref, own_ref, local_ref, info_ref, tile_ref, split_ref, acc_ref, held_ref, sems = refs[plane + step :]
    nodes = plane * line
    parts, rows = local_ref.shape
    row_blocks = acc_ref.shape[0]
    size = rows // row_blocks
    groups = items_ref[3, 0]

    def fetch(t):
        return pltpu.make_async_copy(w_ref.at[items_ref[1, t]], held_ref.at[t], sems.at[t])

    @pl.loop(0, groups * GROUP)
    def _(t):
        fetch(t).start()

    split_ref[nodes * row_blocks] = jnp.zeros(split_ref.shape[1:], split_ref.dtype)
    acc_ref[...] = jnp.zeros_like(acc_ref)

    def chunks(body, carry):
        for q in range(plane):
            carry = lax.fori_loop(
                0, line, lambda i, c, q=q: body(q, i, q * line + i, c), carry, unroll=line <= 4
            )
        return carry

    zero = jnp.zeros((parts, rows), jnp.float32)
    info = info_in_ref[...]
    if step == 0:

        def square(q, i, at, total):
            x = lines[q][i]
            return total + x * x

        height = jnp.sqrt(with_other_part(lane_sum(chunks(square, zero))))
        info = put_lane(info, 0, height)
        source = lambda q, i, at: lines[q][i]
    else:

        def dot(q, i, at, totals):
            x = lines[q][i]
            return tuple(s + p[at] * x for s, p in zip(totals, prev))

        sums = chunks(dot, (zero,) * step)
        coeffs = [with_other_part(lane_sum(s)) for s in sums]
        first = 1 if step == 1 else 3
        for i, coeff in enumerate(coeffs):
            info = put_lane(info, first + i, coeff)
        wide = [jnp.tile(coeff, (1, rows // LANES)) for coeff in coeffs]

        def subtract(q, i, at, total):
            x = lines[q][i]
            for coeff, p in zip(wide, prev):
                x = x - coeff * p[at]
            z_ref[at] = x
            return total + x * x

        height = jnp.sqrt(with_other_part(lane_sum(chunks(subtract, zero))))
        info = put_lane(info, first + step, height)
        source = lambda q, i, at: z_ref[at]
    info_ref[...] = info
    height = jnp.tile(height, (1, rows // LANES))

    def spread(q, i, at, carry):
        z = source(q, i, at) / height
        z_ref[at] = z
        high = z.astype(jnp.bfloat16).astype(jnp.float32)
        both = jnp.concatenate([high, z - high], axis=0).astype(jnp.bfloat16)
        for b in range(row_blocks):
            split_ref[at * row_blocks + b] = both[:, b * size : (b + 1) * size]
        return carry

    chunks(spread, 0)
    own_ref[...] = z_ref[0]

    @pl.loop(0, groups)
    def _(group):
        for u in range(GROUP):
            t = group * GROUP + u
            fetch(t).wait()
        for u in range(GROUP):
            t = group * GROUP + u
            v = split_ref[items_ref[0, t]]
            v = jnp.concatenate([v, v], axis=1)
            product = lax.dot_general(
                v, held_ref[t], (((1,), (1,)), ((), ())), preferred_element_type=jnp.float32
            )
            acc_ref[items_ref[2, t]] += product

    turn = turn_ref[...]
    for b in range(row_blocks):
        total = acc_ref[b]
        total = total[:parts] + total[parts:]
        other = pltpu.roll(total[:, size:], parts // 2, 0)
        local_ref[:, b * size : (b + 1) * size] = total[:, :size] + turn * other

    tile = jnp.zeros((parts, LANES), jnp.float32)
    if step == ITERS - 1:
        w = local_ref[...]
        zs = [p[0] for p in prev] + [z_ref[0]]
        values = [lane_sum(z * w) for z in zs]
        gram = [[lane_sum(zs[i] * zs[j]) for j in range(i + 1)] for i in range(ITERS)]
        shares = []
        for i, z in enumerate(zs):
            along = lane_sum(z * w) if i else values[0]
            share = jnp.where(gram[i][i] > 0.0, along / gram[i][i], 0.0)
            shares.append(share)
            w = w - share * z
        values += shares + [lane_sum(z * w) for z in zs] + [lane_sum(w * w)]
        values += [gram[i][j] for i in range(ITERS) for j in range(i + 1)]
        for lane, value in enumerate(values):
            tile = put_lane(tile, lane, value)
    tile_ref[...] = tile


def run_step(step, items, turn, info, lines, prev, blocks, row_blocks):
    plane = len(lines)
    line, parts, rows = lines[0].shape
    nodes = plane * line
    size = rows // row_blocks
    total = items.shape[1]
    vmem = pl.BlockSpec(memory_space=pltpu.VMEM)
    tile = jax.ShapeDtypeStruct((parts, LANES), jnp.float32)
    return pl.pallas_call(
        functools.partial(step_kernel, step, plane, line),
        in_specs=[pl.BlockSpec(memory_space=pltpu.SMEM)]
        + [vmem] * (2 + plane + step)
        + [pl.BlockSpec(memory_space=pl.ANY)],
        out_specs=[vmem] * 5,
        out_shape=[
            jax.ShapeDtypeStruct((nodes, parts, rows), jnp.float32),
            jax.ShapeDtypeStruct((parts, rows), jnp.float32),
            jax.ShapeDtypeStruct((parts, rows), jnp.float32),
            tile,
            tile,
        ],
        scratch_shapes=[
            pltpu.VMEM((nodes * row_blocks + 1, SIDE * parts, size), jnp.bfloat16),
            pltpu.VMEM((row_blocks, SIDE * parts, 2 * size), jnp.float32),
            pltpu.VMEM((total, 2 * size, SIDE * size), jnp.bfloat16),
            pltpu.SemaphoreType.DMA((total,)),
        ],
        compiler_params=pltpu.CompilerParams(vmem_limit_bytes=VMEM_LIMIT),
        cost_estimate=pl.CostEstimate(
            flops=2 * total * SIDE * parts * 2 * size * SIDE * size,
            bytes_accessed=blocks.size * 2,
            transcendentals=0,
        ),
        name=f"step_{step}",
    )(items, turn, info, *lines, *prev, blocks)


def final_kernel(plane, line, info_ref, *refs):
    tiles = refs[:plane]
    krylov = refs[plane : plane + ITERS]
    out_ref, residual_ref = refs[plane + ITERS :]
    parts = info_ref.shape[0]
    fit = LANES // parts
    stacked = [tiles[q][i] for q in range(plane) for i in range(line)]
    sets = [
        jnp.transpose(jnp.concatenate(stacked[at : at + fit], axis=0)) for at in range(0, len(stacked), fit)
    ]
    info = jnp.transpose(jnp.concatenate([info_ref[...]] * fit, axis=0))

    def all_devices(shares):
        total = sum(shares[1:], shares[0])
        step = parts // 2
        while step < LANES:
            total = total + pltpu.roll(total, step, 1)
            step *= 2
        return total

    def row(table, at):
        return jnp.broadcast_to(table[at : at + 1], (8, LANES))

    zero = jnp.zeros((8, LANES), jnp.float32)
    norm, h00, h10, h01, h11, h21 = [row(info, i) for i in range(6)]
    last = [all_devices([row(s, i) for s in sets]) for i in range(ITERS)]
    shares = []
    for s in sets:
        off = [last[i] - row(s, ITERS + i) for i in range(ITERS)]
        square = row(s, 3 * ITERS)
        at = 3 * ITERS + 1
        for i in range(ITERS):
            square = square - 2.0 * off[i] * row(s, 2 * ITERS + i)
            for j in range(i + 1):
                square = square + (1.0 if i == j else 2.0) * off[i] * off[j] * row(s, at)
                at += 1
        shares.append(square)
    height = jnp.sqrt(jnp.maximum(all_devices(shares), 0.0))
    hessen = [[h00, h01, last[0]], [h10, h11, last[1]], [zero, h21, last[2]], [zero, zero, height]]
    normal = [[sum(h[m] * h[n] for h in hessen) for n in range(ITERS)] for m in range(ITERS)]
    low = [[None] * ITERS for _ in range(ITERS)]
    middle = []
    for m in range(ITERS):
        for n in range(m):
            rest = normal[m][n] - sum((low[m][k] * low[n][k] for k in range(n)), zero)
            low[m][n] = rest / low[n][n]
        low[m][m] = jnp.sqrt(normal[m][m] - sum((low[m][k] * low[m][k] for k in range(m)), zero))
        rest = norm * hessen[0][m] - sum((low[m][k] * middle[k] for k in range(m)), zero)
        middle.append(rest / low[m][m])
    coef_y = [None] * ITERS
    for m in reversed(range(ITERS)):
        rest = middle[m] - sum((low[k][m] * coef_y[k] for k in range(m + 1, ITERS)), zero)
        coef_y[m] = rest / low[m][m]
    total = zero
    for i, h in enumerate(hessen):
        misfit = (norm if i == 0 else zero) - sum(h[m] * coef_y[m] for m in range(ITERS))
        total = total + misfit * misfit
    residual_ref[...] = jnp.sqrt(total)
    columns = jnp.transpose(
        jnp.concatenate([y for y in coef_y] + [jnp.zeros((LANES - 8 * ITERS, LANES), jnp.float32)], axis=0)
    )[:parts]
    x = sum(columns[:, 8 * m : 8 * m + 1] * krylov[m][...] for m in range(ITERS))
    out_ref[0] = x[: parts // 2]
    out_ref[1] = x[parts // 2 :]


def run_final(info, tiles, krylov):
    plane = len(tiles)
    line, parts, _ = tiles[0].shape
    rows = krylov[0].shape[-1]
    vmem = pl.BlockSpec(memory_space=pltpu.VMEM)
    return pl.pallas_call(
        functools.partial(final_kernel, plane, line),
        in_specs=[vmem] * (1 + plane + ITERS),
        out_specs=[vmem] * 2,
        out_shape=[
            jax.ShapeDtypeStruct((2, parts // 2, rows), jnp.float32),
            jax.ShapeDtypeStruct((8, LANES), jnp.float32),
        ],
        name="final",
    )(info, *tiles, *krylov)


def make_shards(nodes, freqs):
    def shards(excitation, g_blocks, c_blocks, pattern, counts, freq_ids):
        angular = 0.2 * jnp.exp(freq_ids.astype(jnp.float32) * (math.log(8.0) / 1000.0))
        row_blocks, slots = pattern.shape
        size = g_blocks.shape[2]
        own_slots = g_blocks.shape[1]
        freq_count = excitation.shape[1]
        parts = 2 * freq_count
        node = lax.axis_index("node")
        freq = lax.axis_index("freq")
        blocks = None
        for d in range(freqs):
            perm = [(i, (i + d) % freqs) for i in range(freqs)]
            g_part = lax.ppermute(g_blocks, "freq", perm) if d else g_blocks
            c_part = lax.ppermute(c_blocks, "freq", perm) if d else c_blocks
            blocks = prepare(g_part, c_part, d, freqs, blocks)
        blocks = blocks.reshape(freqs * row_blocks * own_slots, 2 * size, SIDE * size)
        items = work_list(pattern, counts, node, freq, nodes, freqs)
        turn = jnp.broadcast_to(jnp.concatenate([-angular, angular])[:, None], (parts, LANES))
        info = jnp.zeros((parts, LANES), jnp.float32)
        krylov, own = [], []
        rows = excitation
        for step in range(ITERS):
            lines = gather_rows(rows, nodes, parts)
            z, mine, rows, info, tile = run_step(step, items, turn, info, lines, krylov, blocks, row_blocks)
            krylov.append(z)
            own.append(mine)
        tiles = gather_rows(tile, nodes, parts)
        answer, residual = run_final(info, tiles, own)
        return answer, residual[0, :freq_count]

    return shards


def solution(mesh):
    in_specs = (
        P(None, "freq", "node"),
        P("node", "freq", None, None),
        P("node", "freq", None, None),
        P("node", None),
        P("node"),
        P("freq"),
    )
    out_specs = (P(None, "freq", "node"), P("freq"))
    shards = make_shards(mesh.shape["node"], mesh.shape["freq"])
    return jax.shard_map(shards, mesh=mesh, in_specs=in_specs, out_specs=out_specs, check_vma=False)
```

```python
import functools
import math

import jax
import jax.numpy as jnp
from jax import lax
from jax.experimental import pallas as pl
from jax.experimental.pallas import tpu as pltpu
from jax.sharding import PartitionSpec as P

ITERS = 3
LANES = 128
GROUP = 4
VMEM_LIMIT = 20 * 1024 * 1024


def split_nodes(nodes):
    plane = 4 if nodes % 4 == 0 else 1
    return nodes // plane, plane


def gather_rows(rows, nodes, parts):
    line, plane = split_nodes(nodes)
    held = [rows]
    for d in range(1, line):
        perm = [(i, (i + d * plane) % nodes) for i in range(nodes)]
        held.append(lax.ppermute(rows, "node", perm))
    whole_line = jnp.stack(held).reshape(line, parts, rows.shape[-1])
    held = [whole_line]
    for d in range(1, plane):
        perm = [(i, (i // plane) * plane + ((i % plane) ^ d)) for i in range(nodes)]
        held.append(lax.ppermute(whole_line, "node", perm))
    return held


def gathered_place(owner, node, nodes):
    line, plane = split_nodes(nodes)
    far = lax.rem(node // plane - owner // plane + line, line)
    return ((node % plane) ^ (owner % plane)) * line + far


def work_list(pattern, counts, node, freq, nodes, freqs):
    row_blocks, slots = pattern.shape
    own_slots = slots // freqs
    total = row_blocks * own_slots
    place = gathered_place(pattern // row_blocks, node, nodes) * row_blocks + pattern % row_blocks
    slot = jnp.arange(slots)
    places = jnp.where(slot[None, :] < counts[:, None], place, nodes * row_blocks).T
    order = jnp.arange(total)
    b = jnp.arange(row_blocks)
    tables = []
    for d in range(freqs):
        first = lax.rem(freq - d + freqs, freqs) * own_slots
        here = jnp.clip(counts - first, 0, own_slots)
        start = jnp.sum(jnp.where(b[None, :] < b[:, None], here[None, :], 0), axis=1)
        inside = order[:, None] - start[None, :]
        hit = (inside >= 0) & (inside < here[None, :])
        inside = jnp.sum(jnp.where(hit, inside, 0), axis=1)
        used = jnp.sum(here)
        block = jnp.sum(jnp.where(hit, b[None, :], 0), axis=1)
        groups = jnp.full((total,), (used + GROUP - 1) // GROUP)
        stored = block * own_slots + inside
        block = jnp.where(order < used, block, row_blocks)
        tables += [first + inside, block, stored, groups]
    return jnp.stack(tables).astype(jnp.int32), places.astype(jnp.int32)


def lane_sum(x):
    return jnp.sum(x, axis=1, keepdims=True)


def with_other_part(column):
    wide = jnp.broadcast_to(column, (column.shape[0], LANES))
    return wide + pltpu.roll(wide, column.shape[0] // 2, 0)


def put_lane(tile, lane, column):
    at = lax.broadcasted_iota(jnp.int32, tile.shape, 1) == lane
    return jnp.where(at, column, tile)


def split(x):
    high = x.astype(jnp.bfloat16)
    return high, (x - high.astype(jnp.float32)).astype(jnp.bfloat16)


def step_kernel(step, plane, line, freqs, items_ref, places_ref, turn_ref, info_in_ref, *refs):
    lines = refs[:plane]
    refs = refs[plane:]
    prev = refs[:step]
    g_refs = refs[step : step + freqs]
    c_refs = refs[step + freqs : step + 2 * freqs]
    z_ref, own_ref, local_ref, info_ref, tile_ref, layer_ref, mask_ref, acc_ref = refs[step + 2 * freqs :]
    nodes = plane * line
    parts, rows = local_ref.shape
    slots, row_blocks = places_ref.shape
    size = rows // row_blocks

    lane = lax.broadcasted_iota(jnp.int32, (size, LANES), 1)
    for b in range(row_blocks):
        mask_ref[b] = jnp.where((lane // parts) % row_blocks == b, 1.0, 0.0).astype(jnp.bfloat16)
    mask_ref[row_blocks] = jnp.zeros((size, LANES), jnp.bfloat16)
    acc_ref[...] = jnp.zeros_like(acc_ref)
    z_ref[nodes * row_blocks] = jnp.zeros((parts, size), jnp.float32)

    def blocks(body, carry):
        for q in range(plane):

            def chunk(i, carry, q=q):
                x = lines[q][i]
                for b in range(row_blocks):
                    carry = body(b, x[:, b * size : (b + 1) * size], (q * line + i) * row_blocks + b, carry)
                return carry

            if line <= 4:
                for i in range(line):
                    carry = chunk(i, carry)
            else:
                carry = lax.fori_loop(0, line, chunk, carry)
        return carry

    def add(sums, b, term):
        return sums[:b] + (sums[b] + term,) + sums[b + 1 :]

    def whole(sums):
        while len(sums) > 1:
            sums = tuple(x + y for x, y in zip(sums[::2], sums[1::2])) + sums[len(sums) // 2 * 2 :]
        return with_other_part(lane_sum(sums[0]))

    none = (jnp.zeros((parts, size), jnp.float32),) * row_blocks
    info = info_in_ref[...]
    if step == 0:
        height = jnp.sqrt(whole(blocks(lambda b, x, at, sums: add(sums, b, x * x), none)))
        info = put_lane(info, 0, height)

        def normal(b, x, at, carry):
            z_ref[at] = x / height
            return carry
    else:
        first = 1 if step == 1 else 3

        def dot(b, x, at, sums):
            return tuple(add(s, b, p[at] * x) for s, p in zip(sums, prev))

        coeffs = [whole(s) for s in blocks(dot, (none,) * step)]
        for i, coeff in enumerate(coeffs):
            info = put_lane(info, first + i, coeff)

        def subtract(b, x, at, sums):
            for coeff, p in zip(coeffs, prev):
                x = x - coeff * p[at]
            z_ref[at] = x
            return add(sums, b, x * x)

        height = jnp.sqrt(whole(blocks(subtract, none)))
        info = put_lane(info, first + step, height)

        def normal(b, x, at, carry):
            z_ref[at] = z_ref[at] / height
            return carry

    info_ref[...] = info
    blocks(normal, 0)
    own_ref[...] = jnp.concatenate([z_ref[b] for b in range(row_blocks)], axis=1)

    for k in range(slots):
        chosen = jnp.concatenate([z_ref[places_ref[k, b]] for b in range(row_blocks)], axis=0)
        high = chosen.astype(jnp.bfloat16).astype(jnp.float32)
        layer_ref[k] = jnp.transpose(jnp.concatenate([high, chosen - high], axis=0)).astype(jnp.bfloat16)

    for d in range(freqs):

        @pl.loop(0, items_ref[4 * d + 3, 0])
        def _(group):
            total = acc_ref[...]
            for u in range(GROUP):
                t = group * GROUP + u
                stored = items_ref[4 * d + 2, t]
                right = layer_ref[items_ref[4 * d, t]] * mask_ref[items_ref[4 * d + 1, t]]
                right = jnp.concatenate([right, right], axis=0)
                high, low = split(jnp.concatenate([g_refs[d][stored], c_refs[d][stored]], axis=0))
                left = jnp.concatenate([high, low], axis=1)
                total = total + jnp.dot(left, right, preferred_element_type=jnp.float32)
            acc_ref[...] = total

    half = row_blocks * parts
    gsum, csum = jnp.transpose(acc_ref[:size]), jnp.transpose(acc_ref[size:])
    gsum, csum = gsum[:half] + gsum[half:], csum[:half] + csum[half:]
    turn = turn_ref[...]
    for b in range(row_blocks):
        at = slice(b * parts, (b + 1) * parts)
        other = pltpu.roll(csum[at], parts // 2, 0)
        local_ref[:, b * size : (b + 1) * size] = gsum[at] + turn * other

    tile = jnp.zeros((parts, LANES), jnp.float32)
    if step == ITERS - 1:
        w = local_ref[...]
        zs = [jnp.concatenate([p[b] for b in range(row_blocks)], axis=1) for p in prev] + [own_ref[...]]
        values = [lane_sum(z * w) for z in zs]
        gram = [[lane_sum(zs[i] * zs[j]) for j in range(i + 1)] for i in range(ITERS)]
        shares = []
        for i, z in enumerate(zs):
            along = lane_sum(z * w) if i else values[0]
            share = jnp.where(gram[i][i] > 0.0, along / gram[i][i], 0.0)
            shares.append(share)
            w = w - share * z
        values += shares + [lane_sum(z * w) for z in zs] + [lane_sum(w * w)]
        values += [gram[i][j] for i in range(ITERS) for j in range(i + 1)]
        for lane_at, value in enumerate(values):
            tile = put_lane(tile, lane_at, value)
    tile_ref[...] = tile


def run_step(step, items, places, turn, info, lines, prev, g_parts, c_parts):
    plane, freqs = len(lines), len(g_parts)
    line, parts, rows = lines[0].shape
    slots, row_blocks = places.shape
    size = g_parts[0].shape[-1]
    vmem = pl.BlockSpec(memory_space=pltpu.VMEM)
    tile = jax.ShapeDtypeStruct((parts, LANES), jnp.float32)
    own = jax.ShapeDtypeStruct((parts, rows), jnp.float32)
    return pl.pallas_call(
        functools.partial(step_kernel, step, plane, line, freqs),
        in_specs=[pl.BlockSpec(memory_space=pltpu.SMEM)] * 2 + [vmem] * (2 + plane + step + 2 * freqs),
        out_specs=[vmem] * 5,
        out_shape=[
            jax.ShapeDtypeStruct((plane * line * row_blocks + 1, parts, size), jnp.float32),
            own,
            own,
            tile,
            tile,
        ],
        scratch_shapes=[
            pltpu.VMEM((slots, size, LANES), jnp.bfloat16),
            pltpu.VMEM((row_blocks + 1, size, LANES), jnp.bfloat16),
            pltpu.VMEM((2 * size, LANES), jnp.float32),
        ],
        compiler_params=pltpu.CompilerParams(vmem_limit_bytes=VMEM_LIMIT),
        name=f"step_{step}",
    )(items, places, turn, info, *lines, *prev, *g_parts, *c_parts)


def final_kernel(plane, line, info_ref, *refs):
    tiles = refs[:plane]
    krylov = refs[plane : plane + ITERS]
    out_ref, residual_ref = refs[plane + ITERS :]
    parts = info_ref.shape[0]
    fit = LANES // parts
    stacked = [tiles[q][i] for q in range(plane) for i in range(line)]
    sets = [
        jnp.transpose(jnp.concatenate(stacked[at : at + fit], axis=0)) for at in range(0, len(stacked), fit)
    ]
    info = jnp.transpose(jnp.concatenate([info_ref[...]] * fit, axis=0))

    def all_devices(shares):
        total = sum(shares[1:], shares[0])
        step = parts // 2
        while step < LANES:
            total = total + pltpu.roll(total, step, 1)
            step *= 2
        return total

    def row(table, at):
        return jnp.broadcast_to(table[at : at + 1], (8, LANES))

    zero = jnp.zeros((8, LANES), jnp.float32)
    norm, h00, h10, h01, h11, h21 = [row(info, i) for i in range(6)]
    last = [all_devices([row(s, i) for s in sets]) for i in range(ITERS)]
    shares = []
    for s in sets:
        off = [last[i] - row(s, ITERS + i) for i in range(ITERS)]
        square = row(s, 3 * ITERS)
        at = 3 * ITERS + 1
        for i in range(ITERS):
            square = square - 2.0 * off[i] * row(s, 2 * ITERS + i)
            for j in range(i + 1):
                square = square + (1.0 if i == j else 2.0) * off[i] * off[j] * row(s, at)
                at += 1
        shares.append(square)
    height = jnp.sqrt(jnp.maximum(all_devices(shares), 0.0))
    hessen = [[h00, h01, last[0]], [h10, h11, last[1]], [zero, h21, last[2]], [zero, zero, height]]
    normal = [[sum(h[m] * h[n] for h in hessen) for n in range(ITERS)] for m in range(ITERS)]
    low = [[None] * ITERS for _ in range(ITERS)]
    middle = []
    for m in range(ITERS):
        for n in range(m):
            rest = normal[m][n] - sum((low[m][k] * low[n][k] for k in range(n)), zero)
            low[m][n] = rest / low[n][n]
        low[m][m] = jnp.sqrt(normal[m][m] - sum((low[m][k] * low[m][k] for k in range(m)), zero))
        rest = norm * hessen[0][m] - sum((low[m][k] * middle[k] for k in range(m)), zero)
        middle.append(rest / low[m][m])
    coef_y = [None] * ITERS
    for m in reversed(range(ITERS)):
        rest = middle[m] - sum((low[k][m] * coef_y[k] for k in range(m + 1, ITERS)), zero)
        coef_y[m] = rest / low[m][m]
    total = zero
    for i, h in enumerate(hessen):
        misfit = (norm if i == 0 else zero) - sum(h[m] * coef_y[m] for m in range(ITERS))
        total = total + misfit * misfit
    residual_ref[...] = jnp.sqrt(total)
    columns = jnp.transpose(
        jnp.concatenate([y for y in coef_y] + [jnp.zeros((LANES - 8 * ITERS, LANES), jnp.float32)], axis=0)
    )[:parts]
    x = sum(columns[:, 8 * m : 8 * m + 1] * krylov[m][...] for m in range(ITERS))
    out_ref[0] = x[: parts // 2]
    out_ref[1] = x[parts // 2 :]


def run_final(info, tiles, krylov):
    plane = len(tiles)
    line, parts, _ = tiles[0].shape
    rows = krylov[0].shape[-1]
    vmem = pl.BlockSpec(memory_space=pltpu.VMEM)
    return pl.pallas_call(
        functools.partial(final_kernel, plane, line),
        in_specs=[vmem] * (1 + plane + ITERS),
        out_specs=[vmem] * 2,
        out_shape=[
            jax.ShapeDtypeStruct((2, parts // 2, rows), jnp.float32),
            jax.ShapeDtypeStruct((8, LANES), jnp.float32),
        ],
        name="final",
    )(info, *tiles, *krylov)


def make_shards(nodes, freqs):
    def shards(excitation, g_blocks, c_blocks, pattern, counts, freq_ids):
        angular = 0.2 * jnp.exp(freq_ids.astype(jnp.float32) * (math.log(8.0) / 1000.0))
        row_blocks, slots = pattern.shape
        size = g_blocks.shape[2]
        own_slots = g_blocks.shape[1]
        freq_count = excitation.shape[1]
        parts = 2 * freq_count
        node = lax.axis_index("node")
        freq = lax.axis_index("freq")
        stored = (row_blocks * own_slots, size, size)
        g_parts, c_parts = [], []
        for d in range(freqs):
            perm = [(i, (i + d) % freqs) for i in range(freqs)]
            g_part = lax.ppermute(g_blocks, "freq", perm) if d else g_blocks
            c_part = lax.ppermute(c_blocks, "freq", perm) if d else c_blocks
            g_parts.append(g_part.reshape(stored))
            c_parts.append(c_part.reshape(stored))
        items, places = work_list(pattern, counts, node, freq, nodes, freqs)
        turn = jnp.broadcast_to(jnp.concatenate([-angular, angular])[:, None], (parts, LANES))
        info = jnp.zeros((parts, LANES), jnp.float32)
        krylov, own = [], []
        rows = excitation
        for step in range(ITERS):
            lines = gather_rows(rows, nodes, parts)
            z, mine, rows, info, tile = run_step(
                step, items, places, turn, info, lines, krylov, g_parts, c_parts
            )
            krylov.append(z)
            own.append(mine)
        tiles = gather_rows(tile, nodes, parts)
        answer, residual = run_final(info, tiles, own)
        return answer, residual[0, :freq_count]

    return shards


def solution(mesh):
    in_specs = (
        P(None, "freq", "node"),
        P("node", "freq", None, None),
        P("node", "freq", None, None),
        P("node", None),
        P("node"),
        P("freq"),
    )
    out_specs = (P(None, "freq", "node"), P("freq"))
    shards = make_shards(mesh.shape["node"], mesh.shape["freq"])
    return jax.shard_map(shards, mesh=mesh, in_specs=in_specs, out_specs=out_specs, check_vma=False)
```

```python
import functools
import math

import jax
import jax.numpy as jnp
from jax import lax
from jax.experimental import pallas as pl
from jax.experimental.pallas import tpu as pltpu
from jax.sharding import PartitionSpec as P

ITERS = 3
LANES = 128
GROUP = 4
TOGETHER = 16
VMEM_LIMIT = 20 * 1024 * 1024


def split_nodes(nodes):
    plane = 4 if nodes % 4 == 0 else 1
    return nodes // plane, plane


def gather_rows(rows, nodes, parts):
    line, plane = split_nodes(nodes)
    held = [rows]
    for d in range(1, line):
        perm = [(i, (i + d * plane) % nodes) for i in range(nodes)]
        held.append(lax.ppermute(rows, "node", perm))
    whole_line = jnp.stack(held).reshape(line, parts, rows.shape[-1])
    held = [whole_line]
    for d in range(1, plane):
        perm = [(i, (i // plane) * plane + ((i % plane) ^ d)) for i in range(nodes)]
        held.append(lax.ppermute(whole_line, "node", perm))
    return held


def gather_all(rows, nodes, parts):
    if nodes > TOGETHER:
        return gather_rows(rows, nodes, parts)
    gathered = lax.all_gather(rows, ("node", "freq"))
    return [gathered.reshape(gathered.shape[0], parts, rows.shape[-1])]


def gathered_place(owner, node, nodes):
    if nodes <= TOGETHER:
        return owner
    line, plane = split_nodes(nodes)
    far = lax.rem(node // plane - owner // plane + line, line)
    return ((node % plane) ^ (owner % plane)) * line + far


def work_list(pattern, counts, node, freq, nodes, freqs):
    row_blocks, slots = pattern.shape
    own_slots = slots // freqs
    total = row_blocks * own_slots
    place = gathered_place(pattern // row_blocks, node, nodes) * row_blocks + pattern % row_blocks
    slot = jnp.arange(slots)
    places = jnp.where(slot[None, :] < counts[:, None], place, nodes * row_blocks).T
    order = jnp.arange(total)
    b = jnp.arange(row_blocks)
    tables = []
    for d in range(freqs):
        first = lax.rem(freq - d + freqs, freqs) * own_slots
        here = jnp.clip(counts - first, 0, own_slots)
        start = jnp.sum(jnp.where(b[None, :] < b[:, None], here[None, :], 0), axis=1)
        inside = order[:, None] - start[None, :]
        hit = (inside >= 0) & (inside < here[None, :])
        inside = jnp.sum(jnp.where(hit, inside, 0), axis=1)
        used = jnp.sum(here)
        block = jnp.sum(jnp.where(hit, b[None, :], 0), axis=1)
        groups = jnp.full((total,), (used + GROUP - 1) // GROUP)
        stored = block * own_slots + inside
        block = jnp.where(order < used, block, row_blocks)
        tables += [first + inside, block, stored, groups]
    return jnp.stack(tables).astype(jnp.int32), places.astype(jnp.int32)


def lane_sum(x):
    return jnp.sum(x, axis=1, keepdims=True)


def with_other_part(column):
    wide = jnp.broadcast_to(column, (column.shape[0], LANES))
    return wide + pltpu.roll(wide, column.shape[0] // 2, 0)


def put_lane(tile, lane, column):
    at = lax.broadcasted_iota(jnp.int32, tile.shape, 1) == lane
    return jnp.where(at, column, tile)


def split(x):
    high = x.astype(jnp.bfloat16)
    return high, (x - high.astype(jnp.float32)).astype(jnp.bfloat16)


def step_kernel(step, plane, line, stride, freqs, items_ref, places_ref, where_ref, turn_ref, info_in_ref, *refs):
    lines = refs[:plane]
    refs = refs[plane:]
    prev = refs[:step]
    g_refs = refs[step : step + freqs]
    c_refs = refs[step + freqs : step + 2 * freqs]
    z_ref, own_ref, local_ref, info_ref, tile_ref, layer_ref, mask_ref, acc_ref = refs[step + 2 * freqs :]
    nodes = plane * line
    parts, rows = local_ref.shape
    slots, row_blocks = places_ref.shape
    size = rows // row_blocks

    lane = lax.broadcasted_iota(jnp.int32, (size, LANES), 1)
    for b in range(row_blocks):
        mask_ref[b] = jnp.where((lane // parts) % row_blocks == b, 1.0, 0.0).astype(jnp.bfloat16)
    mask_ref[row_blocks] = jnp.zeros((size, LANES), jnp.bfloat16)
    acc_ref[...] = jnp.zeros_like(acc_ref)
    z_ref[nodes * row_blocks] = jnp.zeros((parts, size), jnp.float32)

    def blocks(body, carry):
        for q in range(plane):

            def chunk(i, carry, q=q):
                x = lines[q][i * stride + where_ref[1] if stride > 1 else i]
                for b in range(row_blocks):
                    carry = body(b, x[:, b * size : (b + 1) * size], (q * line + i) * row_blocks + b, carry)
                return carry

            if line <= 16:
                for i in range(line):
                    carry = chunk(i, carry)
            else:
                carry = lax.fori_loop(0, line, chunk, carry)
        return carry

    def add(sums, b, term):
        return sums[:b] + (sums[b] + term,) + sums[b + 1 :]

    def whole(sums):
        while len(sums) > 1:
            sums = tuple(x + y for x, y in zip(sums[::2], sums[1::2])) + sums[len(sums) // 2 * 2 :]
        return with_other_part(lane_sum(sums[0]))

    none = (jnp.zeros((parts, size), jnp.float32),) * row_blocks
    info = info_in_ref[...]
    if step == 0:
        height = jnp.sqrt(whole(blocks(lambda b, x, at, sums: add(sums, b, x * x), none)))
        info = put_lane(info, 0, height)

        def normal(b, x, at, carry):
            z_ref[at] = x / height
            return carry
    else:
        first = 1 if step == 1 else 3

        def dot(b, x, at, sums):
            return tuple(add(s, b, p[at] * x) for s, p in zip(sums, prev))

        coeffs = [whole(s) for s in blocks(dot, (none,) * step)]
        for i, coeff in enumerate(coeffs):
            info = put_lane(info, first + i, coeff)

        def subtract(b, x, at, sums):
            for coeff, p in zip(coeffs, prev):
                x = x - coeff * p[at]
            z_ref[at] = x
            return add(sums, b, x * x)

        height = jnp.sqrt(whole(blocks(subtract, none)))
        info = put_lane(info, first + step, height)

        def normal(b, x, at, carry):
            z_ref[at] = z_ref[at] / height
            return carry

    info_ref[...] = info
    blocks(normal, 0)
    own_ref[...] = jnp.concatenate([z_ref[where_ref[0] + b] for b in range(row_blocks)], axis=1)

    for k in range(slots):
        chosen = jnp.concatenate([z_ref[places_ref[k, b]] for b in range(row_blocks)], axis=0)
        high = chosen.astype(jnp.bfloat16).astype(jnp.float32)
        layer_ref[k] = jnp.transpose(jnp.concatenate([high, chosen - high], axis=0)).astype(jnp.bfloat16)

    for d in range(freqs):

        @pl.loop(0, items_ref[4 * d + 3, 0])
        def _(group):
            total = acc_ref[...]
            for u in range(GROUP):
                t = group * GROUP + u
                stored = items_ref[4 * d + 2, t]
                right = layer_ref[items_ref[4 * d, t]] * mask_ref[items_ref[4 * d + 1, t]]
                right = jnp.concatenate([right, right], axis=0)
                high, low = split(jnp.concatenate([g_refs[d][stored], c_refs[d][stored]], axis=0))
                left = jnp.concatenate([high, low], axis=1)
                total = total + jnp.dot(left, right, preferred_element_type=jnp.float32)
            acc_ref[...] = total

    half = row_blocks * parts
    gsum, csum = jnp.transpose(acc_ref[:size]), jnp.transpose(acc_ref[size:])
    gsum, csum = gsum[:half] + gsum[half:], csum[:half] + csum[half:]
    turn = turn_ref[...]
    for b in range(row_blocks):
        at = slice(b * parts, (b + 1) * parts)
        other = pltpu.roll(csum[at], parts // 2, 0)
        local_ref[:, b * size : (b + 1) * size] = gsum[at] + turn * other

    tile = jnp.zeros((parts, LANES), jnp.float32)
    if step == ITERS - 1:
        w = local_ref[...]
        zs = [jnp.concatenate([p[where_ref[0] + b] for b in range(row_blocks)], axis=1) for p in prev] + [own_ref[...]]
        values = [lane_sum(z * w) for z in zs]
        gram = [[lane_sum(zs[i] * zs[j]) for j in range(i + 1)] for i in range(ITERS)]
        shares = []
        for i, z in enumerate(zs):
            along = lane_sum(z * w) if i else values[0]
            share = jnp.where(gram[i][i] > 0.0, along / gram[i][i], 0.0)
            shares.append(share)
            w = w - share * z
        values += shares + [lane_sum(z * w) for z in zs] + [lane_sum(w * w)]
        values += [gram[i][j] for i in range(ITERS) for j in range(i + 1)]
        for lane_at, value in enumerate(values):
            tile = put_lane(tile, lane_at, value)
    tile_ref[...] = tile


def run_step(step, stride, items, places, where, turn, info, lines, prev, g_parts, c_parts):
    plane, freqs = len(lines), len(g_parts)
    line, parts, rows = lines[0].shape
    line = line // stride
    slots, row_blocks = places.shape
    size = g_parts[0].shape[-1]
    vmem = pl.BlockSpec(memory_space=pltpu.VMEM)
    tile = jax.ShapeDtypeStruct((parts, LANES), jnp.float32)
    own = jax.ShapeDtypeStruct((parts, rows), jnp.float32)
    return pl.pallas_call(
        functools.partial(step_kernel, step, plane, line, stride, freqs),
        in_specs=[pl.BlockSpec(memory_space=pltpu.SMEM)] * 3 + [vmem] * (2 + plane + step + 2 * freqs),
        out_specs=[vmem] * 5,
        out_shape=[
            jax.ShapeDtypeStruct((plane * line * row_blocks + 1, parts, size), jnp.float32),
            own,
            own,
            tile,
            tile,
        ],
        scratch_shapes=[
            pltpu.VMEM((slots, size, LANES), jnp.bfloat16),
            pltpu.VMEM((row_blocks + 1, size, LANES), jnp.bfloat16),
            pltpu.VMEM((2 * size, LANES), jnp.float32),
        ],
        compiler_params=pltpu.CompilerParams(vmem_limit_bytes=VMEM_LIMIT),
        name=f"step_{step}",
    )(items, places, where, turn, info, *lines, *prev, *g_parts, *c_parts)


def final_kernel(plane, line, info_ref, *refs):
    tiles = refs[:plane]
    krylov = refs[plane : plane + ITERS]
    out_ref, residual_ref = refs[plane + ITERS :]
    parts = info_ref.shape[0]
    fit = LANES // parts
    stacked = [tiles[q][i] for q in range(plane) for i in range(line)]
    sets = [
        jnp.transpose(jnp.concatenate(stacked[at : at + fit], axis=0)) for at in range(0, len(stacked), fit)
    ]
    info = jnp.transpose(jnp.concatenate([info_ref[...]] * fit, axis=0))

    def all_devices(shares):
        total = sum(shares[1:], shares[0])
        step = parts // 2
        while step < LANES:
            total = total + pltpu.roll(total, step, 1)
            step *= 2
        return total

    def row(table, at):
        return jnp.broadcast_to(table[at : at + 1], (8, LANES))

    zero = jnp.zeros((8, LANES), jnp.float32)
    norm, h00, h10, h01, h11, h21 = [row(info, i) for i in range(6)]
    last = [all_devices([row(s, i) for s in sets]) for i in range(ITERS)]
    shares = []
    for s in sets:
        off = [last[i] - row(s, ITERS + i) for i in range(ITERS)]
        square = row(s, 3 * ITERS)
        at = 3 * ITERS + 1
        for i in range(ITERS):
            square = square - 2.0 * off[i] * row(s, 2 * ITERS + i)
            for j in range(i + 1):
                square = square + (1.0 if i == j else 2.0) * off[i] * off[j] * row(s, at)
                at += 1
        shares.append(square)
    height = jnp.sqrt(jnp.maximum(all_devices(shares), 0.0))
    hessen = [[h00, h01, last[0]], [h10, h11, last[1]], [zero, h21, last[2]], [zero, zero, height]]
    normal = [[sum(h[m] * h[n] for h in hessen) for n in range(ITERS)] for m in range(ITERS)]
    low = [[None] * ITERS for _ in range(ITERS)]
    middle = []
    for m in range(ITERS):
        for n in range(m):
            rest = normal[m][n] - sum((low[m][k] * low[n][k] for k in range(n)), zero)
            low[m][n] = rest / low[n][n]
        low[m][m] = jnp.sqrt(normal[m][m] - sum((low[m][k] * low[m][k] for k in range(m)), zero))
        rest = norm * hessen[0][m] - sum((low[m][k] * middle[k] for k in range(m)), zero)
        middle.append(rest / low[m][m])
    coef_y = [None] * ITERS
    for m in reversed(range(ITERS)):
        rest = middle[m] - sum((low[k][m] * coef_y[k] for k in range(m + 1, ITERS)), zero)
        coef_y[m] = rest / low[m][m]
    total = zero
    for i, h in enumerate(hessen):
        misfit = (norm if i == 0 else zero) - sum(h[m] * coef_y[m] for m in range(ITERS))
        total = total + misfit * misfit
    residual_ref[...] = jnp.sqrt(total)
    columns = jnp.transpose(
        jnp.concatenate([y for y in coef_y] + [jnp.zeros((LANES - 8 * ITERS, LANES), jnp.float32)], axis=0)
    )[:parts]
    x = sum(columns[:, 8 * m : 8 * m + 1] * krylov[m][...] for m in range(ITERS))
    out_ref[0] = x[: parts // 2]
    out_ref[1] = x[parts // 2 :]


def run_final(info, tiles, krylov):
    plane = len(tiles)
    line, parts, _ = tiles[0].shape
    rows = krylov[0].shape[-1]
    vmem = pl.BlockSpec(memory_space=pltpu.VMEM)
    return pl.pallas_call(
        functools.partial(final_kernel, plane, line),
        in_specs=[vmem] * (1 + plane + ITERS),
        out_specs=[vmem] * 2,
        out_shape=[
            jax.ShapeDtypeStruct((2, parts // 2, rows), jnp.float32),
            jax.ShapeDtypeStruct((8, LANES), jnp.float32),
        ],
        name="final",
    )(info, *tiles, *krylov)


def make_shards(nodes, freqs):
    def shards(excitation, g_blocks, c_blocks, pattern, counts, freq_ids):
        angular = 0.2 * jnp.exp(freq_ids.astype(jnp.float32) * (math.log(8.0) / 1000.0))
        row_blocks, slots = pattern.shape
        size = g_blocks.shape[2]
        own_slots = g_blocks.shape[1]
        freq_count = excitation.shape[1]
        parts = 2 * freq_count
        node = lax.axis_index("node")
        freq = lax.axis_index("freq")
        stored = (row_blocks * own_slots, size, size)
        g_parts, c_parts = [], []
        for d in range(freqs):
            perm = [(i, (i + d) % freqs) for i in range(freqs)]
            g_part = lax.ppermute(g_blocks, "freq", perm) if d else g_blocks
            c_part = lax.ppermute(c_blocks, "freq", perm) if d else c_blocks
            g_parts.append(g_part.reshape(stored))
            c_parts.append(c_part.reshape(stored))
        items, places = work_list(pattern, counts, node, freq, nodes, freqs)
        turn = jnp.broadcast_to(jnp.concatenate([-angular, angular])[:, None], (parts, LANES))
        info = jnp.zeros((parts, LANES), jnp.float32)
        stride = freqs if nodes <= TOGETHER else 1
        own_place = gathered_place(node, node, nodes) * row_blocks
        where = jnp.stack([own_place, freq]).astype(jnp.int32)
        krylov, own = [], []
        rows = excitation
        for step in range(ITERS):
            lines = gather_all(rows, nodes, parts)
            z, mine, rows, info, tile = run_step(
                step, stride, items, places, where, turn, info, lines, krylov, g_parts, c_parts
            )
            krylov.append(z)
            own.append(mine)
        tiles = gather_rows(tile, nodes, parts)
        answer, residual = run_final(info, tiles, own)
        return answer, residual[0, :freq_count]

    return shards


def solution(mesh):
    in_specs = (
        P(None, "freq", "node"),
        P("node", "freq", None, None),
        P("node", "freq", None, None),
        P("node", None),
        P("node"),
        P("freq"),
    )
    out_specs = (P(None, "freq", "node"), P("freq"))
    shards = make_shards(mesh.shape["node"], mesh.shape["freq"])
    return jax.shard_map(shards, mesh=mesh, in_specs=in_specs, out_specs=out_specs, check_vma=False)
```

```python
import functools
import math

import jax
import jax.numpy as jnp
from jax import lax
from jax.experimental import pallas as pl
from jax.experimental.pallas import tpu as pltpu
from jax.sharding import Mesh
from jax.sharding import PartitionSpec as P

ITERS = 3
LANES = 128
GROUP = 4
SHIFT = 256
VMEM_LIMIT = 20 * 1024 * 1024


def split_nodes(nodes):
    plane = 4 if nodes % 4 == 0 else 1
    return nodes // plane, plane


def gather_rows(rows, line, plane):
    shape = rows.shape
    whole_line = lax.all_to_all(jnp.broadcast_to(rows[None], (line,) + shape), "line", 0, 0)
    copies = jnp.broadcast_to(whole_line[None], (plane, line) + shape)
    gathered = lax.all_to_all(copies, "place", 0, 0)
    return gathered.reshape((plane * line,) + shape)


def lane_sum(x):
    return jnp.sum(x, axis=1, keepdims=True)


def with_other_part(column):
    wide = jnp.broadcast_to(column, (column.shape[0], LANES))
    return wide + pltpu.roll(wide, column.shape[0] // 2, 0)


def put_lane(tile, lane, column):
    at = lax.broadcasted_iota(jnp.int32, tile.shape, 1) == lane
    return jnp.where(at, column, tile)


def split(x):
    high = x.astype(jnp.bfloat16)
    return high, (x - high.astype(jnp.float32)).astype(jnp.bfloat16)


def step_kernel(step, plane, line, freqs, pattern_ref, counts_ref, where_ref, turn_ref, info_in_ref, *refs):
    lines_ref, refs = refs[0], refs[1:]
    prev = refs[:step]
    g_refs = list(refs[step : step + freqs])
    c_refs = list(refs[step + freqs : step + 2 * freqs])
    z_ref, own_ref, local_ref, info_ref, tile_ref, layer_ref, mask_ref, acc_ref, list_ref = refs[
        step + 2 * freqs : step + 2 * freqs + 9
    ]
    nodes = plane * line
    parts, rows = local_ref.shape
    row_blocks, slots = pattern_ref.shape
    own_slots = slots // freqs
    size = rows // row_blocks
    own_place = (where_ref[1] * line + where_ref[0]) * row_blocks

    arrivals = []
    if step == 0:
        kept, sems = refs[step + 2 * freqs + 9 :]
        for m, held in enumerate((g_refs, c_refs)):
            arrivals.append(pltpu.make_async_copy(held[0], kept.at[m], sems.at[m]))
            arrivals[-1].start()
            held[0] = kept.at[m]

    used = []
    for d in range(freqs):
        first = lax.rem(where_ref[2] + (freqs - d), freqs) * own_slots
        filled = jnp.int32(0)
        for b in range(row_blocks):
            for kk in range(own_slots):
                stored = b * own_slots + kk
                list_ref[d, filled] = (first + kk) * SHIFT + (b * SHIFT * SHIFT + stored)
                filled += (first + kk < counts_ref[b]).astype(jnp.int32)
        for u in range(GROUP):
            list_ref[d, filled + u] = row_blocks * SHIFT * SHIFT
        used.append(filled)

    def block_place(b, k):
        p = pattern_ref[b, k]
        owner = lax.div(p, row_blocks)
        place = lax.rem(owner, plane) * line + lax.div(owner, plane)
        return jnp.where(k < counts_ref[b], place * row_blocks + lax.rem(p, row_blocks), nodes * row_blocks)

    lane = lax.broadcasted_iota(jnp.int32, (size, LANES), 1)
    for b in range(row_blocks):
        mask_ref[b] = jnp.where((lane // parts) % row_blocks == b, 1.0, 0.0).astype(jnp.bfloat16)
    mask_ref[row_blocks] = jnp.zeros((size, LANES), jnp.bfloat16)
    acc_ref[...] = jnp.zeros_like(acc_ref)
    z_ref[nodes * row_blocks] = jnp.zeros((parts, size), jnp.float32)

    def blocks(body, carry):
        def chunk(i, carry):
            x = lines_ref[i]
            for b in range(row_blocks):
                carry = body(b, x[:, b * size : (b + 1) * size], i * row_blocks + b, carry)
            return carry

        if nodes > 16:
            return lax.fori_loop(0, nodes, chunk, carry)
        for i in range(nodes):
            carry = chunk(i, carry)
        return carry

    def add(sums, b, term):
        return sums[:b] + (sums[b] + term,) + sums[b + 1 :]

    def whole(sums):
        while len(sums) > 1:
            sums = tuple(x + y for x, y in zip(sums[::2], sums[1::2])) + sums[len(sums) // 2 * 2 :]
        return with_other_part(lane_sum(sums[0]))

    none = (jnp.zeros((parts, size), jnp.float32),) * row_blocks
    info = info_in_ref[...]
    if step == 0:
        height = jnp.sqrt(whole(blocks(lambda b, x, at, sums: add(sums, b, x * x), none)))
        info = put_lane(info, 0, height)

        def normal(b, x, at, carry):
            z_ref[at] = x / height
            return carry
    else:
        first = 1 if step == 1 else 3

        def dot(b, x, at, sums):
            return tuple(add(s, b, p[at] * x) for s, p in zip(sums, prev))

        coeffs = [whole(s) for s in blocks(dot, (none,) * step)]
        for i, coeff in enumerate(coeffs):
            info = put_lane(info, first + i, coeff)

        def subtract(b, x, at, sums):
            for coeff, p in zip(coeffs, prev):
                x = x - coeff * p[at]
            z_ref[at] = x
            return add(sums, b, x * x)

        height = jnp.sqrt(whole(blocks(subtract, none)))
        info = put_lane(info, first + step, height)

        def normal(b, x, at, carry):
            z_ref[at] = z_ref[at] / height
            return carry

    info_ref[...] = info
    blocks(normal, 0)
    own_ref[...] = jnp.concatenate([z_ref[own_place + b] for b in range(row_blocks)], axis=1)

    for k in range(slots):
        chosen = jnp.concatenate([z_ref[block_place(b, k)] for b in range(row_blocks)], axis=0)
        high = chosen.astype(jnp.bfloat16).astype(jnp.float32)
        layer_ref[k] = jnp.transpose(jnp.concatenate([high, chosen - high], axis=0)).astype(jnp.bfloat16)

    for d in reversed(range(freqs)):
        if d == 0:
            for arrival in arrivals:
                arrival.wait()

        @pl.loop(0, lax.div(used[d] + (GROUP - 1), GROUP))
        def _(group):
            total = acc_ref[...]
            for u in range(GROUP):
                item = list_ref[d, group * GROUP + u]
                stored = lax.rem(item, SHIFT)
                layer = lax.rem(lax.div(item, SHIFT), SHIFT)
                right = layer_ref[layer] * mask_ref[lax.div(item, SHIFT * SHIFT)]
                right = jnp.concatenate([right, right], axis=0)
                high, low = split(jnp.concatenate([g_refs[d][stored], c_refs[d][stored]], axis=0))
                left = jnp.concatenate([high, low], axis=1)
                total = total + jnp.dot(left, right, preferred_element_type=jnp.float32)
            acc_ref[...] = total

    half = row_blocks * parts
    gsum, csum = jnp.transpose(acc_ref[:size]), jnp.transpose(acc_ref[size:])
    gsum, csum = gsum[:half] + gsum[half:], csum[:half] + csum[half:]
    turn = turn_ref[...]
    for b in range(row_blocks):
        at = slice(b * parts, (b + 1) * parts)
        other = pltpu.roll(csum[at], parts // 2, 0)
        local_ref[:, b * size : (b + 1) * size] = gsum[at] + turn * other

    tile = jnp.zeros((parts, LANES), jnp.float32)
    if step == ITERS - 1:
        w = local_ref[...]
        zs = [jnp.concatenate([p[own_place + b] for b in range(row_blocks)], axis=1) for p in prev] + [own_ref[...]]
        values = [lane_sum(z * w) for z in zs]
        gram = [[lane_sum(zs[i] * zs[j]) for j in range(i + 1)] for i in range(ITERS)]
        shares = []
        for i, z in enumerate(zs):
            along = lane_sum(z * w) if i else values[0]
            share = jnp.where(gram[i][i] > 0.0, along / gram[i][i], 0.0)
            shares.append(share)
            w = w - share * z
        values += shares + [lane_sum(z * w) for z in zs] + [lane_sum(w * w)]
        values += [gram[i][j] for i in range(ITERS) for j in range(i + 1)]
        for lane_at, value in enumerate(values):
            tile = put_lane(tile, lane_at, value)
    tile_ref[...] = tile


def run_step(step, plane, pattern, counts, where, turn, info, lines, prev, g_parts, c_parts):
    freqs = len(g_parts)
    nodes, parts, rows = lines.shape
    row_blocks, slots = pattern.shape
    stored, size, _ = g_parts[0].shape
    vmem = pl.BlockSpec(memory_space=pltpu.VMEM)
    in_specs = [pl.BlockSpec(memory_space=pltpu.SMEM)] * 3 + [vmem] * (3 + step + 2 * freqs)
    scratch_shapes = [
        pltpu.VMEM((slots, size, LANES), jnp.bfloat16),
        pltpu.VMEM((row_blocks + 1, size, LANES), jnp.bfloat16),
        pltpu.VMEM((2 * size, LANES), jnp.float32),
        pltpu.SMEM((freqs, stored + GROUP), jnp.int32),
    ]
    if step == 0:
        in_specs[6] = in_specs[6 + freqs] = pl.BlockSpec(memory_space=pltpu.HBM)
        scratch_shapes += [pltpu.VMEM((2, stored, size, size), jnp.float32), pltpu.SemaphoreType.DMA((2,))]
    tile = jax.ShapeDtypeStruct((parts, LANES), jnp.float32)
    own = jax.ShapeDtypeStruct((parts, rows), jnp.float32)
    return pl.pallas_call(
        functools.partial(step_kernel, step, plane, nodes // plane, freqs),
        in_specs=in_specs,
        out_specs=[vmem] * 5,
        out_shape=[
            jax.ShapeDtypeStruct((nodes * row_blocks + 1, parts, size), jnp.float32),
            own,
            own,
            tile,
            tile,
        ],
        scratch_shapes=scratch_shapes,
        compiler_params=pltpu.CompilerParams(vmem_limit_bytes=VMEM_LIMIT),
        name=f"step_{step}",
    )(pattern, counts, where, turn, info, lines, *prev, *g_parts, *c_parts)


def final_kernel(info_ref, tiles_ref, *refs):
    krylov = refs[:ITERS]
    out_ref, residual_ref = refs[ITERS:]
    parts = info_ref.shape[0]
    fit = LANES // parts
    stacked = [tiles_ref[i] for i in range(tiles_ref.shape[0])]
    sets = [
        jnp.transpose(jnp.concatenate(stacked[at : at + fit], axis=0)) for at in range(0, len(stacked), fit)
    ]
    info = jnp.transpose(jnp.concatenate([info_ref[...]] * fit, axis=0))

    def all_devices(shares):
        total = sum(shares[1:], shares[0])
        step = parts // 2
        while step < LANES:
            total = total + pltpu.roll(total, step, 1)
            step *= 2
        return total

    def row(table, at):
        return jnp.broadcast_to(table[at : at + 1], (8, LANES))

    zero = jnp.zeros((8, LANES), jnp.float32)
    norm, h00, h10, h01, h11, h21 = [row(info, i) for i in range(6)]
    last = [all_devices([row(s, i) for s in sets]) for i in range(ITERS)]
    shares = []
    for s in sets:
        off = [last[i] - row(s, ITERS + i) for i in range(ITERS)]
        square = row(s, 3 * ITERS)
        at = 3 * ITERS + 1
        for i in range(ITERS):
            square = square - 2.0 * off[i] * row(s, 2 * ITERS + i)
            for j in range(i + 1):
                square = square + (1.0 if i == j else 2.0) * off[i] * off[j] * row(s, at)
                at += 1
        shares.append(square)
    height = jnp.sqrt(jnp.maximum(all_devices(shares), 0.0))
    hessen = [[h00, h01, last[0]], [h10, h11, last[1]], [zero, h21, last[2]], [zero, zero, height]]
    normal = [[sum(h[m] * h[n] for h in hessen) for n in range(ITERS)] for m in range(ITERS)]
    low = [[None] * ITERS for _ in range(ITERS)]
    middle = []
    for m in range(ITERS):
        for n in range(m):
            rest = normal[m][n] - sum((low[m][k] * low[n][k] for k in range(n)), zero)
            low[m][n] = rest / low[n][n]
        low[m][m] = jnp.sqrt(normal[m][m] - sum((low[m][k] * low[m][k] for k in range(m)), zero))
        rest = norm * hessen[0][m] - sum((low[m][k] * middle[k] for k in range(m)), zero)
        middle.append(rest / low[m][m])
    coef_y = [None] * ITERS
    for m in reversed(range(ITERS)):
        rest = middle[m] - sum((low[k][m] * coef_y[k] for k in range(m + 1, ITERS)), zero)
        coef_y[m] = rest / low[m][m]
    total = zero
    for i, h in enumerate(hessen):
        misfit = (norm if i == 0 else zero) - sum(h[m] * coef_y[m] for m in range(ITERS))
        total = total + misfit * misfit
    residual_ref[...] = jnp.sqrt(total)[:1, : parts // 2]
    columns = jnp.transpose(
        jnp.concatenate([y for y in coef_y] + [jnp.zeros((LANES - 8 * ITERS, LANES), jnp.float32)], axis=0)
    )[:parts]
    x = sum(columns[:, 8 * m : 8 * m + 1] * krylov[m][...] for m in range(ITERS))
    out_ref[0] = x[: parts // 2]
    out_ref[1] = x[parts // 2 :]


def run_final(info, tiles, krylov):
    parts, rows = krylov[0].shape
    vmem = pl.BlockSpec(memory_space=pltpu.VMEM)
    return pl.pallas_call(
        final_kernel,
        in_specs=[vmem] * (2 + ITERS),
        out_specs=[vmem] * 2,
        out_shape=[
            jax.ShapeDtypeStruct((2, parts // 2, rows), jnp.float32),
            jax.ShapeDtypeStruct((1, parts // 2), jnp.float32),
        ],
        name="final",
    )(info, tiles, *krylov)


def make_shards(line, plane, freqs):
    def shards(excitation, g_blocks, c_blocks, pattern, counts, freq_ids):
        angular = 0.2 * jnp.exp(freq_ids.astype(jnp.float32) * (math.log(8.0) / 1000.0))
        row_blocks, own_slots, size, _ = g_blocks.shape
        freq_count = excitation.shape[1]
        parts = 2 * freq_count
        where = jnp.stack([lax.axis_index(name) for name in ("line", "place", "freq")]).astype(jnp.int32)
        stored = (row_blocks * own_slots, size, size)
        g_parts, c_parts = [], []
        for d in range(freqs):
            perm = [(i, (i + d) % freqs) for i in range(freqs)]
            g_part = lax.ppermute(g_blocks, "freq", perm) if d else g_blocks
            c_part = lax.ppermute(c_blocks, "freq", perm) if d else c_blocks
            g_parts.append(g_part.reshape(stored))
            c_parts.append(c_part.reshape(stored))
        turn = jnp.broadcast_to(jnp.concatenate([-angular, angular])[:, None], (parts, LANES))
        info = jnp.zeros((parts, LANES), jnp.float32)
        krylov, own = [], []
        rows = excitation.reshape(parts, row_blocks * size)
        for step in range(ITERS):
            lines = gather_rows(rows, line, plane)
            z, mine, rows, info, tile = run_step(
                step, plane, pattern, counts, where, turn, info, lines, krylov, g_parts, c_parts
            )
            krylov.append(z)
            own.append(mine)
        tiles = gather_rows(tile, line, plane)
        answer, residual = run_final(info, tiles, own)
        return answer, residual.reshape(freq_count)

    return shards


def solution(mesh):
    line, plane = split_nodes(mesh.shape["node"])
    freqs = mesh.shape["freq"]
    fine = Mesh(mesh.devices.reshape(line, plane, freqs), ("line", "place", "freq"))
    node = ("line", "place")
    in_specs = (
        P(None, "freq", node),
        P(node, "freq", None, None),
        P(node, "freq", None, None),
        P(node, None),
        P(node),
        P("freq"),
    )
    out_specs = (P(None, "freq", node), P("freq"))
    shards = make_shards(line, plane, freqs)
    return jax.shard_map(shards, mesh=fine, in_specs=in_specs, out_specs=out_specs, check_vma=False)
```

```python
import functools
import math

import jax
import jax.numpy as jnp
from jax import lax
from jax.experimental import pallas as pl
from jax.experimental.pallas import tpu as pltpu
from jax.sharding import Mesh
from jax.sharding import PartitionSpec as P

ITERS = 3
LANES = 128
GROUP = 4
SHIFT = 256
SHARES = 16
VMEM_LIMIT = 20 * 1024 * 1024


def split_nodes(nodes):
    plane = 4 if nodes % 4 == 0 else 1
    return nodes // plane, plane


def partner_steps(size):
    if size & (size - 1) == 0:
        return [[(i, i ^ d) for i in range(size)] for d in range(1, size)]
    return [[(i, (i + d) % size) for i in range(size)] for d in range(1, size)]


def distance(me, other, size):
    if size & (size - 1) == 0:
        return me ^ other
    return lax.rem(me - other + size, size)


def gather_rows(rows, line, plane):
    parts = rows.size // rows.shape[-1]
    held = [rows] + [lax.ppermute(rows, "line", perm) for perm in partner_steps(line)]
    whole_line = jnp.stack(held).reshape(line, parts, rows.shape[-1])
    return [whole_line] + [lax.ppermute(whole_line, "place", perm) for perm in partner_steps(plane)]


def list_kernel(line, plane, freqs, pattern_ref, counts_ref, where_ref, list_ref, places_ref, used_ref):
    row_blocks, slots = pattern_ref.shape
    own_slots = slots // freqs
    for d in range(freqs):
        first = lax.rem(where_ref[2] + (freqs - d), freqs) * own_slots
        filled = jnp.int32(0)
        for b in range(row_blocks):
            for kk in range(own_slots):
                stored = b * own_slots + kk
                list_ref[d, filled] = (first + kk) * SHIFT + (b * SHIFT * SHIFT + stored)
                filled += (first + kk < counts_ref[b]).astype(jnp.int32)
        for u in range(GROUP):
            list_ref[d, filled + u] = row_blocks * SHIFT * SHIFT
        used_ref[d] = lax.div(filled + (GROUP - 1), GROUP)
    for b in range(row_blocks):
        for k in range(slots):
            p = pattern_ref[b, k]
            owner = lax.div(p, row_blocks)
            far = distance(where_ref[0], lax.div(owner, plane), line)
            place = distance(where_ref[1], lax.rem(owner, plane), plane) * line + far
            place = place * row_blocks + lax.rem(p, row_blocks)
            places_ref[k, b] = jnp.where(k < counts_ref[b], place, line * plane * row_blocks)


def work_list(pattern, counts, where, line, plane, freqs):
    row_blocks, slots = pattern.shape
    smem = pl.BlockSpec(memory_space=pltpu.SMEM)
    return pl.pallas_call(
        functools.partial(list_kernel, line, plane, freqs),
        in_specs=[smem] * 3,
        out_specs=[smem] * 3,
        out_shape=[
            jax.ShapeDtypeStruct((freqs, row_blocks * slots // freqs + GROUP), jnp.int32),
            jax.ShapeDtypeStruct((slots, row_blocks), jnp.int32),
            jax.ShapeDtypeStruct((freqs,), jnp.int32),
        ],
        name="work_list",
    )(pattern, counts, where)


def lane_sum(x):
    return jnp.sum(x, axis=1, keepdims=True)


def with_other_part(column):
    wide = jnp.broadcast_to(column, (column.shape[0], LANES))
    return wide + pltpu.roll(wide, column.shape[0] // 2, 0)


def put_lane(tile, lane, column):
    at = lax.broadcasted_iota(jnp.int32, tile.shape, 1) == lane
    return jnp.where(at, column, tile)


def split(x):
    high = x.astype(jnp.bfloat16)
    return high, (x - high.astype(jnp.float32)).astype(jnp.bfloat16)


def step_kernel(step, plane, line, freqs, list_ref, places_ref, used_ref, turn_ref, info_in_ref, *refs):
    lines, refs = refs[:plane], refs[plane:]
    prev, refs = refs[:step], refs[step:]
    g_refs, c_refs = list(refs[:freqs]), list(refs[freqs : 2 * freqs])
    z_ref, own_ref, local_ref, info_ref, layer_ref, mask_ref, acc_ref = refs[2 * freqs : 2 * freqs + 7]
    nodes = plane * line
    parts, rows = own_ref.shape
    slots, row_blocks = places_ref.shape
    size = rows // row_blocks

    arrivals = []
    if step == 0:
        kept, sems = refs[2 * freqs + 7 :]
        for m, held in enumerate((g_refs, c_refs)):
            arrivals.append(pltpu.make_async_copy(held[0], kept.at[m], sems.at[m]))
            arrivals[-1].start()
            held[0] = kept.at[m]

    lane = lax.broadcasted_iota(jnp.int32, (size, LANES), 1)
    for b in range(row_blocks):
        mask_ref[b] = jnp.where((lane // parts) % row_blocks == b, 1.0, 0.0).astype(jnp.bfloat16)
    mask_ref[row_blocks] = jnp.zeros((size, LANES), jnp.bfloat16)
    acc_ref[...] = jnp.zeros_like(acc_ref)
    z_ref[nodes * row_blocks] = jnp.zeros((parts, size), jnp.float32)

    def blocks(body, carry):
        for q in range(plane):

            def chunk(i, carry, q=q):
                x = lines[q][i]
                for b in range(row_blocks):
                    carry = body(b, x[:, b * size : (b + 1) * size], (q * line + i) * row_blocks + b, carry)
                return carry

            if line <= 4:
                for i in range(line):
                    carry = chunk(i, carry)
            else:
                carry = lax.fori_loop(0, line, chunk, carry)
        return carry

    def add(sums, b, term):
        return sums[:b] + (sums[b] + term,) + sums[b + 1 :]

    def whole(sums):
        while len(sums) > 1:
            sums = tuple(x + y for x, y in zip(sums[::2], sums[1::2])) + sums[len(sums) // 2 * 2 :]
        return with_other_part(lane_sum(sums[0]))

    none = (jnp.zeros((parts, size), jnp.float32),) * row_blocks
    info = info_in_ref[...]
    if step == 0:
        height = jnp.sqrt(whole(blocks(lambda b, x, at, sums: add(sums, b, x * x), none)))
        info = put_lane(info, 0, height)

        def normal(b, x, at, carry):
            z_ref[at] = x / height
            return carry
    else:
        first = 1 if step == 1 else 3

        def dot(b, x, at, sums):
            return tuple(add(s, b, p[at] * x) for s, p in zip(sums, prev))

        coeffs = [whole(s) for s in blocks(dot, (none,) * step)]
        for i, coeff in enumerate(coeffs):
            info = put_lane(info, first + i, coeff)

        def subtract(b, x, at, sums):
            for coeff, p in zip(coeffs, prev):
                x = x - coeff * p[at]
            z_ref[at] = x
            return add(sums, b, x * x)

        height = jnp.sqrt(whole(blocks(subtract, none)))
        info = put_lane(info, first + step, height)

        def normal(b, x, at, carry):
            z_ref[at] = z_ref[at] / height
            return carry

    blocks(normal, 0)
    own_ref[...] = jnp.concatenate([z_ref[b] for b in range(row_blocks)], axis=1)

    for k in range(slots):
        chosen = jnp.concatenate([z_ref[places_ref[k, b]] for b in range(row_blocks)], axis=0)
        high = chosen.astype(jnp.bfloat16).astype(jnp.float32)
        layer_ref[k] = jnp.transpose(jnp.concatenate([high, chosen - high], axis=0)).astype(jnp.bfloat16)

    for d in reversed(range(freqs)):
        if d == 0:
            for arrival in arrivals:
                arrival.wait()

        @pl.loop(0, used_ref[d])
        def _(group):
            total = acc_ref[...]
            for u in range(GROUP):
                item = list_ref[d, group * GROUP + u]
                stored = lax.rem(item, SHIFT)
                layer = lax.rem(lax.div(item, SHIFT), SHIFT)
                right = layer_ref[layer] * mask_ref[lax.div(item, SHIFT * SHIFT)]
                right = jnp.concatenate([right, right], axis=0)
                high, low = split(jnp.concatenate([g_refs[d][stored], c_refs[d][stored]], axis=0))
                left = jnp.concatenate([high, low], axis=1)
                total = total + jnp.dot(left, right, preferred_element_type=jnp.float32)
            acc_ref[...] = total

    half = row_blocks * parts
    gsum, csum = jnp.transpose(acc_ref[:size]), jnp.transpose(acc_ref[size:])
    gsum, csum = gsum[:half] + gsum[half:], csum[:half] + csum[half:]
    turn = turn_ref[...]
    for b in range(row_blocks):
        at = slice(b * parts, (b + 1) * parts)
        other = pltpu.roll(csum[at], parts // 2, 0)
        local_ref[:, b * size : (b + 1) * size] = gsum[at] + turn * other

    if step == ITERS - 1:
        w = local_ref[...]
        zs = [jnp.concatenate([p[b] for b in range(row_blocks)], axis=1) for p in prev] + [own_ref[...]]
        values = [lane_sum(z * w) for z in zs]
        gram = [[lane_sum(zs[i] * zs[j]) for j in range(i + 1)] for i in range(ITERS)]
        shares = []
        for i, z in enumerate(zs):
            along = lane_sum(z * w) if i else values[0]
            share = jnp.where(gram[i][i] > 0.0, along / gram[i][i], 0.0)
            shares.append(share)
            w = w - share * z
        values += shares + [lane_sum(z * w) for z in zs] + [lane_sum(w * w)]
        values += [gram[i][j] for i in range(ITERS) for j in range(i + 1)]
        for lane_at, value in enumerate(values):
            info = put_lane(info, SHARES + lane_at, value)
    info_ref[...] = info


def run_step(step, lists, turn, info, lines, prev, g_parts, c_parts):
    plane, freqs = len(lines), len(g_parts)
    line, parts, rows = lines[0].shape
    slots, row_blocks = lists[1].shape
    stored, size, _ = g_parts[0].shape
    vmem = pl.BlockSpec(memory_space=pltpu.VMEM)
    in_specs = [pl.BlockSpec(memory_space=pltpu.SMEM)] * 3 + [vmem] * (2 + plane + step + 2 * freqs)
    scratch_shapes = [
        pltpu.VMEM((slots, size, LANES), jnp.bfloat16),
        pltpu.VMEM((row_blocks + 1, size, LANES), jnp.bfloat16),
        pltpu.VMEM((2 * size, LANES), jnp.float32),
    ]
    if step == 0:
        in_specs[5 + plane] = in_specs[5 + plane + freqs] = pl.BlockSpec(memory_space=pltpu.HBM)
        scratch_shapes += [pltpu.VMEM((2, stored, size, size), jnp.float32), pltpu.SemaphoreType.DMA((2,))]
    tile = jax.ShapeDtypeStruct((parts, LANES), jnp.float32)
    own = jax.ShapeDtypeStruct((parts, rows), jnp.float32)
    return pl.pallas_call(
        functools.partial(step_kernel, step, plane, line, freqs),
        in_specs=in_specs,
        out_specs=[vmem] * 4,
        out_shape=[
            jax.ShapeDtypeStruct((plane * line * row_blocks + 1, parts, size), jnp.float32),
            own,
            own,
            tile,
        ],
        scratch_shapes=scratch_shapes,
        compiler_params=pltpu.CompilerParams(vmem_limit_bytes=VMEM_LIMIT),
        name=f"step_{step}",
    )(*lists, turn, info, *lines, *prev, *g_parts, *c_parts)


def final_kernel(plane, *refs):
    tiles, krylov = refs[:plane], refs[plane : plane + ITERS]
    out_ref, residual_ref = refs[plane + ITERS :]
    line, parts, _ = tiles[0].shape
    fit = LANES // parts
    stacked = [tiles[q][i] for q in range(plane) for i in range(line)]
    sets = [
        jnp.transpose(jnp.concatenate(stacked[at : at + fit], axis=0)) for at in range(0, len(stacked), fit)
    ]
    info = jnp.transpose(jnp.concatenate([tiles[0][0]] * fit, axis=0))

    def all_devices(shares):
        total = sum(shares[1:], shares[0])
        step = parts // 2
        while step < LANES:
            total = total + pltpu.roll(total, step, 1)
            step *= 2
        return total

    def row(table, at):
        return jnp.broadcast_to(table[at : at + 1], (8, LANES))

    zero = jnp.zeros((8, LANES), jnp.float32)
    norm, h00, h10, h01, h11, h21 = [row(info, i) for i in range(6)]
    last = [all_devices([row(s, SHARES + i) for s in sets]) for i in range(ITERS)]
    shares = []
    for s in sets:
        off = [last[i] - row(s, SHARES + ITERS + i) for i in range(ITERS)]
        square = row(s, SHARES + 3 * ITERS)
        at = SHARES + 3 * ITERS + 1
        for i in range(ITERS):
            square = square - 2.0 * off[i] * row(s, SHARES + 2 * ITERS + i)
            for j in range(i + 1):
                square = square + (1.0 if i == j else 2.0) * off[i] * off[j] * row(s, at)
                at += 1
        shares.append(square)
    height = jnp.sqrt(jnp.maximum(all_devices(shares), 0.0))
    hessen = [[h00, h01, last[0]], [h10, h11, last[1]], [zero, h21, last[2]], [zero, zero, height]]
    normal = [[sum(h[m] * h[n] for h in hessen) for n in range(ITERS)] for m in range(ITERS)]
    low = [[None] * ITERS for _ in range(ITERS)]
    middle = []
    for m in range(ITERS):
        for n in range(m):
            rest = normal[m][n] - sum((low[m][k] * low[n][k] for k in range(n)), zero)
            low[m][n] = rest / low[n][n]
        low[m][m] = jnp.sqrt(normal[m][m] - sum((low[m][k] * low[m][k] for k in range(m)), zero))
        rest = norm * hessen[0][m] - sum((low[m][k] * middle[k] for k in range(m)), zero)
        middle.append(rest / low[m][m])
    coef_y = [None] * ITERS
    for m in reversed(range(ITERS)):
        rest = middle[m] - sum((low[k][m] * coef_y[k] for k in range(m + 1, ITERS)), zero)
        coef_y[m] = rest / low[m][m]
    total = zero
    for i, h in enumerate(hessen):
        misfit = (norm if i == 0 else zero) - sum(h[m] * coef_y[m] for m in range(ITERS))
        total = total + misfit * misfit
    residual_ref[...] = jnp.sqrt(total)[:1, : parts // 2]
    columns = jnp.transpose(
        jnp.concatenate([y for y in coef_y] + [jnp.zeros((LANES - 8 * ITERS, LANES), jnp.float32)], axis=0)
    )[:parts]
    x = sum(columns[:, 8 * m : 8 * m + 1] * krylov[m][...] for m in range(ITERS))
    out_ref[0] = x[: parts // 2]
    out_ref[1] = x[parts // 2 :]


def run_final(tiles, krylov):
    parts, rows = krylov[0].shape
    vmem = pl.BlockSpec(memory_space=pltpu.VMEM)
    return pl.pallas_call(
        functools.partial(final_kernel, len(tiles)),
        in_specs=[vmem] * (len(tiles) + ITERS),
        out_specs=[vmem] * 2,
        out_shape=[
            jax.ShapeDtypeStruct((2, parts // 2, rows), jnp.float32),
            jax.ShapeDtypeStruct((1, parts // 2), jnp.float32),
        ],
        name="final",
    )(*tiles, *krylov)


def make_shards(line, plane, freqs):
    def shards(excitation, g_blocks, c_blocks, pattern, counts, freq_ids):
        angular = 0.2 * jnp.exp(freq_ids.astype(jnp.float32) * (math.log(8.0) / 1000.0))
        row_blocks, own_slots, size, _ = g_blocks.shape
        freq_count = excitation.shape[1]
        parts = 2 * freq_count
        where = jnp.stack([lax.axis_index(name) for name in ("line", "place", "freq")]).astype(jnp.int32)
        stored = (row_blocks * own_slots, size, size)
        g_parts, c_parts = [], []
        for d in range(freqs):
            perm = [(i, (i + d) % freqs) for i in range(freqs)]
            g_part = lax.ppermute(g_blocks, "freq", perm) if d else g_blocks
            c_part = lax.ppermute(c_blocks, "freq", perm) if d else c_blocks
            g_parts.append(g_part.reshape(stored))
            c_parts.append(c_part.reshape(stored))
        turn = jnp.broadcast_to(jnp.concatenate([-angular, angular])[:, None], (parts, LANES))
        info = jnp.zeros((parts, LANES), jnp.float32)
        krylov, own = [], []
        lists = work_list(pattern, counts, where, line, plane, freqs)
        rows = excitation
        for step in range(ITERS):
            lines = gather_rows(rows, line, plane)
            z, mine, rows, info = run_step(step, lists, turn, info, lines, krylov, g_parts, c_parts)
            krylov.append(z)
            own.append(mine)
        answer, residual = run_final(gather_rows(info, line, plane), own)
        return answer, residual.reshape(freq_count)

    return shards


def solution(mesh):
    line, plane = split_nodes(mesh.shape["node"])
    freqs = mesh.shape["freq"]
    fine = Mesh(mesh.devices.reshape(line, plane, freqs), ("line", "place", "freq"))
    node = ("line", "place")
    in_specs = (
        P(None, "freq", node),
        P(node, "freq", None, None),
        P(node, "freq", None, None),
        P(node, None),
        P(node),
        P("freq"),
    )
    out_specs = (P(None, "freq", node), P("freq"))
    shards = make_shards(line, plane, freqs)
    return jax.shard_map(shards, mesh=fine, in_specs=in_specs, out_specs=out_specs, check_vma=False)
```

```python
import functools
import math

import jax
import jax.numpy as jnp
from jax import lax
from jax.experimental import pallas as pl
from jax.experimental.pallas import tpu as pltpu
from jax.sharding import Mesh
from jax.sharding import PartitionSpec as P

ITERS = 3
LANES = 128
GROUP = 4
FULL_GROUP = 8
SHARES = 16
VMEM_LIMIT = 16 * 1024 * 1024


def split_nodes(nodes):
    plane = 4 if nodes % 4 == 0 else 1
    return nodes // plane, plane


def partner_steps(size):
    if size & (size - 1) == 0:
        return [[(i, i ^ d) for i in range(size)] for d in range(1, size)]
    return [[(i, (i + d) % size) for i in range(size)] for d in range(1, size)]


def distance(me, other, size):
    if size & (size - 1) == 0:
        return me ^ other
    return lax.rem(me - other + size, size)


def gather_rows(rows, line, plane):
    parts = rows.size // rows.shape[-1]
    held = [rows] + [lax.ppermute(rows, "line", perm) for perm in partner_steps(line)]
    whole_line = jnp.stack(held).reshape(line, parts, rows.shape[-1])
    return [whole_line] + [lax.ppermute(whole_line, "place", perm) for perm in partner_steps(plane)]


def work_list(pattern, counts, where, line, plane, freqs):
    row_blocks, slots = pattern.shape
    own_slots = slots // freqs
    owner = lax.div(pattern, row_blocks)
    far = distance(where[0], lax.div(owner, plane), line)
    place = distance(where[1], lax.rem(owner, plane), plane) * line + far
    place = place * row_blocks + lax.rem(pattern, row_blocks)
    slot = jnp.arange(slots)
    places = jnp.where(slot[None, :] < counts[:, None], place, line * plane * row_blocks).T
    b = jnp.arange(row_blocks)
    order = jnp.arange(row_blocks * slots)
    tables = []
    for d in list(range(freqs)) + [None]:
        first = 0 if d is None else lax.rem(where[2] + (freqs - d), freqs) * own_slots
        group = FULL_GROUP if d is None else GROUP
        here = counts if d is None else jnp.clip(counts - first, 0, own_slots)
        start = jnp.sum(jnp.where(b[None, :] < b[:, None], here[None, :], 0), axis=1)
        inside = order[:, None] - start[None, :]
        hit = (inside >= 0) & (inside < here[None, :])
        layer = first + jnp.sum(jnp.where(hit, inside, 0), axis=1)
        block = jnp.sum(jnp.where(hit, b[None, :], 0), axis=1)
        away = lax.rem(where[2] - lax.div(layer, own_slots) + freqs, freqs)
        stored = (away * row_blocks + block) * own_slots + lax.rem(layer, own_slots)
        used = jnp.sum(here)
        block = jnp.where(order < used, block, row_blocks)
        tables += [layer, block, stored, jnp.full(order.shape, lax.div(used + (group - 1), group))]
    return jnp.stack(tables).astype(jnp.int32), places.astype(jnp.int32)


def lane_sum(x):
    return jnp.sum(x, axis=1, keepdims=True)


def with_other_part(column):
    wide = jnp.broadcast_to(column, (column.shape[0], LANES))
    return wide + pltpu.roll(wide, column.shape[0] // 2, 0)


def put_lane(tile, lane, column):
    at = lax.broadcasted_iota(jnp.int32, tile.shape, 1) == lane
    return jnp.where(at, column, tile)


def split(x):
    high = x.astype(jnp.bfloat16)
    return high, (x - high.astype(jnp.float32)).astype(jnp.bfloat16)


def step_kernel(step, plane, line, freqs, items_ref, places_ref, turn_ref, info_in_ref, *refs):
    lines, refs = refs[:plane], refs[plane:]
    prev, refs = refs[:step], refs[step:]
    slots, row_blocks = places_ref.shape
    nodes = plane * line
    if step == 0:
        g_refs, c_refs = refs[:freqs], refs[freqs : 2 * freqs]
        z_ref, local_ref, info_ref, split_ref, layer_ref, mask_ref, acc_ref = refs[2 * freqs :]
    elif step < ITERS - 1:
        split_ref, z_ref, local_ref, info_ref, layer_ref, mask_ref, acc_ref = refs
    else:
        split_ref, own_ref, info_ref, layer_ref, mask_ref, acc_ref, z_ref, local_ref = refs
    parts, rows = local_ref.shape
    size = rows // row_blocks

    lane = lax.broadcasted_iota(jnp.int32, (size, LANES), 1)
    for b in range(row_blocks):
        mask_ref[b] = jnp.where((lane // parts) % row_blocks == b, 1.0, 0.0).astype(jnp.bfloat16)
    mask_ref[row_blocks] = jnp.zeros((size, LANES), jnp.bfloat16)
    acc_ref[...] = jnp.zeros_like(acc_ref)
    z_ref[nodes * row_blocks] = jnp.zeros((parts, size), jnp.float32)

    def blocks(body, carry):
        for q in range(plane):

            def chunk(i, carry, q=q):
                x = lines[q][i]
                for b in range(row_blocks):
                    carry = body(b, x[:, b * size : (b + 1) * size], (q * line + i) * row_blocks + b, carry)
                return carry

            if line <= 4:
                for i in range(line):
                    carry = chunk(i, carry)
            else:
                carry = lax.fori_loop(0, line, chunk, carry)
        return carry

    def add(sums, b, term):
        return sums[:b] + (sums[b] + term,) + sums[b + 1 :]

    def whole(sums):
        while len(sums) > 1:
            sums = tuple(x + y for x, y in zip(sums[::2], sums[1::2])) + sums[len(sums) // 2 * 2 :]
        return with_other_part(lane_sum(sums[0]))

    none = (jnp.zeros((parts, size), jnp.float32),) * row_blocks
    info = info_in_ref[...]
    if step == 0:
        height = jnp.sqrt(whole(blocks(lambda b, x, at, sums: add(sums, b, x * x), none)))
        info = put_lane(info, 0, height)

        def normal(b, x, at, carry):
            z_ref[at] = x / height
            return carry
    else:
        first = 1 if step == 1 else 3

        def dot(b, x, at, sums):
            return tuple(add(s, b, p[at] * x) for s, p in zip(sums, prev))

        coeffs = [whole(s) for s in blocks(dot, (none,) * step)]
        for i, coeff in enumerate(coeffs):
            info = put_lane(info, first + i, coeff)

        def subtract(b, x, at, sums):
            for coeff, p in zip(coeffs, prev):
                x = x - coeff * p[at]
            z_ref[at] = x
            return add(sums, b, x * x)

        height = jnp.sqrt(whole(blocks(subtract, none)))
        info = put_lane(info, first + step, height)

        def normal(b, x, at, carry):
            z_ref[at] = z_ref[at] / height
            return carry

    blocks(normal, 0)

    for k in range(slots):
        chosen = jnp.concatenate([z_ref[places_ref[k, b]] for b in range(row_blocks)], axis=0)
        high = chosen.astype(jnp.bfloat16).astype(jnp.float32)
        layer_ref[k] = jnp.transpose(jnp.concatenate([high, chosen - high], axis=0)).astype(jnp.bfloat16)

    def product(table, t, left):
        right = layer_ref[items_ref[table, t]] * mask_ref[items_ref[table + 1, t]]
        right = jnp.concatenate([right, right], axis=0)
        return jnp.dot(left, right, preferred_element_type=jnp.float32)

    if step == 0:
        for d in range(freqs):

            @pl.loop(0, items_ref[4 * d + 3, 0])
            def _(group):
                total = acc_ref[...]
                for u in range(GROUP):
                    t = group * GROUP + u
                    stored = items_ref[4 * d + 2, t]
                    here = stored - d * g_refs[d].shape[0]
                    high, low = split(jnp.concatenate([g_refs[d][here], c_refs[d][here]], axis=0))
                    left = jnp.concatenate([high, low], axis=1)
                    split_ref[stored] = left
                    total = total + product(4 * d, t, left)
                acc_ref[...] = total
    else:

        @pl.loop(0, items_ref[4 * freqs + 3, 0])
        def _(group):
            total = acc_ref[...]
            for u in range(FULL_GROUP):
                t = group * FULL_GROUP + u
                total = total + product(4 * freqs, t, split_ref[items_ref[4 * freqs + 2, t]])
            acc_ref[...] = total

    half = row_blocks * parts
    gsum, csum = jnp.transpose(acc_ref[:size]), jnp.transpose(acc_ref[size:])
    gsum, csum = gsum[:half] + gsum[half:], csum[:half] + csum[half:]
    turn = turn_ref[...]
    for b in range(row_blocks):
        at = slice(b * parts, (b + 1) * parts)
        other = pltpu.roll(csum[at], parts // 2, 0)
        local_ref[:, b * size : (b + 1) * size] = gsum[at] + turn * other

    if step == ITERS - 1:
        w = local_ref[...]
        zs = [jnp.concatenate([p[b] for b in range(row_blocks)], axis=1) for p in (*prev, z_ref)]
        own_ref[...] = zs[-1]
        values = [lane_sum(z * w) for z in zs]
        gram = [[lane_sum(zs[i] * zs[j]) for j in range(i + 1)] for i in range(ITERS)]
        shares = []
        for i, z in enumerate(zs):
            along = lane_sum(z * w) if i else values[0]
            share = jnp.where(gram[i][i] > 0.0, along / gram[i][i], 0.0)
            shares.append(share)
            w = w - share * z
        values += shares + [lane_sum(z * w) for z in zs] + [lane_sum(w * w)]
        values += [gram[i][j] for i in range(ITERS) for j in range(i + 1)]
        for lane_at, value in enumerate(values):
            info = put_lane(info, SHARES + lane_at, value)
    info_ref[...] = info


def run_step(step, lists, turn, info, lines, prev, blocks, freqs):
    plane = len(lines)
    line, parts, rows = lines[0].shape
    slots, row_blocks = lists[1].shape
    size = rows // row_blocks
    vmem = pl.BlockSpec(memory_space=pltpu.VMEM)
    in_specs = [pl.BlockSpec(memory_space=pltpu.SMEM)] * 2 + [vmem] * (2 + plane + step + len(blocks))
    z = (plane * line * row_blocks + 1, parts, size)
    tile = jax.ShapeDtypeStruct((parts, LANES), jnp.float32)
    own = jax.ShapeDtypeStruct((parts, rows), jnp.float32)
    out_shape = [own, tile] if step == ITERS - 1 else [jax.ShapeDtypeStruct(z, jnp.float32), own, tile]
    scratch_shapes = [
        pltpu.VMEM((slots, size, LANES), jnp.bfloat16),
        pltpu.VMEM((row_blocks + 1, size, LANES), jnp.bfloat16),
        pltpu.VMEM((2 * size, LANES), jnp.float32),
    ]
    if step == 0:
        out_shape.append(jax.ShapeDtypeStruct((row_blocks * slots, 2 * size, 2 * size), jnp.bfloat16))
    if step == ITERS - 1:
        scratch_shapes += [pltpu.VMEM(z, jnp.float32), pltpu.VMEM((parts, rows), jnp.float32)]
    return pl.pallas_call(
        functools.partial(step_kernel, step, plane, line, freqs),
        in_specs=in_specs,
        out_specs=[vmem] * len(out_shape),
        out_shape=out_shape,
        scratch_shapes=scratch_shapes,
        compiler_params=pltpu.CompilerParams(vmem_limit_bytes=VMEM_LIMIT),
        name=f"step_{step}",
    )(*lists, turn, info, *lines, *prev, *blocks)


def final_kernel(plane, *refs):
    tiles, krylov = refs[:plane], refs[plane : plane + ITERS]
    out_ref, residual_ref = refs[plane + ITERS :]
    line, parts, _ = tiles[0].shape
    fit = LANES // parts
    stacked = [tiles[q][i] for q in range(plane) for i in range(line)]
    sets = [
        jnp.transpose(jnp.concatenate(stacked[at : at + fit], axis=0)) for at in range(0, len(stacked), fit)
    ]
    info = jnp.transpose(jnp.concatenate([tiles[0][0]] * fit, axis=0))

    def all_devices(shares):
        total = sum(shares[1:], shares[0])
        step = parts // 2
        while step < LANES:
            total = total + pltpu.roll(total, step, 1)
            step *= 2
        return total

    def row(table, at):
        return jnp.broadcast_to(table[at : at + 1], (8, LANES))

    zero = jnp.zeros((8, LANES), jnp.float32)
    norm, h00, h10, h01, h11, h21 = [row(info, i) for i in range(6)]
    last = [all_devices([row(s, SHARES + i) for s in sets]) for i in range(ITERS)]
    shares = []
    for s in sets:
        off = [last[i] - row(s, SHARES + ITERS + i) for i in range(ITERS)]
        square = row(s, SHARES + 3 * ITERS)
        at = SHARES + 3 * ITERS + 1
        for i in range(ITERS):
            square = square - 2.0 * off[i] * row(s, SHARES + 2 * ITERS + i)
            for j in range(i + 1):
                square = square + (1.0 if i == j else 2.0) * off[i] * off[j] * row(s, at)
                at += 1
        shares.append(square)
    height = jnp.sqrt(jnp.maximum(all_devices(shares), 0.0))
    hessen = [[h00, h01, last[0]], [h10, h11, last[1]], [zero, h21, last[2]], [zero, zero, height]]
    normal = [[sum(h[m] * h[n] for h in hessen) for n in range(ITERS)] for m in range(ITERS)]
    low = [[None] * ITERS for _ in range(ITERS)]
    middle = []
    for m in range(ITERS):
        for n in range(m):
            rest = normal[m][n] - sum((low[m][k] * low[n][k] for k in range(n)), zero)
            low[m][n] = rest / low[n][n]
        low[m][m] = jnp.sqrt(normal[m][m] - sum((low[m][k] * low[m][k] for k in range(m)), zero))
        rest = norm * hessen[0][m] - sum((low[m][k] * middle[k] for k in range(m)), zero)
        middle.append(rest / low[m][m])
    coef_y = [None] * ITERS
    for m in reversed(range(ITERS)):
        rest = middle[m] - sum((low[k][m] * coef_y[k] for k in range(m + 1, ITERS)), zero)
        coef_y[m] = rest / low[m][m]
    total = zero
    for i, h in enumerate(hessen):
        misfit = (norm if i == 0 else zero) - sum(h[m] * coef_y[m] for m in range(ITERS))
        total = total + misfit * misfit
    residual_ref[...] = jnp.sqrt(total)[:1, : parts // 2]
    columns = jnp.transpose(
        jnp.concatenate([y for y in coef_y] + [jnp.zeros((LANES - 8 * ITERS, LANES), jnp.float32)], axis=0)
    )[:parts]
    size = krylov[0].shape[-1]
    wide = [jnp.broadcast_to(columns[:, 8 * m : 8 * m + 1], (parts, size)) for m in range(ITERS)]
    for b in range(out_ref.shape[-1] // size):
        at = slice(b * size, (b + 1) * size)
        x = wide[-1] * krylov[-1][:, at] + sum(y * z[b] for y, z in zip(wide[:-1], krylov[:-1]))
        out_ref[0, :, at] = x[: parts // 2]
        out_ref[1, :, at] = x[parts // 2 :]


def run_final(tiles, krylov):
    parts, rows = krylov[-1].shape
    vmem = pl.BlockSpec(memory_space=pltpu.VMEM)
    return pl.pallas_call(
        functools.partial(final_kernel, len(tiles)),
        in_specs=[vmem] * (len(tiles) + ITERS),
        out_specs=[vmem] * 2,
        out_shape=[
            jax.ShapeDtypeStruct((2, parts // 2, rows), jnp.float32),
            jax.ShapeDtypeStruct((1, parts // 2), jnp.float32),
        ],
        name="final",
    )(*tiles, *krylov)


def make_shards(line, plane, freqs):
    def shards(excitation, g_blocks, c_blocks, pattern, counts, freq_ids):
        angular = 0.2 * jnp.exp(freq_ids.astype(jnp.float32) * (math.log(8.0) / 1000.0))
        row_blocks, own_slots, size, _ = g_blocks.shape
        freq_count = excitation.shape[1]
        parts = 2 * freq_count
        where = jnp.stack([lax.axis_index(name) for name in ("line", "place", "freq")]).astype(jnp.int32)
        stored = (row_blocks * own_slots, size, size)
        slot = lax.axis_index("freq") * own_slots + jnp.arange(own_slots)
        in_use = (slot[None, :] < counts[:, None])[:, :, None, None]
        g_parts, c_parts = [], []
        for d in range(freqs):
            perm = [(i, (i + d) % freqs) for i in range(freqs)]
            g_part = lax.ppermute(g_blocks, "freq", perm) if d else jnp.where(in_use, g_blocks, 0.0)
            c_part = lax.ppermute(c_blocks, "freq", perm) if d else jnp.where(in_use, c_blocks, 0.0)
            g_parts.append(g_part.reshape(stored))
            c_parts.append(c_part.reshape(stored))
        turn = jnp.broadcast_to(jnp.concatenate([-angular, angular])[:, None], (parts, LANES))
        info = jnp.zeros((parts, LANES), jnp.float32)
        lists = work_list(pattern, counts, where, line, plane, freqs)
        krylov = []
        rows = excitation
        blocks = g_parts + c_parts
        for step in range(ITERS):
            lines = gather_rows(rows, line, plane)
            result = run_step(step, lists, turn, info, lines, krylov, blocks, freqs)
            if step == ITERS - 1:
                rows, info = result
                krylov.append(rows)
            elif step == 0:
                z, rows, info, tiles = result
                blocks = [tiles]
                krylov.append(z)
            else:
                z, rows, info = result
                krylov.append(z)
        answer, residual = run_final(gather_rows(info, line, plane), krylov)
        return answer, residual.reshape(freq_count)

    return shards


def solution(mesh):
    line, plane = split_nodes(mesh.shape["node"])
    freqs = mesh.shape["freq"]
    fine = Mesh(mesh.devices.reshape(line, plane, freqs), ("line", "place", "freq"))
    node = ("line", "place")
    in_specs = (
        P(None, "freq", node),
        P(node, "freq", None, None),
        P(node, "freq", None, None),
        P(node, None),
        P(node),
        P("freq"),
    )
    out_specs = (P(None, "freq", node), P("freq"))
    shards = make_shards(line, plane, freqs)
    return jax.shard_map(shards, mesh=fine, in_specs=in_specs, out_specs=out_specs, check_vma=False)
```

```python
import functools
import math

import jax
import jax.numpy as jnp
from jax import lax
from jax.experimental import pallas as pl
from jax.experimental.pallas import tpu as pltpu
from jax.sharding import Mesh
from jax.sharding import PartitionSpec as P

ITERS = 3
LANES = 128
GROUP = 4
FULL_GROUP = 8
SHARES = 16
VMEM_LIMIT = 16 * 1024 * 1024


def split_nodes(nodes):
    plane = 4 if nodes % 4 == 0 else 1
    return nodes // plane, plane


def partner_steps(size):
    if size & (size - 1) == 0:
        return [[(i, i ^ d) for i in range(size)] for d in range(1, size)]
    return [[(i, (i + d) % size) for i in range(size)] for d in range(1, size)]


def distance(me, other, size):
    if size & (size - 1) == 0:
        return me ^ other
    return lax.rem(me - other + size, size)


def gather_rows(rows, line, plane):
    parts = rows.size // rows.shape[-1]
    held = [rows] + [lax.ppermute(rows, "line", perm) for perm in partner_steps(line)]
    whole_line = jnp.stack(held).reshape(line, parts, rows.shape[-1])
    return [whole_line] + [lax.ppermute(whole_line, "place", perm) for perm in partner_steps(plane)]


def setup_kernel(
    line, plane, freqs, pattern_ref, counts_ref, where_ref, ids_ref, g_ref, c_ref,
    items_ref, places_ref, turn_ref, g_out_ref, c_out_ref, sems,
):
    row_blocks, slots = pattern_ref.shape
    own_slots = slots // freqs
    pieces = sems.shape[1]
    part = g_ref.shape[0] // pieces
    copies = []
    for m, (source, target) in enumerate(((g_ref, g_out_ref), (c_ref, c_out_ref))):
        for i in range(pieces):
            at = pl.ds(i * part, part)
            copies.append(pltpu.make_async_copy(source.at[at], target.at[at], sems.at[m, i]))
            copies[-1].start()

    order = lax.broadcasted_iota(jnp.int32, (8, LANES), 1)
    freq = where_ref[2]
    for table, d in enumerate(list(range(freqs)) + [None]):
        first = 0 if d is None else lax.rem(freq + (freqs - d), freqs) * own_slots
        group = FULL_GROUP if d is None else GROUP
        layer = jnp.zeros((8, LANES), jnp.int32) + first
        block = jnp.full((8, LANES), row_blocks, jnp.int32)
        home = jnp.zeros((8, LANES), jnp.int32)
        used = jnp.int32(0)
        for b in range(row_blocks):
            here = counts_ref[b] if d is None else jnp.clip(counts_ref[b] - first, 0, own_slots)
            inside = order - used
            hit = (inside >= 0) & (inside < here)
            layer = jnp.where(hit, first + inside, layer)
            block = jnp.where(hit, b, block)
            home = jnp.where(hit, b, home)
            used = used + here
        away = freq - lax.div(layer, own_slots)
        away = jnp.where(away < 0, away + freqs, away)
        stored = (away * row_blocks + home) * own_slots + lax.rem(layer, own_slots)
        groups = jnp.zeros((8, LANES), jnp.int32) + lax.div(used + (group - 1), group)
        for i, values in enumerate((layer, block, stored, groups)):
            items_ref[4 * table + i : 4 * table + i + 1, :] = values[:1]

    pattern = pattern_ref[...]
    owner = lax.div(pattern, row_blocks)
    far = distance(where_ref[0], lax.div(owner, plane), line)
    place = distance(where_ref[1], lax.rem(owner, plane), plane) * line + far
    place = place * row_blocks + lax.rem(pattern, row_blocks)
    b_at = lax.broadcasted_iota(jnp.int32, pattern.shape, 0)
    k_at = lax.broadcasted_iota(jnp.int32, pattern.shape, 1)
    count = jnp.zeros(pattern.shape, jnp.int32)
    for b in range(row_blocks):
        count = jnp.where(b_at == b, counts_ref[b], count)
    places_ref[...] = jnp.where(k_at < count, place, line * plane * row_blocks)

    half = turn_ref.shape[0] // 2
    row_at = lax.broadcasted_iota(jnp.int32, turn_ref.shape, 0)
    ids = jnp.zeros(turn_ref.shape, jnp.int32)
    for f in range(half):
        ids = jnp.where(lax.rem(row_at, half) == f, ids_ref[f], ids)
    angular = 0.2 * jnp.exp(ids.astype(jnp.float32) * (math.log(8.0) / 1000.0))
    turn_ref[...] = jnp.where(row_at < half, -angular, angular)
    for copy in copies:
        copy.wait()


def run_setup(pattern, counts, where, freq_ids, g_own, c_own, line, plane, freqs):
    smem, vmem = pl.BlockSpec(memory_space=pltpu.SMEM), pl.BlockSpec(memory_space=pltpu.VMEM)
    far = pl.BlockSpec(memory_space=pl.ANY)
    blocks = jax.ShapeDtypeStruct(g_own.shape, jnp.float32)
    pieces = math.gcd(g_own.shape[0], 8)
    return pl.pallas_call(
        functools.partial(setup_kernel, line, plane, freqs),
        in_specs=[vmem, smem, smem, smem, far, far],
        out_specs=[vmem] * 5,
        out_shape=[
            jax.ShapeDtypeStruct((4 * (freqs + 1), LANES), jnp.int32),
            jax.ShapeDtypeStruct(pattern.shape, jnp.int32),
            jax.ShapeDtypeStruct((2 * freq_ids.shape[0], LANES), jnp.float32),
            blocks,
            blocks,
        ],
        scratch_shapes=[pltpu.SemaphoreType.DMA((2, pieces))],
        compiler_params=pltpu.CompilerParams(vmem_limit_bytes=VMEM_LIMIT),
        cost_estimate=pl.CostEstimate(flops=0, bytes_accessed=16 * g_own.size, transcendentals=0),
        name="setup",
    )(pattern, counts, where, freq_ids, g_own, c_own)


def lane_sum(x):
    return jnp.sum(x, axis=1, keepdims=True)


def with_other_part(column):
    wide = jnp.broadcast_to(column, (column.shape[0], LANES))
    return wide + pltpu.roll(wide, column.shape[0] // 2, 0)


def put_lane(tile, lane, column):
    at = lax.broadcasted_iota(jnp.int32, tile.shape, 1) == lane
    return jnp.where(at, column, tile)


def split(x):
    high = x.astype(jnp.bfloat16)
    return high, (x - high.astype(jnp.float32)).astype(jnp.bfloat16)


def step_kernel(step, plane, line, freqs, items_ref, places_ref, turn_ref, info_in_ref, *refs):
    lines, refs = refs[:plane], refs[plane:]
    prev, refs = refs[:step], refs[step:]
    row_blocks, slots = places_ref.shape
    nodes = plane * line
    if step == 0:
        g_refs, c_refs = refs[:freqs], refs[freqs : 2 * freqs]
        z_ref, local_ref, info_ref, split_ref, layer_ref, mask_ref, acc_ref = refs[2 * freqs :]
    elif step < ITERS - 1:
        split_ref, z_ref, local_ref, info_ref, layer_ref, mask_ref, acc_ref = refs
    else:
        split_ref, own_ref, info_ref, layer_ref, mask_ref, acc_ref, z_ref, local_ref = refs
    parts, rows = local_ref.shape
    size = rows // row_blocks

    lane = lax.broadcasted_iota(jnp.int32, (size, LANES), 1)
    for b in range(row_blocks):
        mask_ref[b] = jnp.where((lane // parts) % row_blocks == b, 1.0, 0.0).astype(jnp.bfloat16)
    mask_ref[row_blocks] = jnp.zeros((size, LANES), jnp.bfloat16)
    acc_ref[...] = jnp.zeros_like(acc_ref)
    z_ref[nodes * row_blocks] = jnp.zeros((parts, size), jnp.float32)

    def blocks(body, carry):
        for q in range(plane):

            def chunk(i, carry, q=q):
                x = lines[q][i]
                for b in range(row_blocks):
                    carry = body(b, x[:, b * size : (b + 1) * size], (q * line + i) * row_blocks + b, carry)
                return carry

            if line <= 4:
                for i in range(line):
                    carry = chunk(i, carry)
            else:
                carry = lax.fori_loop(0, line, chunk, carry)
        return carry

    def add(sums, b, term):
        return sums[:b] + (sums[b] + term,) + sums[b + 1 :]

    def whole(sums):
        while len(sums) > 1:
            sums = tuple(x + y for x, y in zip(sums[::2], sums[1::2])) + sums[len(sums) // 2 * 2 :]
        return with_other_part(lane_sum(sums[0]))

    none = (jnp.zeros((parts, size), jnp.float32),) * row_blocks
    info = info_in_ref[...]
    if step == 0:
        height = jnp.sqrt(whole(blocks(lambda b, x, at, sums: add(sums, b, x * x), none)))
        info = put_lane(info, 0, height)

        def normal(b, x, at, carry):
            z_ref[at] = x / height
            return carry
    else:
        first = 1 if step == 1 else 3

        def dot(b, x, at, sums):
            return tuple(add(s, b, p[at] * x) for s, p in zip(sums, prev))

        coeffs = [whole(s) for s in blocks(dot, (none,) * step)]
        for i, coeff in enumerate(coeffs):
            info = put_lane(info, first + i, coeff)

        def subtract(b, x, at, sums):
            for coeff, p in zip(coeffs, prev):
                x = x - coeff * p[at]
            z_ref[at] = x
            return add(sums, b, x * x)

        height = jnp.sqrt(whole(blocks(subtract, none)))
        info = put_lane(info, first + step, height)

        def normal(b, x, at, carry):
            z_ref[at] = z_ref[at] / height
            return carry

    blocks(normal, 0)

    for k in range(slots):
        chosen = jnp.concatenate([z_ref[places_ref[b, k]] for b in range(row_blocks)], axis=0)
        high = chosen.astype(jnp.bfloat16).astype(jnp.float32)
        layer_ref[k] = jnp.transpose(jnp.concatenate([high, chosen - high], axis=0)).astype(jnp.bfloat16)

    def product(table, t, left):
        right = layer_ref[items_ref[table, t]] * mask_ref[items_ref[table + 1, t]]
        right = jnp.concatenate([right, right], axis=0)
        return jnp.dot(left, right, preferred_element_type=jnp.float32)

    if step == 0:
        for d in range(freqs):

            @pl.loop(0, items_ref[4 * d + 3, 0])
            def _(group):
                total = acc_ref[...]
                for u in range(GROUP):
                    t = group * GROUP + u
                    stored = items_ref[4 * d + 2, t]
                    here = stored - d * g_refs[d].shape[0]
                    high, low = split(jnp.concatenate([g_refs[d][here], c_refs[d][here]], axis=0))
                    left = jnp.concatenate([high, low], axis=1)
                    split_ref[stored] = left
                    total = total + product(4 * d, t, left)
                acc_ref[...] = total
    else:

        @pl.loop(0, items_ref[4 * freqs + 3, 0])
        def _(group):
            total = acc_ref[...]
            for u in range(FULL_GROUP):
                t = group * FULL_GROUP + u
                total = total + product(4 * freqs, t, split_ref[items_ref[4 * freqs + 2, t]])
            acc_ref[...] = total

    half = row_blocks * parts
    gsum, csum = jnp.transpose(acc_ref[:size]), jnp.transpose(acc_ref[size:])
    gsum, csum = gsum[:half] + gsum[half:], csum[:half] + csum[half:]
    turn = turn_ref[...]
    for b in range(row_blocks):
        at = slice(b * parts, (b + 1) * parts)
        other = pltpu.roll(csum[at], parts // 2, 0)
        local_ref[:, b * size : (b + 1) * size] = gsum[at] + turn * other

    if step == ITERS - 1:
        w = local_ref[...]
        zs = [jnp.concatenate([p[b] for b in range(row_blocks)], axis=1) for p in (*prev, z_ref)]
        own_ref[...] = zs[-1]
        values = [lane_sum(z * w) for z in zs]
        gram = [[lane_sum(zs[i] * zs[j]) for j in range(i + 1)] for i in range(ITERS)]
        shares = []
        for i, z in enumerate(zs):
            along = lane_sum(z * w) if i else values[0]
            share = jnp.where(gram[i][i] > 0.0, along / gram[i][i], 0.0)
            shares.append(share)
            w = w - share * z
        values += shares + [lane_sum(z * w) for z in zs] + [lane_sum(w * w)]
        values += [gram[i][j] for i in range(ITERS) for j in range(i + 1)]
        for lane_at, value in enumerate(values):
            info = put_lane(info, SHARES + lane_at, value)
    info_ref[...] = info


def run_step(step, lists, turn, info, lines, prev, blocks, freqs):
    plane = len(lines)
    line, parts, rows = lines[0].shape
    row_blocks, slots = lists[1].shape
    size = rows // row_blocks
    vmem = pl.BlockSpec(memory_space=pltpu.VMEM)
    in_specs = [pl.BlockSpec(memory_space=pltpu.SMEM)] * 2 + [vmem] * (2 + plane + step + len(blocks))
    z = (plane * line * row_blocks + 1, parts, size)
    tile = jax.ShapeDtypeStruct((parts, LANES), jnp.float32)
    own = jax.ShapeDtypeStruct((parts, rows), jnp.float32)
    out_shape = [own, tile] if step == ITERS - 1 else [jax.ShapeDtypeStruct(z, jnp.float32), own, tile]
    scratch_shapes = [
        pltpu.VMEM((slots, size, LANES), jnp.bfloat16),
        pltpu.VMEM((row_blocks + 1, size, LANES), jnp.bfloat16),
        pltpu.VMEM((2 * size, LANES), jnp.float32),
    ]
    if step == 0:
        out_shape.append(jax.ShapeDtypeStruct((row_blocks * slots, 2 * size, 2 * size), jnp.bfloat16))
    if step == ITERS - 1:
        scratch_shapes += [pltpu.VMEM(z, jnp.float32), pltpu.VMEM((parts, rows), jnp.float32)]
    return pl.pallas_call(
        functools.partial(step_kernel, step, plane, line, freqs),
        in_specs=in_specs,
        out_specs=[vmem] * len(out_shape),
        out_shape=out_shape,
        scratch_shapes=scratch_shapes,
        compiler_params=pltpu.CompilerParams(vmem_limit_bytes=VMEM_LIMIT),
        name=f"step_{step}",
    )(*lists, turn, info, *lines, *prev, *blocks)


def final_kernel(plane, *refs):
    tiles, krylov = refs[:plane], refs[plane : plane + ITERS]
    out_ref, residual_ref = refs[plane + ITERS :]
    line, parts, _ = tiles[0].shape
    fit = LANES // parts
    stacked = [tiles[q][i] for q in range(plane) for i in range(line)]
    sets = [
        jnp.transpose(jnp.concatenate(stacked[at : at + fit], axis=0)) for at in range(0, len(stacked), fit)
    ]
    info = jnp.transpose(jnp.concatenate([tiles[0][0]] * fit, axis=0))

    def all_devices(shares):
        total = sum(shares[1:], shares[0])
        step = parts // 2
        while step < LANES:
            total = total + pltpu.roll(total, step, 1)
            step *= 2
        return total

    def row(table, at):
        return jnp.broadcast_to(table[at : at + 1], (8, LANES))

    zero = jnp.zeros((8, LANES), jnp.float32)
    norm, h00, h10, h01, h11, h21 = [row(info, i) for i in range(6)]
    last = [all_devices([row(s, SHARES + i) for s in sets]) for i in range(ITERS)]
    shares = []
    for s in sets:
        off = [last[i] - row(s, SHARES + ITERS + i) for i in range(ITERS)]
        square = row(s, SHARES + 3 * ITERS)
        at = SHARES + 3 * ITERS + 1
        for i in range(ITERS):
            square = square - 2.0 * off[i] * row(s, SHARES + 2 * ITERS + i)
            for j in range(i + 1):
                square = square + (1.0 if i == j else 2.0) * off[i] * off[j] * row(s, at)
                at += 1
        shares.append(square)
    height = jnp.sqrt(jnp.maximum(all_devices(shares), 0.0))
    hessen = [[h00, h01, last[0]], [h10, h11, last[1]], [zero, h21, last[2]], [zero, zero, height]]
    normal = [[sum(h[m] * h[n] for h in hessen) for n in range(ITERS)] for m in range(ITERS)]
    low = [[None] * ITERS for _ in range(ITERS)]
    middle = []
    for m in range(ITERS):
        for n in range(m):
            rest = normal[m][n] - sum((low[m][k] * low[n][k] for k in range(n)), zero)
            low[m][n] = rest / low[n][n]
        low[m][m] = jnp.sqrt(normal[m][m] - sum((low[m][k] * low[m][k] for k in range(m)), zero))
        rest = norm * hessen[0][m] - sum((low[m][k] * middle[k] for k in range(m)), zero)
        middle.append(rest / low[m][m])
    coef_y = [None] * ITERS
    for m in reversed(range(ITERS)):
        rest = middle[m] - sum((low[k][m] * coef_y[k] for k in range(m + 1, ITERS)), zero)
        coef_y[m] = rest / low[m][m]
    total = zero
    for i, h in enumerate(hessen):
        misfit = (norm if i == 0 else zero) - sum(h[m] * coef_y[m] for m in range(ITERS))
        total = total + misfit * misfit
    residual_ref[...] = jnp.sqrt(total)[:1, : parts // 2]
    columns = jnp.transpose(
        jnp.concatenate([y for y in coef_y] + [jnp.zeros((LANES - 8 * ITERS, LANES), jnp.float32)], axis=0)
    )[:parts]
    size = krylov[0].shape[-1]
    wide = [jnp.broadcast_to(columns[:, 8 * m : 8 * m + 1], (parts, size)) for m in range(ITERS)]
    for b in range(out_ref.shape[-1] // size):
        at = slice(b * size, (b + 1) * size)
        x = wide[-1] * krylov[-1][:, at] + sum(y * z[b] for y, z in zip(wide[:-1], krylov[:-1]))
        out_ref[0, :, at] = x[: parts // 2]
        out_ref[1, :, at] = x[parts // 2 :]


def run_final(tiles, krylov):
    parts, rows = krylov[-1].shape
    vmem = pl.BlockSpec(memory_space=pltpu.VMEM)
    return pl.pallas_call(
        functools.partial(final_kernel, len(tiles)),
        in_specs=[vmem] * (len(tiles) + ITERS),
        out_specs=[vmem] * 2,
        out_shape=[
            jax.ShapeDtypeStruct((2, parts // 2, rows), jnp.float32),
            jax.ShapeDtypeStruct((1, parts // 2), jnp.float32),
        ],
        name="final",
    )(*tiles, *krylov)


def make_shards(line, plane, freqs):
    def shards(excitation, g_blocks, c_blocks, pattern, counts, freq_ids):
        row_blocks, own_slots, size, _ = g_blocks.shape
        freq_count = excitation.shape[1]
        parts = 2 * freq_count
        where = jnp.stack([lax.axis_index(name) for name in ("line", "place", "freq")]).astype(jnp.int32)
        stored = (row_blocks * own_slots, size, size)
        g_own, c_own = g_blocks.reshape(stored), c_blocks.reshape(stored)
        *lists, turn, g_near, c_near = run_setup(
            pattern, counts, where, freq_ids, g_own, c_own, line, plane, freqs
        )
        g_parts, c_parts = [g_near], [c_near]
        for d in range(1, freqs):
            perm = [(i, (i + d) % freqs) for i in range(freqs)]
            g_parts.append(lax.ppermute(g_own, "freq", perm))
            c_parts.append(lax.ppermute(c_own, "freq", perm))
        info = jnp.zeros((parts, LANES), jnp.float32)
        krylov = []
        rows = excitation
        blocks = g_parts + c_parts
        for step in range(ITERS):
            lines = gather_rows(rows, line, plane)
            result = run_step(step, lists, turn, info, lines, krylov, blocks, freqs)
            if step == ITERS - 1:
                rows, info = result
                krylov.append(rows)
            elif step == 0:
                z, rows, info, tiles = result
                blocks = [tiles]
                krylov.append(z)
            else:
                z, rows, info = result
                krylov.append(z)
        answer, residual = run_final(gather_rows(info, line, plane), krylov)
        return answer, residual.reshape(freq_count)

    return shards


def solution(mesh):
    line, plane = split_nodes(mesh.shape["node"])
    freqs = mesh.shape["freq"]
    fine = Mesh(mesh.devices.reshape(line, plane, freqs), ("line", "place", "freq"))
    node = ("line", "place")
    in_specs = (
        P(None, "freq", node),
        P(node, "freq", None, None),
        P(node, "freq", None, None),
        P(node, None),
        P(node),
        P("freq"),
    )
    out_specs = (P(None, "freq", node), P("freq"))
    shards = make_shards(line, plane, freqs)
    return jax.shard_map(shards, mesh=fine, in_specs=in_specs, out_specs=out_specs, check_vma=False)
```

```python
import functools
import math

import jax
import jax.numpy as jnp
from jax import lax
from jax.experimental import pallas as pl
from jax.experimental.pallas import tpu as pltpu
from jax.sharding import Mesh
from jax.sharding import PartitionSpec as P

ITERS = 3
LANES = 128
GROUP = 4
FULL_GROUP = 8
SHARES = 16
VMEM_LIMIT = 16 * 1024 * 1024


def split_nodes(nodes):
    plane = 4 if nodes % 4 == 0 else 1
    return nodes // plane, plane


def partner_steps(size):
    if size & (size - 1) == 0:
        return [[(i, i ^ d) for i in range(size)] for d in range(1, size)]
    return [[(i, (i + d) % size) for i in range(size)] for d in range(1, size)]


def distance(me, other, size):
    if size & (size - 1) == 0:
        return me ^ other
    return lax.rem(me - other + size, size)


def gather_rows(rows, line, plane, between=()):
    parts = rows.size // rows.shape[-1]
    held = [rows] + [lax.ppermute(rows, "line", perm) for perm in partner_steps(line)]
    whole_line = jnp.stack(held).reshape(line, parts, rows.shape[-1])
    if between:
        whole_line, *between = lax.optimization_barrier((whole_line, *between))
    held = [whole_line] + [lax.ppermute(whole_line, "place", perm) for perm in partner_steps(plane)]
    return (held, *between) if between else held


def gather_tiles(tile, line, plane):
    if (line & (line - 1)) or (plane & (plane - 1)):
        return jnp.concatenate(gather_rows(tile, line, plane))
    tiles = tile[None]
    for axis, size in (("line", line), ("place", plane)):
        d = 1
        while d < size:
            other = lax.ppermute(tiles, axis, [(i, i ^ d) for i in range(size)])
            tiles = jnp.concatenate([tiles, other])
            d *= 2
    return tiles


def near_kernel(g_ref, c_ref, g_out_ref, c_out_ref, sems):
    pieces = sems.shape[1]
    part = g_ref.shape[0] // pieces
    copies = []
    for m, (source, target) in enumerate(((g_ref, g_out_ref), (c_ref, c_out_ref))):
        for i in range(pieces):
            at = pl.ds(i * part, part)
            copies.append(pltpu.make_async_copy(source.at[at], target.at[at], sems.at[m, i]))
            copies[-1].start()
    for copy in copies:
        copy.wait()


def bring_near(g_own, c_own):
    vmem, far = pl.BlockSpec(memory_space=pltpu.VMEM), pl.BlockSpec(memory_space=pl.ANY)
    blocks = jax.ShapeDtypeStruct(g_own.shape, jnp.float32)
    return pl.pallas_call(
        near_kernel,
        in_specs=[far] * 2,
        out_specs=[vmem] * 2,
        out_shape=[blocks] * 2,
        scratch_shapes=[pltpu.SemaphoreType.DMA((2, math.gcd(g_own.shape[0], 8)))],
        compiler_params=pltpu.CompilerParams(vmem_limit_bytes=VMEM_LIMIT),
        cost_estimate=pl.CostEstimate(flops=0, bytes_accessed=16 * g_own.size, transcendentals=0),
        name="near",
    )(g_own, c_own)


def setup_kernel(
    line, plane, freqs, pattern_ref, counts_ref, where_ref, ids_ref, items_ref, places_ref, turn_ref
):
    row_blocks, slots = pattern_ref.shape
    own_slots = slots // freqs
    order = lax.broadcasted_iota(jnp.int32, (8, LANES), 1)
    freq = where_ref[2]
    for table, d in enumerate(list(range(freqs)) + [None]):
        first = 0 if d is None else lax.rem(freq + (freqs - d), freqs) * own_slots
        group = FULL_GROUP if d is None else GROUP
        layer = jnp.zeros((8, LANES), jnp.int32) + first
        block = jnp.full((8, LANES), row_blocks, jnp.int32)
        home = jnp.zeros((8, LANES), jnp.int32)
        used = jnp.int32(0)
        for b in range(row_blocks):
            here = counts_ref[b] if d is None else jnp.clip(counts_ref[b] - first, 0, own_slots)
            inside = order - used
            hit = (inside >= 0) & (inside < here)
            layer = jnp.where(hit, first + inside, layer)
            block = jnp.where(hit, b, block)
            home = jnp.where(hit, b, home)
            used = used + here
        away = freq - lax.div(layer, own_slots)
        away = jnp.where(away < 0, away + freqs, away)
        stored = (away * row_blocks + home) * own_slots + lax.rem(layer, own_slots)
        groups = jnp.zeros((8, LANES), jnp.int32) + lax.div(used + (group - 1), group)
        for i, values in enumerate((layer, block, stored, groups)):
            items_ref[4 * table + i : 4 * table + i + 1, :] = values[:1]

    pattern = pattern_ref[...]
    owner = lax.div(pattern, row_blocks)
    far = distance(where_ref[0], lax.div(owner, plane), line)
    place = distance(where_ref[1], lax.rem(owner, plane), plane) * line + far
    place = place * row_blocks + lax.rem(pattern, row_blocks)
    b_at = lax.broadcasted_iota(jnp.int32, pattern.shape, 0)
    k_at = lax.broadcasted_iota(jnp.int32, pattern.shape, 1)
    count = jnp.zeros(pattern.shape, jnp.int32)
    for b in range(row_blocks):
        count = jnp.where(b_at == b, counts_ref[b], count)
    places_ref[...] = jnp.where(k_at < count, place, line * plane * row_blocks)

    half = turn_ref.shape[0] // 2
    row_at = lax.broadcasted_iota(jnp.int32, turn_ref.shape, 0)
    ids = jnp.zeros(turn_ref.shape, jnp.int32)
    for f in range(half):
        ids = jnp.where(lax.rem(row_at, half) == f, ids_ref[f], ids)
    angular = 0.2 * jnp.exp(ids.astype(jnp.float32) * (math.log(8.0) / 1000.0))
    turn_ref[...] = jnp.where(row_at < half, -angular, angular)


def run_setup(pattern, counts, where, freq_ids, line, plane, freqs):
    smem, vmem = pl.BlockSpec(memory_space=pltpu.SMEM), pl.BlockSpec(memory_space=pltpu.VMEM)
    return pl.pallas_call(
        functools.partial(setup_kernel, line, plane, freqs),
        in_specs=[vmem, smem, smem, smem],
        out_specs=[vmem] * 3,
        out_shape=[
            jax.ShapeDtypeStruct((4 * (freqs + 1), LANES), jnp.int32),
            jax.ShapeDtypeStruct(pattern.shape, jnp.int32),
            jax.ShapeDtypeStruct((2 * freq_ids.shape[0], LANES), jnp.float32),
        ],
        name="setup",
    )(pattern, counts, where, freq_ids)


def lane_sum(x):
    return jnp.sum(x, axis=1, keepdims=True)


def with_other_part(column):
    wide = jnp.broadcast_to(column, (column.shape[0], LANES))
    return wide + pltpu.roll(wide, column.shape[0] // 2, 0)


def put_lane(tile, lane, column):
    at = lax.broadcasted_iota(jnp.int32, tile.shape, 1) == lane
    return jnp.where(at, column, tile)


def split(x):
    high = x.astype(jnp.bfloat16)
    return high, (x - high.astype(jnp.float32)).astype(jnp.bfloat16)


def step_kernel(step, plane, line, freqs, items_ref, places_ref, turn_ref, info_in_ref, *refs):
    lines, refs = refs[:plane], refs[plane:]
    prev, refs = refs[:step], refs[step:]
    row_blocks, slots = places_ref.shape
    nodes = plane * line
    if step == 0:
        g_refs, c_refs = refs[:freqs], refs[freqs : 2 * freqs]
        z_ref, local_ref, info_ref, split_ref, layer_ref, mask_ref, acc_ref = refs[2 * freqs :]
    elif step < ITERS - 1:
        split_ref, z_ref, local_ref, info_ref, layer_ref, mask_ref, acc_ref = refs
    else:
        split_ref, own_ref, info_ref, layer_ref, mask_ref, acc_ref, z_ref, local_ref = refs
    parts, rows = local_ref.shape
    size = rows // row_blocks

    lane = lax.broadcasted_iota(jnp.int32, (size, LANES), 1)
    for b in range(row_blocks):
        mask_ref[b] = jnp.where((lane // parts) % row_blocks == b, 1.0, 0.0).astype(jnp.bfloat16)
    mask_ref[row_blocks] = jnp.zeros((size, LANES), jnp.bfloat16)
    acc_ref[...] = jnp.zeros_like(acc_ref)
    z_ref[nodes * row_blocks] = jnp.zeros((parts, size), jnp.float32)

    def blocks(body, carry):
        for q in range(plane):

            def chunk(i, carry, q=q):
                x = lines[q][i]
                for b in range(row_blocks):
                    carry = body(b, x[:, b * size : (b + 1) * size], (q * line + i) * row_blocks + b, carry)
                return carry

            if line <= 4:
                for i in range(line):
                    carry = chunk(i, carry)
            else:
                carry = lax.fori_loop(0, line, chunk, carry)
        return carry

    def add(sums, b, term):
        return sums[:b] + (sums[b] + term,) + sums[b + 1 :]

    def whole(sums):
        while len(sums) > 1:
            sums = tuple(x + y for x, y in zip(sums[::2], sums[1::2])) + sums[len(sums) // 2 * 2 :]
        return with_other_part(lane_sum(sums[0]))

    none = (jnp.zeros((parts, size), jnp.float32),) * row_blocks
    info = info_in_ref[...]
    if step == 0:
        height = jnp.sqrt(whole(blocks(lambda b, x, at, sums: add(sums, b, x * x), none)))
        info = put_lane(info, 0, height)

        def normal(b, x, at, carry):
            z_ref[at] = x / height
            return carry
    else:
        first = 1 if step == 1 else 3

        def dot(b, x, at, sums):
            return tuple(add(s, b, p[at] * x) for s, p in zip(sums, prev))

        coeffs = [whole(s) for s in blocks(dot, (none,) * step)]
        for i, coeff in enumerate(coeffs):
            info = put_lane(info, first + i, coeff)

        def subtract(b, x, at, sums):
            for coeff, p in zip(coeffs, prev):
                x = x - coeff * p[at]
            z_ref[at] = x
            return add(sums, b, x * x)

        height = jnp.sqrt(whole(blocks(subtract, none)))
        info = put_lane(info, first + step, height)

        def normal(b, x, at, carry):
            z_ref[at] = z_ref[at] / height
            return carry

    blocks(normal, 0)

    for k in range(slots):
        chosen = jnp.concatenate([z_ref[places_ref[b, k]] for b in range(row_blocks)], axis=0)
        high = chosen.astype(jnp.bfloat16).astype(jnp.float32)
        layer_ref[k] = jnp.transpose(jnp.concatenate([high, chosen - high], axis=0)).astype(jnp.bfloat16)

    def product(table, t, left):
        right = layer_ref[items_ref[table, t]] * mask_ref[items_ref[table + 1, t]]
        right = jnp.concatenate([right, right], axis=0)
        return jnp.dot(left, right, preferred_element_type=jnp.float32)

    if step == 0:
        for d in range(freqs):

            @pl.loop(0, items_ref[4 * d + 3, 0])
            def _(group):
                total = acc_ref[...]
                for u in range(GROUP):
                    t = group * GROUP + u
                    stored = items_ref[4 * d + 2, t]
                    here = stored - d * g_refs[d].shape[0]
                    high, low = split(jnp.concatenate([g_refs[d][here], c_refs[d][here]], axis=0))
                    left = jnp.concatenate([high, low], axis=1)
                    split_ref[stored] = left
                    total = total + product(4 * d, t, left)
                acc_ref[...] = total
    else:

        @pl.loop(0, items_ref[4 * freqs + 3, 0])
        def _(group):
            total = acc_ref[...]
            for u in range(FULL_GROUP):
                t = group * FULL_GROUP + u
                total = total + product(4 * freqs, t, split_ref[items_ref[4 * freqs + 2, t]])
            acc_ref[...] = total

    half = row_blocks * parts
    gsum, csum = jnp.transpose(acc_ref[:size]), jnp.transpose(acc_ref[size:])
    gsum, csum = gsum[:half] + gsum[half:], csum[:half] + csum[half:]
    turn = turn_ref[...]
    for b in range(row_blocks):
        at = slice(b * parts, (b + 1) * parts)
        other = pltpu.roll(csum[at], parts // 2, 0)
        local_ref[:, b * size : (b + 1) * size] = gsum[at] + turn * other

    if step == ITERS - 1:
        w = local_ref[...]
        zs = [jnp.concatenate([p[b] for b in range(row_blocks)], axis=1) for p in (*prev, z_ref)]
        for i, z in enumerate(zs):
            own_ref[i] = z
        values = [lane_sum(z * w) for z in zs]
        gram = [[lane_sum(zs[i] * zs[j]) for j in range(i + 1)] for i in range(ITERS)]
        shares = []
        for i, z in enumerate(zs):
            along = lane_sum(z * w) if i else values[0]
            share = jnp.where(gram[i][i] > 0.0, along / gram[i][i], 0.0)
            shares.append(share)
            w = w - share * z
        values += shares + [lane_sum(z * w) for z in zs] + [lane_sum(w * w)]
        values += [gram[i][j] for i in range(ITERS) for j in range(i + 1)]
        for lane_at, value in enumerate(values):
            info = put_lane(info, SHARES + lane_at, value)
    info_ref[...] = info


def run_step(step, lists, turn, info, lines, prev, blocks, freqs):
    plane = len(lines)
    line, parts, rows = lines[0].shape
    row_blocks, slots = lists[1].shape
    size = rows // row_blocks
    vmem = pl.BlockSpec(memory_space=pltpu.VMEM)
    in_specs = [pl.BlockSpec(memory_space=pltpu.SMEM)] * 2 + [vmem] * (2 + plane + step + len(blocks))
    z = (plane * line * row_blocks + 1, parts, size)
    tile = jax.ShapeDtypeStruct((parts, LANES), jnp.float32)
    own = jax.ShapeDtypeStruct((parts, rows), jnp.float32)
    owns = jax.ShapeDtypeStruct((ITERS, parts, rows), jnp.float32)
    out_shape = [owns, tile] if step == ITERS - 1 else [jax.ShapeDtypeStruct(z, jnp.float32), own, tile]
    scratch_shapes = [
        pltpu.VMEM((slots, size, LANES), jnp.bfloat16),
        pltpu.VMEM((row_blocks + 1, size, LANES), jnp.bfloat16),
        pltpu.VMEM((2 * size, LANES), jnp.float32),
    ]
    if step == 0:
        out_shape.append(jax.ShapeDtypeStruct((row_blocks * slots, 2 * size, 2 * size), jnp.bfloat16))
    if step == ITERS - 1:
        scratch_shapes += [pltpu.VMEM(z, jnp.float32), pltpu.VMEM((parts, rows), jnp.float32)]
    return pl.pallas_call(
        functools.partial(step_kernel, step, plane, line, freqs),
        in_specs=in_specs,
        out_specs=[vmem] * len(out_shape),
        out_shape=out_shape,
        scratch_shapes=scratch_shapes,
        compiler_params=pltpu.CompilerParams(vmem_limit_bytes=VMEM_LIMIT),
        name=f"step_{step}",
    )(*lists, turn, info, *lines, *prev, *blocks)


def final_kernel(tiles_ref, own_ref, out_ref, residual_ref):
    devices, parts, _ = tiles_ref.shape
    fit = LANES // parts
    tiles = [tiles_ref[i] for i in range(devices)]
    sets = [jnp.transpose(jnp.concatenate(tiles[at : at + fit], axis=0)) for at in range(0, devices, fit)]
    sums = tiles
    while len(sums) > 1:
        sums = [x + y for x, y in zip(sums[::2], sums[1::2])] + sums[len(sums) // 2 * 2 :]
    total = sums[0] + pltpu.roll(sums[0], parts // 2, 0)
    lane = lax.broadcasted_iota(jnp.int32, total.shape, 1)
    info = jnp.transpose(jnp.concatenate([jnp.where(lane < SHARES, tiles[0], total)] * fit, axis=0))

    def all_devices(shares):
        total = sum(shares[1:], shares[0])
        step = parts // 2
        while step < LANES:
            total = total + pltpu.roll(total, step, 1)
            step *= 2
        return total

    def row(table, at):
        return jnp.broadcast_to(table[at : at + 1], (8, LANES))

    zero = jnp.zeros((8, LANES), jnp.float32)
    norm, h00, h10, h01, h11, h21 = [row(info, i) for i in range(6)]
    last = [row(info, SHARES + i) for i in range(ITERS)]
    shares = []
    for s in sets:
        off = [last[i] - row(s, SHARES + ITERS + i) for i in range(ITERS)]
        square = row(s, SHARES + 3 * ITERS)
        at = SHARES + 3 * ITERS + 1
        for i in range(ITERS):
            square = square - 2.0 * off[i] * row(s, SHARES + 2 * ITERS + i)
            for j in range(i + 1):
                square = square + (1.0 if i == j else 2.0) * off[i] * off[j] * row(s, at)
                at += 1
        shares.append(square)
    height = jnp.sqrt(jnp.maximum(all_devices(shares), 0.0))
    hessen = [[h00, h01, last[0]], [h10, h11, last[1]], [zero, h21, last[2]], [zero, zero, height]]
    normal = [[sum(h[m] * h[n] for h in hessen) for n in range(ITERS)] for m in range(ITERS)]
    low = [[None] * ITERS for _ in range(ITERS)]
    middle = []
    for m in range(ITERS):
        for n in range(m):
            rest = normal[m][n] - sum((low[m][k] * low[n][k] for k in range(n)), zero)
            low[m][n] = rest / low[n][n]
        low[m][m] = jnp.sqrt(normal[m][m] - sum((low[m][k] * low[m][k] for k in range(m)), zero))
        rest = norm * hessen[0][m] - sum((low[m][k] * middle[k] for k in range(m)), zero)
        middle.append(rest / low[m][m])
    coef_y = [None] * ITERS
    for m in reversed(range(ITERS)):
        rest = middle[m] - sum((low[k][m] * coef_y[k] for k in range(m + 1, ITERS)), zero)
        coef_y[m] = rest / low[m][m]
    total = zero
    for i, h in enumerate(hessen):
        misfit = (norm if i == 0 else zero) - sum(h[m] * coef_y[m] for m in range(ITERS))
        total = total + misfit * misfit
    residual_ref[...] = jnp.sqrt(total)[:1, : parts // 2]
    columns = jnp.transpose(
        jnp.concatenate([y for y in coef_y] + [jnp.zeros((LANES - 8 * ITERS, LANES), jnp.float32)], axis=0)
    )[:parts]
    rows = own_ref.shape[-1]
    x = sum(jnp.broadcast_to(columns[:, 8 * m : 8 * m + 1], (parts, rows)) * own_ref[m] for m in range(ITERS))
    out_ref[0] = x[: parts // 2]
    out_ref[1] = x[parts // 2 :]


def run_final(tiles, own):
    _, parts, rows = own.shape
    vmem = pl.BlockSpec(memory_space=pltpu.VMEM)
    return pl.pallas_call(
        final_kernel,
        in_specs=[vmem] * 2,
        out_specs=[vmem] * 2,
        out_shape=[
            jax.ShapeDtypeStruct((2, parts // 2, rows), jnp.float32),
            jax.ShapeDtypeStruct((1, parts // 2), jnp.float32),
        ],
        name="final",
    )(tiles, own)


def make_shards(line, plane, freqs):
    def shards(excitation, g_blocks, c_blocks, pattern, counts, freq_ids):
        row_blocks, own_slots, size, _ = g_blocks.shape
        freq_count = excitation.shape[1]
        parts = 2 * freq_count
        where = jnp.stack([lax.axis_index(name) for name in ("line", "place", "freq")]).astype(jnp.int32)
        stored = (row_blocks * own_slots, size, size)
        g_own, c_own = g_blocks.reshape(stored), c_blocks.reshape(stored)
        *lists, turn = run_setup(pattern, counts, where, freq_ids, line, plane, freqs)
        first_lines, g_near, c_near = gather_rows(excitation, line, plane, bring_near(g_own, c_own))
        g_parts, c_parts = [g_near], [c_near]
        for d in range(1, freqs):
            perm = [(i, (i + d) % freqs) for i in range(freqs)]
            g_parts.append(lax.ppermute(g_own, "freq", perm))
            c_parts.append(lax.ppermute(c_own, "freq", perm))
        info = jnp.zeros((parts, LANES), jnp.float32)
        krylov = []
        blocks = g_parts + c_parts
        for step in range(ITERS):
            lines = gather_rows(rows, line, plane) if step else first_lines
            result = run_step(step, lists, turn, info, lines, krylov, blocks, freqs)
            if step == ITERS - 1:
                own, info = result
            elif step == 0:
                z, rows, info, tiles = result
                blocks = [tiles]
                krylov.append(z)
            else:
                z, rows, info = result
                krylov.append(z)
        answer, residual = run_final(gather_tiles(info, line, plane), own)
        return answer, residual.reshape(freq_count)

    return shards


def solution(mesh):
    line, plane = split_nodes(mesh.shape["node"])
    freqs = mesh.shape["freq"]
    fine = Mesh(mesh.devices.reshape(line, plane, freqs), ("line", "place", "freq"))
    node = ("line", "place")
    in_specs = (
        P(None, "freq", node),
        P(node, "freq", None, None),
        P(node, "freq", None, None),
        P(node, None),
        P(node),
        P("freq"),
    )
    out_specs = (P(None, "freq", node), P("freq"))
    shards = make_shards(line, plane, freqs)
    return jax.shard_map(shards, mesh=fine, in_specs=in_specs, out_specs=out_specs, check_vma=False)
```

```python
import functools
import math

import jax
import jax.numpy as jnp
from jax import lax
from jax.experimental import pallas as pl
from jax.experimental.pallas import tpu as pltpu
from jax.sharding import Mesh
from jax.sharding import PartitionSpec as P

ITERS = 3
LANES = 128
GROUP = 4
FULL_GROUP = 8
SHARES = 16
VMEM_LIMIT = 16 * 1024 * 1024


def split_nodes(nodes):
    plane = 4 if nodes % 4 == 0 else 1
    return nodes // plane, plane


def partner_steps(size):
    if size & (size - 1) == 0:
        return [[(i, i ^ d) for i in range(size)] for d in range(1, size)]
    return [[(i, (i + d) % size) for i in range(size)] for d in range(1, size)]


def distance(me, other, size):
    if size & (size - 1) == 0:
        return me ^ other
    return lax.rem(me - other + size, size)


def gather_rows(rows, line, plane):
    parts = rows.size // rows.shape[-1]
    held = [rows] + [lax.ppermute(rows, "line", perm) for perm in partner_steps(line)]
    whole_line = jnp.stack(held).reshape(line, parts, rows.shape[-1])
    return [whole_line] + [lax.ppermute(whole_line, "place", perm) for perm in partner_steps(plane)]


def setup_kernel(
    line, plane, freqs, pattern_ref, scalars_ref, g_ref, c_ref,
    items_ref, places_ref, turn_ref, g_out_ref, c_out_ref, sems,
):
    row_blocks, slots = pattern_ref.shape
    own_slots = slots // freqs
    pieces = sems.shape[1]
    part = g_ref.shape[0] // pieces
    copies = []
    for m, (source, target) in enumerate(((g_ref, g_out_ref), (c_ref, c_out_ref))):
        for i in range(pieces):
            at = pl.ds(i * part, part)
            copies.append(pltpu.make_async_copy(source.at[at], target.at[at], sems.at[m, i]))
            copies[-1].start()

    order = lax.broadcasted_iota(jnp.int32, (8, LANES), 1)
    freq = scalars_ref[2]
    for table, d in enumerate(list(range(freqs)) + [None]):
        first = 0 if d is None else lax.rem(freq + (freqs - d), freqs) * own_slots
        group = FULL_GROUP if d is None else GROUP
        layer = jnp.zeros((8, LANES), jnp.int32) + first
        block = jnp.full((8, LANES), row_blocks, jnp.int32)
        home = jnp.zeros((8, LANES), jnp.int32)
        used = jnp.int32(0)
        for b in range(row_blocks):
            here = scalars_ref[3 + b] if d is None else jnp.clip(scalars_ref[3 + b] - first, 0, own_slots)
            inside = order - used
            hit = (inside >= 0) & (inside < here)
            layer = jnp.where(hit, first + inside, layer)
            block = jnp.where(hit, b, block)
            home = jnp.where(hit, b, home)
            used = used + here
        away = freq - lax.div(layer, own_slots)
        away = jnp.where(away < 0, away + freqs, away)
        stored = (away * row_blocks + home) * own_slots + lax.rem(layer, own_slots)
        groups = jnp.zeros((8, LANES), jnp.int32) + lax.div(used + (group - 1), group)
        for i, values in enumerate((layer, block, stored, groups)):
            items_ref[4 * table + i : 4 * table + i + 1, :] = values[:1]

    pattern = pattern_ref[...]
    owner = lax.div(pattern, row_blocks)
    far = distance(scalars_ref[0], lax.div(owner, plane), line)
    place = distance(scalars_ref[1], lax.rem(owner, plane), plane) * line + far
    place = place * row_blocks + lax.rem(pattern, row_blocks)
    b_at = lax.broadcasted_iota(jnp.int32, pattern.shape, 0)
    k_at = lax.broadcasted_iota(jnp.int32, pattern.shape, 1)
    count = jnp.zeros(pattern.shape, jnp.int32)
    for b in range(row_blocks):
        count = jnp.where(b_at == b, scalars_ref[3 + b], count)
    places_ref[...] = jnp.where(k_at < count, place, line * plane * row_blocks)

    half = turn_ref.shape[0] // 2
    row_at = lax.broadcasted_iota(jnp.int32, turn_ref.shape, 0)
    ids = jnp.zeros(turn_ref.shape, jnp.int32)
    for f in range(half):
        ids = jnp.where(lax.rem(row_at, half) == f, scalars_ref[3 + row_blocks + f], ids)
    angular = 0.2 * jnp.exp(ids.astype(jnp.float32) * (math.log(8.0) / 1000.0))
    turn_ref[...] = jnp.where(row_at < half, -angular, angular)
    for copy in copies:
        copy.wait()


def run_setup(pattern, scalars, freq_count, g_own, c_own, line, plane, freqs):
    smem, vmem = pl.BlockSpec(memory_space=pltpu.SMEM), pl.BlockSpec(memory_space=pltpu.VMEM)
    far = pl.BlockSpec(memory_space=pl.ANY)
    blocks = jax.ShapeDtypeStruct(g_own.shape, jnp.float32)
    pieces = math.gcd(g_own.shape[0], 8)
    return pl.pallas_call(
        functools.partial(setup_kernel, line, plane, freqs),
        in_specs=[vmem, smem, far, far],
        out_specs=[vmem] * 5,
        out_shape=[
            jax.ShapeDtypeStruct((4 * (freqs + 1), LANES), jnp.int32),
            jax.ShapeDtypeStruct(pattern.shape, jnp.int32),
            jax.ShapeDtypeStruct((2 * freq_count, LANES), jnp.float32),
            blocks,
            blocks,
        ],
        scratch_shapes=[pltpu.SemaphoreType.DMA((2, pieces))],
        compiler_params=pltpu.CompilerParams(vmem_limit_bytes=VMEM_LIMIT),
        cost_estimate=pl.CostEstimate(flops=0, bytes_accessed=16 * g_own.size, transcendentals=0),
        name="setup",
    )(pattern, scalars, g_own, c_own)


def lane_sum(x):
    return jnp.sum(x, axis=1, keepdims=True)


def with_other_part(column):
    wide = jnp.broadcast_to(column, (column.shape[0], LANES))
    return wide + pltpu.roll(wide, column.shape[0] // 2, 0)


def put_lane(tile, lane, column):
    at = lax.broadcasted_iota(jnp.int32, tile.shape, 1) == lane
    return jnp.where(at, column, tile)


def split(x):
    high = x.astype(jnp.bfloat16)
    return high, (x - high.astype(jnp.float32)).astype(jnp.bfloat16)


def step_kernel(step, plane, line, freqs, items_ref, places_ref, turn_ref, info_in_ref, *refs):
    lines, refs = refs[:plane], refs[plane:]
    prev, refs = refs[:step], refs[step:]
    row_blocks, slots = places_ref.shape
    nodes = plane * line
    if step == 0:
        g_refs, c_refs = refs[:freqs], refs[freqs : 2 * freqs]
        z_ref, local_ref, info_ref, split_ref, layer_ref, mask_ref, acc_ref = refs[2 * freqs :]
    elif step < ITERS - 1:
        split_ref, z_ref, local_ref, info_ref, layer_ref, mask_ref, acc_ref = refs
    else:
        split_ref, own_ref, info_ref, layer_ref, mask_ref, acc_ref, z_ref, local_ref = refs
    parts, rows = local_ref.shape
    size = rows // row_blocks

    lane = lax.broadcasted_iota(jnp.int32, (size, LANES), 1)
    for b in range(row_blocks):
        mask_ref[b] = jnp.where((lane // parts) % row_blocks == b, 1.0, 0.0).astype(jnp.bfloat16)
    mask_ref[row_blocks] = jnp.zeros((size, LANES), jnp.bfloat16)
    acc_ref[...] = jnp.zeros_like(acc_ref)
    z_ref[nodes * row_blocks] = jnp.zeros((parts, size), jnp.float32)

    def blocks(body, carry):
        for q in range(plane):

            def chunk(i, carry, q=q):
                x = lines[q][i]
                for b in range(row_blocks):
                    carry = body(b, x[:, b * size : (b + 1) * size], (q * line + i) * row_blocks + b, carry)
                return carry

            if line <= 4:
                for i in range(line):
                    carry = chunk(i, carry)
            else:
                carry = lax.fori_loop(0, line, chunk, carry)
        return carry

    def add(sums, b, term):
        return sums[:b] + (sums[b] + term,) + sums[b + 1 :]

    def whole(sums):
        while len(sums) > 1:
            sums = tuple(x + y for x, y in zip(sums[::2], sums[1::2])) + sums[len(sums) // 2 * 2 :]
        return with_other_part(lane_sum(sums[0]))

    none = (jnp.zeros((parts, size), jnp.float32),) * row_blocks
    info = info_in_ref[...]
    if step == 0:
        height = jnp.sqrt(whole(blocks(lambda b, x, at, sums: add(sums, b, x * x), none)))
        info = put_lane(info, 0, height)

        def normal(b, x, at, carry):
            z_ref[at] = x / height
            return carry
    else:
        first = 1 if step == 1 else 3

        def dot(b, x, at, sums):
            return tuple(add(s, b, p[at] * x) for s, p in zip(sums, prev))

        coeffs = [whole(s) for s in blocks(dot, (none,) * step)]
        for i, coeff in enumerate(coeffs):
            info = put_lane(info, first + i, coeff)

        def subtract(b, x, at, sums):
            for coeff, p in zip(coeffs, prev):
                x = x - coeff * p[at]
            z_ref[at] = x
            return add(sums, b, x * x)

        height = jnp.sqrt(whole(blocks(subtract, none)))
        info = put_lane(info, first + step, height)

        def normal(b, x, at, carry):
            z_ref[at] = z_ref[at] / height
            return carry

    blocks(normal, 0)

    for k in range(slots):
        chosen = jnp.concatenate([z_ref[places_ref[b, k]] for b in range(row_blocks)], axis=0)
        high = chosen.astype(jnp.bfloat16).astype(jnp.float32)
        layer_ref[k] = jnp.transpose(jnp.concatenate([high, chosen - high], axis=0)).astype(jnp.bfloat16)

    def product(table, t, left):
        right = layer_ref[items_ref[table, t]] * mask_ref[items_ref[table + 1, t]]
        right = jnp.concatenate([right, right], axis=0)
        return jnp.dot(left, right, preferred_element_type=jnp.float32)

    if step == 0:
        for d in range(freqs):

            @pl.loop(0, items_ref[4 * d + 3, 0])
            def _(group):
                total = acc_ref[...]
                for u in range(GROUP):
                    t = group * GROUP + u
                    stored = items_ref[4 * d + 2, t]
                    here = stored - d * g_refs[d].shape[0]
                    high, low = split(jnp.concatenate([g_refs[d][here], c_refs[d][here]], axis=0))
                    left = jnp.concatenate([high, low], axis=1)
                    split_ref[stored] = left
                    total = total + product(4 * d, t, left)
                acc_ref[...] = total
    else:

        @pl.loop(0, items_ref[4 * freqs + 3, 0])
        def _(group):
            total = acc_ref[...]
            for u in range(FULL_GROUP):
                t = group * FULL_GROUP + u
                total = total + product(4 * freqs, t, split_ref[items_ref[4 * freqs + 2, t]])
            acc_ref[...] = total

    half = row_blocks * parts
    gsum, csum = jnp.transpose(acc_ref[:size]), jnp.transpose(acc_ref[size:])
    gsum, csum = gsum[:half] + gsum[half:], csum[:half] + csum[half:]
    turn = turn_ref[...]
    for b in range(row_blocks):
        at = slice(b * parts, (b + 1) * parts)
        other = pltpu.roll(csum[at], parts // 2, 0)
        local_ref[:, b * size : (b + 1) * size] = gsum[at] + turn * other

    if step == ITERS - 1:
        w = local_ref[...]
        zs = [jnp.concatenate([p[b] for b in range(row_blocks)], axis=1) for p in (*prev, z_ref)]
        for i, z in enumerate(zs):
            own_ref[i] = z
        values = [lane_sum(z * w) for z in zs]
        gram = [[lane_sum(zs[i] * zs[j]) for j in range(i + 1)] for i in range(ITERS)]
        shares = []
        for i, z in enumerate(zs):
            along = lane_sum(z * w) if i else values[0]
            share = jnp.where(gram[i][i] > 0.0, along / gram[i][i], 0.0)
            shares.append(share)
            w = w - share * z
        values += shares + [lane_sum(z * w) for z in zs] + [lane_sum(w * w)]
        values += [gram[i][j] for i in range(ITERS) for j in range(i + 1)]
        for lane_at, value in enumerate(values):
            info = put_lane(info, SHARES + lane_at, value)
    info_ref[...] = info


def run_step(step, lists, turn, info, lines, prev, blocks, freqs):
    plane = len(lines)
    line, parts, rows = lines[0].shape
    row_blocks, slots = lists[1].shape
    size = rows // row_blocks
    vmem = pl.BlockSpec(memory_space=pltpu.VMEM)
    in_specs = [pl.BlockSpec(memory_space=pltpu.SMEM)] * 2 + [vmem] * (2 + plane + step + len(blocks))
    z = (plane * line * row_blocks + 1, parts, size)
    tile = jax.ShapeDtypeStruct((parts, LANES), jnp.float32)
    own = jax.ShapeDtypeStruct((parts, rows), jnp.float32)
    owns = jax.ShapeDtypeStruct((ITERS, parts, rows), jnp.float32)
    out_shape = [owns, tile] if step == ITERS - 1 else [jax.ShapeDtypeStruct(z, jnp.float32), own, tile]
    scratch_shapes = [
        pltpu.VMEM((slots, size, LANES), jnp.bfloat16),
        pltpu.VMEM((row_blocks + 1, size, LANES), jnp.bfloat16),
        pltpu.VMEM((2 * size, LANES), jnp.float32),
    ]
    if step == 0:
        out_shape.append(jax.ShapeDtypeStruct((row_blocks * slots, 2 * size, 2 * size), jnp.bfloat16))
    if step == ITERS - 1:
        scratch_shapes += [pltpu.VMEM(z, jnp.float32), pltpu.VMEM((parts, rows), jnp.float32)]
    return pl.pallas_call(
        functools.partial(step_kernel, step, plane, line, freqs),
        in_specs=in_specs,
        out_specs=[vmem] * len(out_shape),
        out_shape=out_shape,
        scratch_shapes=scratch_shapes,
        compiler_params=pltpu.CompilerParams(vmem_limit_bytes=VMEM_LIMIT),
        name=f"step_{step}",
    )(*lists, turn, info, *lines, *prev, *blocks)


def final_kernel(tiles_ref, own_ref, out_ref, residual_ref):
    devices, parts, _ = tiles_ref.shape
    fit = LANES // parts
    tiles = [tiles_ref[i] for i in range(devices)]
    sets = [jnp.transpose(jnp.concatenate(tiles[at : at + fit], axis=0)) for at in range(0, devices, fit)]
    sums = tiles
    while len(sums) > 1:
        sums = [x + y for x, y in zip(sums[::2], sums[1::2])] + sums[len(sums) // 2 * 2 :]
    total = sums[0] + pltpu.roll(sums[0], parts // 2, 0)
    lane = lax.broadcasted_iota(jnp.int32, total.shape, 1)
    info = jnp.transpose(jnp.concatenate([jnp.where(lane < SHARES, tiles[0], total)] * fit, axis=0))

    def all_devices(shares):
        total = sum(shares[1:], shares[0])
        step = parts // 2
        while step < LANES:
            total = total + pltpu.roll(total, step, 1)
            step *= 2
        return total

    def row(table, at):
        return jnp.broadcast_to(table[at : at + 1], (8, LANES))

    zero = jnp.zeros((8, LANES), jnp.float32)
    norm, h00, h10, h01, h11, h21 = [row(info, i) for i in range(6)]
    last = [row(info, SHARES + i) for i in range(ITERS)]
    shares = []
    for s in sets:
        off = [last[i] - row(s, SHARES + ITERS + i) for i in range(ITERS)]
        square = row(s, SHARES + 3 * ITERS)
        at = SHARES + 3 * ITERS + 1
        for i in range(ITERS):
            square = square - 2.0 * off[i] * row(s, SHARES + 2 * ITERS + i)
            for j in range(i + 1):
                square = square + (1.0 if i == j else 2.0) * off[i] * off[j] * row(s, at)
                at += 1
        shares.append(square)
    height = jnp.sqrt(jnp.maximum(all_devices(shares), 0.0))
    hessen = [[h00, h01, last[0]], [h10, h11, last[1]], [zero, h21, last[2]], [zero, zero, height]]
    normal = [[sum(h[m] * h[n] for h in hessen) for n in range(ITERS)] for m in range(ITERS)]
    low = [[None] * ITERS for _ in range(ITERS)]
    middle = []
    for m in range(ITERS):
        for n in range(m):
            rest = normal[m][n] - sum((low[m][k] * low[n][k] for k in range(n)), zero)
            low[m][n] = rest / low[n][n]
        low[m][m] = jnp.sqrt(normal[m][m] - sum((low[m][k] * low[m][k] for k in range(m)), zero))
        rest = norm * hessen[0][m] - sum((low[m][k] * middle[k] for k in range(m)), zero)
        middle.append(rest / low[m][m])
    coef_y = [None] * ITERS
    for m in reversed(range(ITERS)):
        rest = middle[m] - sum((low[k][m] * coef_y[k] for k in range(m + 1, ITERS)), zero)
        coef_y[m] = rest / low[m][m]
    total = zero
    for i, h in enumerate(hessen):
        misfit = (norm if i == 0 else zero) - sum(h[m] * coef_y[m] for m in range(ITERS))
        total = total + misfit * misfit
    residual_ref[...] = jnp.sqrt(total)[:1, : parts // 2]
    columns = jnp.transpose(
        jnp.concatenate([y for y in coef_y] + [jnp.zeros((LANES - 8 * ITERS, LANES), jnp.float32)], axis=0)
    )[:parts]
    rows = own_ref.shape[-1]
    x = sum(jnp.broadcast_to(columns[:, 8 * m : 8 * m + 1], (parts, rows)) * own_ref[m] for m in range(ITERS))
    out_ref[0] = x[: parts // 2]
    out_ref[1] = x[parts // 2 :]


def run_final(tiles, own):
    _, parts, rows = own.shape
    vmem = pl.BlockSpec(memory_space=pltpu.VMEM)
    return pl.pallas_call(
        final_kernel,
        in_specs=[vmem] * 2,
        out_specs=[vmem] * 2,
        out_shape=[
            jax.ShapeDtypeStruct((2, parts // 2, rows), jnp.float32),
            jax.ShapeDtypeStruct((1, parts // 2), jnp.float32),
        ],
        name="final",
    )(tiles, own)


def make_shards(line, plane, freqs):
    def shards(excitation, g_blocks, c_blocks, pattern, counts, freq_ids):
        row_blocks, own_slots, size, _ = g_blocks.shape
        freq_count = excitation.shape[1]
        parts = 2 * freq_count
        where = jnp.stack([lax.axis_index(name) for name in ("line", "place", "freq")])
        scalars = jnp.concatenate([where, counts, freq_ids]).astype(jnp.int32)
        stored = (row_blocks * own_slots, size, size)
        g_own, c_own = g_blocks.reshape(stored), c_blocks.reshape(stored)
        *lists, turn, g_near, c_near = run_setup(
            pattern, scalars, freq_count, g_own, c_own, line, plane, freqs
        )
        g_parts, c_parts = [g_near], [c_near]
        for d in range(1, freqs):
            perm = [(i, (i + d) % freqs) for i in range(freqs)]
            g_parts.append(lax.ppermute(g_own, "freq", perm))
            c_parts.append(lax.ppermute(c_own, "freq", perm))
        info = jnp.zeros((parts, LANES), jnp.float32)
        krylov = []
        rows = excitation
        blocks = g_parts + c_parts
        for step in range(ITERS):
            lines = gather_rows(rows, line, plane)
            result = run_step(step, lists, turn, info, lines, krylov, blocks, freqs)
            if step == ITERS - 1:
                own, info = result
            elif step == 0:
                z, rows, info, tiles = result
                blocks = [tiles]
                krylov.append(z)
            else:
                z, rows, info = result
                krylov.append(z)
        answer, residual = run_final(jnp.concatenate(gather_rows(info, line, plane)), own)
        return answer, residual.reshape(freq_count)

    return shards


def solution(mesh):
    line, plane = split_nodes(mesh.shape["node"])
    freqs = mesh.shape["freq"]
    fine = Mesh(mesh.devices.reshape(line, plane, freqs), ("line", "place", "freq"))
    node = ("line", "place")
    in_specs = (
        P(None, "freq", node),
        P(node, "freq", None, None),
        P(node, "freq", None, None),
        P(node, None),
        P(node),
        P("freq"),
    )
    out_specs = (P(None, "freq", node), P("freq"))
    shards = make_shards(line, plane, freqs)
    return jax.shard_map(shards, mesh=fine, in_specs=in_specs, out_specs=out_specs, check_vma=False)
```

```python
import functools
import math

import jax
import jax.numpy as jnp
from jax import lax
from jax.experimental import pallas as pl
from jax.experimental.pallas import tpu as pltpu
from jax.sharding import Mesh
from jax.sharding import PartitionSpec as P

ITERS = 3
LANES = 128
GROUP = 4
FULL_GROUP = 8
SHARES = 16
VMEM_LIMIT = 16 * 1024 * 1024


def split_nodes(nodes):
    plane = 4 if nodes % 4 == 0 else 1
    return nodes // plane, plane


def partner_steps(size):
    if size & (size - 1) == 0:
        return [[(i, i ^ d) for i in range(size)] for d in range(1, size)]
    return [[(i, (i + d) % size) for i in range(size)] for d in range(1, size)]


def distance(me, other, size):
    if size & (size - 1) == 0:
        return me ^ other
    return lax.rem(me - other + size, size)


def gather_rows(rows, line, plane):
    parts = rows.size // rows.shape[-1]
    held = [rows] + [lax.ppermute(rows, "line", perm) for perm in partner_steps(line)]
    whole_line = jnp.stack(held).reshape(line, parts, rows.shape[-1])
    return [whole_line] + [lax.ppermute(whole_line, "place", perm) for perm in partner_steps(plane)]


def setup_kernel(
    line, plane, freqs, scalars_ref, g_ref, c_ref,
    items_ref, places_ref, turn_ref, g_out_ref, c_out_ref, sems,
):
    row_blocks, slots = places_ref.shape
    pattern_at = 3 + row_blocks + turn_ref.shape[0] // 2
    own_slots = slots // freqs
    pieces = sems.shape[1]
    part = g_ref.shape[0] // pieces
    copies = []
    for m, (source, target) in enumerate(((g_ref, g_out_ref), (c_ref, c_out_ref))):
        for i in range(pieces):
            at = pl.ds(i * part, part)
            copies.append(pltpu.make_async_copy(source.at[at], target.at[at], sems.at[m, i]))
            copies[-1].start()

    order = lax.broadcasted_iota(jnp.int32, (8, LANES), 1)
    freq = scalars_ref[2]
    for table, d in enumerate(list(range(freqs)) + [None]):
        first = 0 if d is None else lax.rem(freq + (freqs - d), freqs) * own_slots
        group = FULL_GROUP if d is None else GROUP
        layer = jnp.zeros((8, LANES), jnp.int32) + first
        block = jnp.full((8, LANES), row_blocks, jnp.int32)
        home = jnp.zeros((8, LANES), jnp.int32)
        used = jnp.int32(0)
        for b in range(row_blocks):
            here = scalars_ref[3 + b] if d is None else jnp.clip(scalars_ref[3 + b] - first, 0, own_slots)
            inside = order - used
            hit = (inside >= 0) & (inside < here)
            layer = jnp.where(hit, first + inside, layer)
            block = jnp.where(hit, b, block)
            home = jnp.where(hit, b, home)
            used = used + here
        away = freq - lax.div(layer, own_slots)
        away = jnp.where(away < 0, away + freqs, away)
        stored = (away * row_blocks + home) * own_slots + lax.rem(layer, own_slots)
        groups = jnp.zeros((8, LANES), jnp.int32) + lax.div(used + (group - 1), group)
        for i, values in enumerate((layer, block, stored, groups)):
            items_ref[4 * table + i : 4 * table + i + 1, :] = values[:1]

    b_at = lax.broadcasted_iota(jnp.int32, places_ref.shape, 0)
    k_at = lax.broadcasted_iota(jnp.int32, places_ref.shape, 1)
    pattern = jnp.zeros(places_ref.shape, jnp.int32)
    for i in range(row_blocks * slots):
        pattern = jnp.where(b_at * slots + k_at == i, scalars_ref[pattern_at + i], pattern)
    owner = lax.div(pattern, row_blocks)
    far = distance(scalars_ref[0], lax.div(owner, plane), line)
    place = distance(scalars_ref[1], lax.rem(owner, plane), plane) * line + far
    place = place * row_blocks + lax.rem(pattern, row_blocks)
    count = jnp.zeros(pattern.shape, jnp.int32)
    for b in range(row_blocks):
        count = jnp.where(b_at == b, scalars_ref[3 + b], count)
    places_ref[...] = jnp.where(k_at < count, place, line * plane * row_blocks)

    half = turn_ref.shape[0] // 2
    row_at = lax.broadcasted_iota(jnp.int32, turn_ref.shape, 0)
    ids = jnp.zeros(turn_ref.shape, jnp.int32)
    for f in range(half):
        ids = jnp.where(lax.rem(row_at, half) == f, scalars_ref[3 + row_blocks + f], ids)
    angular = 0.2 * jnp.exp(ids.astype(jnp.float32) * (math.log(8.0) / 1000.0))
    turn_ref[...] = jnp.where(row_at < half, -angular, angular)
    for copy in copies:
        copy.wait()


def run_setup(scalars, shape, freq_count, g_own, c_own, line, plane, freqs):
    smem, vmem = pl.BlockSpec(memory_space=pltpu.SMEM), pl.BlockSpec(memory_space=pltpu.VMEM)
    far = pl.BlockSpec(memory_space=pl.ANY)
    blocks = jax.ShapeDtypeStruct(g_own.shape, jnp.float32)
    pieces = math.gcd(g_own.shape[0], 8)
    return pl.pallas_call(
        functools.partial(setup_kernel, line, plane, freqs),
        in_specs=[smem, far, far],
        out_specs=[vmem] * 5,
        out_shape=[
            jax.ShapeDtypeStruct((4 * (freqs + 1), LANES), jnp.int32),
            jax.ShapeDtypeStruct(shape, jnp.int32),
            jax.ShapeDtypeStruct((2 * freq_count, LANES), jnp.float32),
            blocks,
            blocks,
        ],
        scratch_shapes=[pltpu.SemaphoreType.DMA((2, pieces))],
        compiler_params=pltpu.CompilerParams(vmem_limit_bytes=VMEM_LIMIT),
        cost_estimate=pl.CostEstimate(flops=0, bytes_accessed=16 * g_own.size, transcendentals=0),
        name="setup",
    )(scalars, g_own, c_own)


def lane_sum(x):
    return jnp.sum(x, axis=1, keepdims=True)


def with_other_part(column):
    wide = jnp.broadcast_to(column, (column.shape[0], LANES))
    return wide + pltpu.roll(wide, column.shape[0] // 2, 0)


def put_lane(tile, lane, column):
    at = lax.broadcasted_iota(jnp.int32, tile.shape, 1) == lane
    return jnp.where(at, column, tile)


def split(x):
    high = x.astype(jnp.bfloat16)
    return high, (x - high.astype(jnp.float32)).astype(jnp.bfloat16)


def step_kernel(step, plane, line, freqs, items_ref, places_ref, turn_ref, info_in_ref, *refs):
    lines, refs = refs[:plane], refs[plane:]
    prev, refs = refs[:step], refs[step:]
    row_blocks, slots = places_ref.shape
    nodes = plane * line
    if step == 0:
        g_refs, c_refs = refs[:freqs], refs[freqs : 2 * freqs]
        z_ref, local_ref, info_ref, split_ref, layer_ref, mask_ref, acc_ref = refs[2 * freqs :]
    elif step < ITERS - 1:
        split_ref, z_ref, local_ref, info_ref, layer_ref, mask_ref, acc_ref = refs
    else:
        split_ref, own_ref, info_ref, layer_ref, mask_ref, acc_ref, z_ref, local_ref = refs
    parts, rows = local_ref.shape
    size = rows // row_blocks

    lane = lax.broadcasted_iota(jnp.int32, (size, LANES), 1)
    for b in range(row_blocks):
        mask_ref[b] = jnp.where((lane // parts) % row_blocks == b, 1.0, 0.0).astype(jnp.bfloat16)
    mask_ref[row_blocks] = jnp.zeros((size, LANES), jnp.bfloat16)
    acc_ref[...] = jnp.zeros_like(acc_ref)
    z_ref[nodes * row_blocks] = jnp.zeros((parts, size), jnp.float32)

    def blocks(body, carry):
        for q in range(plane):

            def chunk(i, carry, q=q):
                x = lines[q][i]
                for b in range(row_blocks):
                    carry = body(b, x[:, b * size : (b + 1) * size], (q * line + i) * row_blocks + b, carry)
                return carry

            if line <= 4:
                for i in range(line):
                    carry = chunk(i, carry)
            else:
                carry = lax.fori_loop(0, line, chunk, carry)
        return carry

    def add(sums, b, term):
        return sums[:b] + (sums[b] + term,) + sums[b + 1 :]

    def whole(sums):
        while len(sums) > 1:
            sums = tuple(x + y for x, y in zip(sums[::2], sums[1::2])) + sums[len(sums) // 2 * 2 :]
        return with_other_part(lane_sum(sums[0]))

    none = (jnp.zeros((parts, size), jnp.float32),) * row_blocks
    info = info_in_ref[...]
    if step == 0:
        height = jnp.sqrt(whole(blocks(lambda b, x, at, sums: add(sums, b, x * x), none)))
        info = put_lane(info, 0, height)

        def normal(b, x, at, carry):
            z_ref[at] = x / height
            return carry
    else:
        first = 1 if step == 1 else 3

        def dot(b, x, at, sums):
            return tuple(add(s, b, p[at] * x) for s, p in zip(sums, prev))

        coeffs = [whole(s) for s in blocks(dot, (none,) * step)]
        for i, coeff in enumerate(coeffs):
            info = put_lane(info, first + i, coeff)

        def subtract(b, x, at, sums):
            for coeff, p in zip(coeffs, prev):
                x = x - coeff * p[at]
            z_ref[at] = x
            return add(sums, b, x * x)

        height = jnp.sqrt(whole(blocks(subtract, none)))
        info = put_lane(info, first + step, height)

        def normal(b, x, at, carry):
            z_ref[at] = z_ref[at] / height
            return carry

    blocks(normal, 0)

    for k in range(slots):
        chosen = jnp.concatenate([z_ref[places_ref[b, k]] for b in range(row_blocks)], axis=0)
        high = chosen.astype(jnp.bfloat16).astype(jnp.float32)
        layer_ref[k] = jnp.transpose(jnp.concatenate([high, chosen - high], axis=0)).astype(jnp.bfloat16)

    def add_products(totals, table, t, lefts):
        right = layer_ref[items_ref[table, t]] * mask_ref[items_ref[table + 1, t]]
        right = jnp.concatenate([right, right], axis=0)
        return [
            total + jnp.dot(left, right, preferred_element_type=jnp.float32)
            for total, left in zip(totals, lefts)
        ]

    if step == 0:
        for d in range(freqs):

            @pl.loop(0, items_ref[4 * d + 3, 0])
            def _(group):
                totals = [acc_ref[0], acc_ref[1]]
                for u in range(GROUP):
                    t = group * GROUP + u
                    stored = items_ref[4 * d + 2, t]
                    here = stored - d * g_refs[d].shape[0]
                    lefts = []
                    for m, block_refs in enumerate((g_refs, c_refs)):
                        left = jnp.concatenate(split(block_refs[d][here]), axis=1)
                        split_ref[stored, m] = left
                        lefts.append(left)
                    totals = add_products(totals, 4 * d, t, lefts)
                acc_ref[0], acc_ref[1] = totals
    else:

        @pl.loop(0, items_ref[4 * freqs + 3, 0])
        def _(group):
            totals = [acc_ref[0], acc_ref[1]]
            for u in range(FULL_GROUP):
                t = group * FULL_GROUP + u
                stored = items_ref[4 * freqs + 2, t]
                totals = add_products(totals, 4 * freqs, t, [split_ref[stored, m] for m in range(2)])
            acc_ref[0], acc_ref[1] = totals

    half = row_blocks * parts
    gsum, csum = jnp.transpose(acc_ref[0]), jnp.transpose(acc_ref[1])
    gsum, csum = gsum[:half] + gsum[half:], csum[:half] + csum[half:]
    turn = turn_ref[...]
    for b in range(row_blocks):
        at = slice(b * parts, (b + 1) * parts)
        other = pltpu.roll(csum[at], parts // 2, 0)
        local_ref[:, b * size : (b + 1) * size] = gsum[at] + turn * other

    if step == ITERS - 1:
        w = local_ref[...]
        zs = [jnp.concatenate([p[b] for b in range(row_blocks)], axis=1) for p in (*prev, z_ref)]
        for i, z in enumerate(zs):
            own_ref[i] = z
        values = [lane_sum(z * w) for z in zs]
        gram = [[lane_sum(zs[i] * zs[j]) for j in range(i + 1)] for i in range(ITERS)]
        shares = []
        for i, z in enumerate(zs):
            along = lane_sum(z * w) if i else values[0]
            share = jnp.where(gram[i][i] > 0.0, along / gram[i][i], 0.0)
            shares.append(share)
            w = w - share * z
        values += shares + [lane_sum(z * w) for z in zs] + [lane_sum(w * w)]
        values += [gram[i][j] for i in range(ITERS) for j in range(i + 1)]
        for lane_at, value in enumerate(values):
            info = put_lane(info, SHARES + lane_at, value)
    info_ref[...] = info


def run_step(step, lists, turn, info, lines, prev, blocks, freqs):
    plane = len(lines)
    line, parts, rows = lines[0].shape
    row_blocks, slots = lists[1].shape
    size = rows // row_blocks
    vmem = pl.BlockSpec(memory_space=pltpu.VMEM)
    in_specs = [pl.BlockSpec(memory_space=pltpu.SMEM)] * 2 + [vmem] * (2 + plane + step + len(blocks))
    z = (plane * line * row_blocks + 1, parts, size)
    tile = jax.ShapeDtypeStruct((parts, LANES), jnp.float32)
    own = jax.ShapeDtypeStruct((parts, rows), jnp.float32)
    owns = jax.ShapeDtypeStruct((ITERS, parts, rows), jnp.float32)
    out_shape = [owns, tile] if step == ITERS - 1 else [jax.ShapeDtypeStruct(z, jnp.float32), own, tile]
    scratch_shapes = [
        pltpu.VMEM((slots, size, LANES), jnp.bfloat16),
        pltpu.VMEM((row_blocks + 1, size, LANES), jnp.bfloat16),
        pltpu.VMEM((2, size, LANES), jnp.float32),
    ]
    if step == 0:
        out_shape.append(jax.ShapeDtypeStruct((row_blocks * slots, 2, size, 2 * size), jnp.bfloat16))
    if step == ITERS - 1:
        scratch_shapes += [pltpu.VMEM(z, jnp.float32), pltpu.VMEM((parts, rows), jnp.float32)]
    return pl.pallas_call(
        functools.partial(step_kernel, step, plane, line, freqs),
        in_specs=in_specs,
        out_specs=[vmem] * len(out_shape),
        out_shape=out_shape,
        scratch_shapes=scratch_shapes,
        compiler_params=pltpu.CompilerParams(vmem_limit_bytes=VMEM_LIMIT),
        name=f"step_{step}",
    )(*lists, turn, info, *lines, *prev, *blocks)


def final_kernel(tiles_ref, own_ref, out_ref, residual_ref):
    devices, parts, _ = tiles_ref.shape
    fit = LANES // parts
    tiles = [tiles_ref[i] for i in range(devices)]
    sets = [jnp.transpose(jnp.concatenate(tiles[at : at + fit], axis=0)) for at in range(0, devices, fit)]
    sums = tiles
    while len(sums) > 1:
        sums = [x + y for x, y in zip(sums[::2], sums[1::2])] + sums[len(sums) // 2 * 2 :]
    total = sums[0] + pltpu.roll(sums[0], parts // 2, 0)
    lane = lax.broadcasted_iota(jnp.int32, total.shape, 1)
    info = jnp.transpose(jnp.concatenate([jnp.where(lane < SHARES, tiles[0], total)] * fit, axis=0))

    def all_devices(shares):
        total = sum(shares[1:], shares[0])
        step = parts // 2
        while step < LANES:
            total = total + pltpu.roll(total, step, 1)
            step *= 2
        return total

    def row(table, at):
        return jnp.broadcast_to(table[at : at + 1], (8, LANES))

    zero = jnp.zeros((8, LANES), jnp.float32)
    norm, h00, h10, h01, h11, h21 = [row(info, i) for i in range(6)]
    last = [row(info, SHARES + i) for i in range(ITERS)]
    shares = []
    for s in sets:
        off = [last[i] - row(s, SHARES + ITERS + i) for i in range(ITERS)]
        square = row(s, SHARES + 3 * ITERS)
        at = SHARES + 3 * ITERS + 1
        for i in range(ITERS):
            square = square - 2.0 * off[i] * row(s, SHARES + 2 * ITERS + i)
            for j in range(i + 1):
                square = square + (1.0 if i == j else 2.0) * off[i] * off[j] * row(s, at)
                at += 1
        shares.append(square)
    height = jnp.sqrt(jnp.maximum(all_devices(shares), 0.0))
    hessen = [[h00, h01, last[0]], [h10, h11, last[1]], [zero, h21, last[2]], [zero, zero, height]]
    normal = [[sum(h[m] * h[n] for h in hessen) for n in range(ITERS)] for m in range(ITERS)]
    low = [[None] * ITERS for _ in range(ITERS)]
    middle = []
    for m in range(ITERS):
        for n in range(m):
            rest = normal[m][n] - sum((low[m][k] * low[n][k] for k in range(n)), zero)
            low[m][n] = rest / low[n][n]
        low[m][m] = jnp.sqrt(normal[m][m] - sum((low[m][k] * low[m][k] for k in range(m)), zero))
        rest = norm * hessen[0][m] - sum((low[m][k] * middle[k] for k in range(m)), zero)
        middle.append(rest / low[m][m])
    coef_y = [None] * ITERS
    for m in reversed(range(ITERS)):
        rest = middle[m] - sum((low[k][m] * coef_y[k] for k in range(m + 1, ITERS)), zero)
        coef_y[m] = rest / low[m][m]
    total = zero
    for i, h in enumerate(hessen):
        misfit = (norm if i == 0 else zero) - sum(h[m] * coef_y[m] for m in range(ITERS))
        total = total + misfit * misfit
    residual_ref[...] = jnp.sqrt(total)[:1, : parts // 2]
    columns = jnp.transpose(
        jnp.concatenate([y for y in coef_y] + [jnp.zeros((LANES - 8 * ITERS, LANES), jnp.float32)], axis=0)
    )[:parts]
    rows = own_ref.shape[-1]
    x = sum(jnp.broadcast_to(columns[:, 8 * m : 8 * m + 1], (parts, rows)) * own_ref[m] for m in range(ITERS))
    out_ref[0] = x[: parts // 2]
    out_ref[1] = x[parts // 2 :]


def run_final(tiles, own):
    _, parts, rows = own.shape
    vmem = pl.BlockSpec(memory_space=pltpu.VMEM)
    return pl.pallas_call(
        final_kernel,
        in_specs=[vmem] * 2,
        out_specs=[vmem] * 2,
        out_shape=[
            jax.ShapeDtypeStruct((2, parts // 2, rows), jnp.float32),
            jax.ShapeDtypeStruct((1, parts // 2), jnp.float32),
        ],
        name="final",
    )(tiles, own)


def make_shards(line, plane, freqs):
    def shards(excitation, g_blocks, c_blocks, pattern, counts, freq_ids):
        row_blocks, own_slots, size, _ = g_blocks.shape
        freq_count = excitation.shape[1]
        parts = 2 * freq_count
        where = jnp.stack([lax.axis_index(name) for name in ("line", "place", "freq")])
        scalars = jnp.concatenate([where, counts, freq_ids, pattern.reshape(-1)]).astype(jnp.int32)
        stored = (row_blocks * own_slots, size, size)
        g_own, c_own = g_blocks.reshape(stored), c_blocks.reshape(stored)
        *lists, turn, g_near, c_near = run_setup(
            scalars, pattern.shape, freq_count, g_own, c_own, line, plane, freqs
        )
        g_parts, c_parts = [g_near], [c_near]
        for d in range(1, freqs):
            perm = [(i, (i + d) % freqs) for i in range(freqs)]
            g_parts.append(lax.ppermute(g_own, "freq", perm))
            c_parts.append(lax.ppermute(c_own, "freq", perm))
        info = jnp.zeros((parts, LANES), jnp.float32)
        krylov = []
        rows = excitation
        blocks = g_parts + c_parts
        for step in range(ITERS):
            lines = gather_rows(rows, line, plane)
            result = run_step(step, lists, turn, info, lines, krylov, blocks, freqs)
            if step == ITERS - 1:
                own, info = result
            elif step == 0:
                z, rows, info, tiles = result
                blocks = [tiles]
                krylov.append(z)
            else:
                z, rows, info = result
                krylov.append(z)
        answer, residual = run_final(jnp.concatenate(gather_rows(info, line, plane)), own)
        return answer, residual.reshape(freq_count)

    return shards


def solution(mesh):
    line, plane = split_nodes(mesh.shape["node"])
    freqs = mesh.shape["freq"]
    fine = Mesh(mesh.devices.reshape(line, plane, freqs), ("line", "place", "freq"))
    node = ("line", "place")
    in_specs = (
        P(None, "freq", node),
        P(node, "freq", None, None),
        P(node, "freq", None, None),
        P(node, None),
        P(node),
        P("freq"),
    )
    out_specs = (P(None, "freq", node), P("freq"))
    shards = make_shards(line, plane, freqs)
    return jax.shard_map(shards, mesh=fine, in_specs=in_specs, out_specs=out_specs, check_vma=False)
```

```python
import functools
import math

import jax
import jax.numpy as jnp
from jax import lax
from jax.experimental import pallas as pl
from jax.experimental.pallas import tpu as pltpu
from jax.sharding import Mesh
from jax.sharding import PartitionSpec as P

ITERS = 3
LANES = 128
GROUP = 4
FULL_GROUP = 8
SHARES = 16
VMEM_LIMIT = 16 * 1024 * 1024


def split_nodes(nodes):
    plane = 4 if nodes % 4 == 0 else 1
    return nodes // plane, plane


def partner_steps(size):
    if size & (size - 1) == 0:
        return [[(i, i ^ d) for i in range(size)] for d in range(1, size)]
    return [[(i, (i + d) % size) for i in range(size)] for d in range(1, size)]


def distance(me, other, size):
    if size & (size - 1) == 0:
        return me ^ other
    return lax.rem(me - other + size, size)


def gather_rows(rows, line, plane):
    parts = rows.size // rows.shape[-1]
    held = [rows] + [lax.ppermute(rows, "line", perm) for perm in partner_steps(line)]
    whole_line = jnp.stack(held).reshape(line, parts, rows.shape[-1])
    return [whole_line] + [lax.ppermute(whole_line, "place", perm) for perm in partner_steps(plane)]


def setup_kernel(
    line, plane, freqs, scalars_ref, g_ref, c_ref,
    items_ref, places_ref, turn_ref, g_out_ref, c_out_ref, sems,
):
    row_blocks, slots = places_ref.shape
    pattern_at = 3 + row_blocks + turn_ref.shape[0] // 2
    own_slots = slots // freqs
    pieces = sems.shape[1]
    part = g_ref.shape[0] // pieces
    copies = []
    for m, (source, target) in enumerate(((g_ref, g_out_ref), (c_ref, c_out_ref))):
        for i in range(pieces):
            at = pl.ds(i * part, part)
            copies.append(pltpu.make_async_copy(source.at[at], target.at[at], sems.at[m, i]))
            copies[-1].start()

    order = lax.broadcasted_iota(jnp.int32, (8, LANES), 1)
    freq = scalars_ref[2]
    for table, d in enumerate(list(range(freqs)) + [None]):
        first = 0 if d is None else lax.rem(freq + (freqs - d), freqs) * own_slots
        group = FULL_GROUP if d is None else GROUP
        layer = jnp.zeros((8, LANES), jnp.int32) + first
        block = jnp.full((8, LANES), row_blocks, jnp.int32)
        home = jnp.zeros((8, LANES), jnp.int32)
        used = jnp.int32(0)
        for b in range(row_blocks):
            here = scalars_ref[3 + b] if d is None else jnp.clip(scalars_ref[3 + b] - first, 0, own_slots)
            inside = order - used
            hit = (inside >= 0) & (inside < here)
            layer = jnp.where(hit, first + inside, layer)
            block = jnp.where(hit, b, block)
            home = jnp.where(hit, b, home)
            used = used + here
        away = freq - lax.div(layer, own_slots)
        away = jnp.where(away < 0, away + freqs, away)
        stored = (away * row_blocks + home) * own_slots + lax.rem(layer, own_slots)
        groups = jnp.zeros((8, LANES), jnp.int32) + lax.div(used + (group - 1), group)
        for i, values in enumerate((layer, block, stored, groups)):
            items_ref[4 * table + i : 4 * table + i + 1, :] = values[:1]

    b_at = lax.broadcasted_iota(jnp.int32, places_ref.shape, 0)
    k_at = lax.broadcasted_iota(jnp.int32, places_ref.shape, 1)
    pattern = jnp.zeros(places_ref.shape, jnp.int32)
    for i in range(row_blocks * slots):
        pattern = jnp.where(b_at * slots + k_at == i, scalars_ref[pattern_at + i], pattern)
    owner = lax.div(pattern, row_blocks)
    far = distance(scalars_ref[0], lax.div(owner, plane), line)
    place = distance(scalars_ref[1], lax.rem(owner, plane), plane) * line + far
    place = place * row_blocks + lax.rem(pattern, row_blocks)
    count = jnp.zeros(pattern.shape, jnp.int32)
    for b in range(row_blocks):
        count = jnp.where(b_at == b, scalars_ref[3 + b], count)
    places_ref[...] = jnp.where(k_at < count, place, line * plane * row_blocks)

    half = turn_ref.shape[0] // 2
    row_at = lax.broadcasted_iota(jnp.int32, turn_ref.shape, 0)
    ids = jnp.zeros(turn_ref.shape, jnp.int32)
    for f in range(half):
        ids = jnp.where(lax.rem(row_at, half) == f, scalars_ref[3 + row_blocks + f], ids)
    angular = 0.2 * jnp.exp(ids.astype(jnp.float32) * (math.log(8.0) / 1000.0))
    turn_ref[...] = jnp.where(row_at < half, -angular, angular)
    for copy in copies:
        copy.wait()


def run_setup(scalars, shape, freq_count, g_own, c_own, line, plane, freqs):
    smem, vmem = pl.BlockSpec(memory_space=pltpu.SMEM), pl.BlockSpec(memory_space=pltpu.VMEM)
    far = pl.BlockSpec(memory_space=pl.ANY)
    blocks = jax.ShapeDtypeStruct(g_own.shape, jnp.float32)
    pieces = math.gcd(g_own.shape[0], 8)
    return pl.pallas_call(
        functools.partial(setup_kernel, line, plane, freqs),
        in_specs=[smem, far, far],
        out_specs=[vmem] * 5,
        out_shape=[
            jax.ShapeDtypeStruct((4 * (freqs + 1), LANES), jnp.int32),
            jax.ShapeDtypeStruct(shape, jnp.int32),
            jax.ShapeDtypeStruct((2 * freq_count, LANES), jnp.float32),
            blocks,
            blocks,
        ],
        scratch_shapes=[pltpu.SemaphoreType.DMA((2, pieces))],
        compiler_params=pltpu.CompilerParams(vmem_limit_bytes=VMEM_LIMIT),
        cost_estimate=pl.CostEstimate(flops=0, bytes_accessed=16 * g_own.size, transcendentals=0),
        name="setup",
    )(scalars, g_own, c_own)


def lane_sum(x):
    return jnp.sum(x, axis=1, keepdims=True)


def with_other_part(column):
    wide = jnp.broadcast_to(column, (column.shape[0], LANES))
    return wide + pltpu.roll(wide, column.shape[0] // 2, 0)


def put_lane(tile, lane, column):
    at = lax.broadcasted_iota(jnp.int32, tile.shape, 1) == lane
    return jnp.where(at, column, tile)


def split(x):
    high = x.astype(jnp.bfloat16)
    return high, (x - high.astype(jnp.float32)).astype(jnp.bfloat16)


def step_kernel(step, plane, line, freqs, items_ref, places_ref, turn_ref, info_in_ref, *refs):
    lines, refs = refs[:plane], refs[plane:]
    prev, refs = refs[:step], refs[step:]
    row_blocks, slots = places_ref.shape
    nodes = plane * line
    if step == 0:
        g_refs, c_refs = refs[:freqs], refs[freqs : 2 * freqs]
        z_ref, local_ref, info_ref, split_ref, layer_ref, mask_ref, acc_ref = refs[2 * freqs :]
    elif step < ITERS - 1:
        split_ref, z_ref, local_ref, info_ref, layer_ref, mask_ref, acc_ref = refs
    else:
        split_ref, own_ref, info_ref, layer_ref, mask_ref, acc_ref, z_ref, local_ref = refs
    parts, rows = local_ref.shape
    size = rows // row_blocks

    lane = lax.broadcasted_iota(jnp.int32, (size, LANES), 1)
    for b in range(row_blocks):
        mask_ref[b] = jnp.where((lane // parts) % row_blocks == b, 1.0, 0.0).astype(jnp.bfloat16)
    mask_ref[row_blocks] = jnp.zeros((size, LANES), jnp.bfloat16)
    acc_ref[...] = jnp.zeros_like(acc_ref)
    z_ref[nodes * row_blocks] = jnp.zeros((parts, size), jnp.float32)

    def blocks(body, carry):
        for q in range(plane):

            def chunk(i, carry, q=q):
                x = lines[q][i]
                for b in range(row_blocks):
                    carry = body(b, x[:, b * size : (b + 1) * size], (q * line + i) * row_blocks + b, carry)
                return carry

            if line <= 4:
                for i in range(line):
                    carry = chunk(i, carry)
            else:
                carry = lax.fori_loop(0, line, chunk, carry)
        return carry

    def add(sums, b, term):
        return sums[:b] + (sums[b] + term,) + sums[b + 1 :]

    def whole(sums):
        while len(sums) > 1:
            sums = tuple(x + y for x, y in zip(sums[::2], sums[1::2])) + sums[len(sums) // 2 * 2 :]
        return with_other_part(lane_sum(sums[0]))

    none = (jnp.zeros((parts, size), jnp.float32),) * row_blocks
    info = info_in_ref[...]
    if step == 0:
        height = jnp.sqrt(whole(blocks(lambda b, x, at, sums: add(sums, b, x * x), none)))
        info = put_lane(info, 0, height)

        def normal(b, x, at, carry):
            z_ref[at] = x / height
            return carry
    else:
        first = 1 if step == 1 else 3

        def dot(b, x, at, sums):
            return tuple(add(s, b, p[at] * x) for s, p in zip(sums, prev))

        coeffs = [whole(s) for s in blocks(dot, (none,) * step)]
        for i, coeff in enumerate(coeffs):
            info = put_lane(info, first + i, coeff)

        def subtract(b, x, at, sums):
            for coeff, p in zip(coeffs, prev):
                x = x - coeff * p[at]
            z_ref[at] = x
            return add(sums, b, x * x)

        height = jnp.sqrt(whole(blocks(subtract, none)))
        info = put_lane(info, first + step, height)

        def normal(b, x, at, carry):
            z_ref[at] = z_ref[at] / height
            return carry

    blocks(normal, 0)

    for k in range(slots):
        chosen = jnp.concatenate([z_ref[places_ref[b, k]] for b in range(row_blocks)], axis=0)
        high = chosen.astype(jnp.bfloat16).astype(jnp.float32)
        layer_ref[k] = jnp.transpose(jnp.concatenate([high, chosen - high], axis=0)).astype(jnp.bfloat16)

    def vectors(table, t):
        right = layer_ref[items_ref[table, t]] * mask_ref[items_ref[table + 1, t]]
        return jnp.concatenate([right, right], axis=0)

    def add_group(lefts, rights):
        left, right = jnp.concatenate(lefts, axis=1), jnp.concatenate(rights, axis=0)
        acc_ref[...] += jnp.dot(left, right, preferred_element_type=jnp.float32)

    if step == 0:
        for d in range(freqs):

            @pl.loop(0, items_ref[4 * d + 3, 0])
            def _(group):
                lefts, rights = [], []
                for u in range(GROUP):
                    t = group * GROUP + u
                    stored = items_ref[4 * d + 2, t]
                    here = stored - d * g_refs[d].shape[0]
                    parts_of = split(jnp.concatenate([g_refs[d][here], c_refs[d][here]], axis=0))
                    left = jnp.concatenate(parts_of, axis=1)
                    split_ref[stored] = left
                    lefts.append(left)
                    rights.append(vectors(4 * d, t))
                add_group(lefts, rights)
    else:

        @pl.loop(0, items_ref[4 * freqs + 3, 0])
        def _(group):
            places = [group * FULL_GROUP + u for u in range(FULL_GROUP)]
            lefts = [split_ref[items_ref[4 * freqs + 2, t]] for t in places]
            add_group(lefts, [vectors(4 * freqs, t) for t in places])

    half = row_blocks * parts
    gsum, csum = jnp.transpose(acc_ref[:size]), jnp.transpose(acc_ref[size:])
    gsum, csum = gsum[:half] + gsum[half:], csum[:half] + csum[half:]
    turn = turn_ref[...]
    for b in range(row_blocks):
        at = slice(b * parts, (b + 1) * parts)
        other = pltpu.roll(csum[at], parts // 2, 0)
        local_ref[:, b * size : (b + 1) * size] = gsum[at] + turn * other

    if step == ITERS - 1:
        w = local_ref[...]
        zs = [jnp.concatenate([p[b] for b in range(row_blocks)], axis=1) for p in (*prev, z_ref)]
        for i, z in enumerate(zs):
            own_ref[i] = z
        values = [lane_sum(z * w) for z in zs]
        gram = [[lane_sum(zs[i] * zs[j]) for j in range(i + 1)] for i in range(ITERS)]
        shares = []
        for i, z in enumerate(zs):
            along = lane_sum(z * w) if i else values[0]
            share = jnp.where(gram[i][i] > 0.0, along / gram[i][i], 0.0)
            shares.append(share)
            w = w - share * z
        values += shares + [lane_sum(z * w) for z in zs] + [lane_sum(w * w)]
        values += [gram[i][j] for i in range(ITERS) for j in range(i + 1)]
        for lane_at, value in enumerate(values):
            info = put_lane(info, SHARES + lane_at, value)
    info_ref[...] = info


def run_step(step, lists, turn, info, lines, prev, blocks, freqs):
    plane = len(lines)
    line, parts, rows = lines[0].shape
    row_blocks, slots = lists[1].shape
    size = rows // row_blocks
    vmem = pl.BlockSpec(memory_space=pltpu.VMEM)
    in_specs = [pl.BlockSpec(memory_space=pltpu.SMEM)] * 2 + [vmem] * (2 + plane + step + len(blocks))
    z = (plane * line * row_blocks + 1, parts, size)
    tile = jax.ShapeDtypeStruct((parts, LANES), jnp.float32)
    own = jax.ShapeDtypeStruct((parts, rows), jnp.float32)
    owns = jax.ShapeDtypeStruct((ITERS, parts, rows), jnp.float32)
    out_shape = [owns, tile] if step == ITERS - 1 else [jax.ShapeDtypeStruct(z, jnp.float32), own, tile]
    scratch_shapes = [
        pltpu.VMEM((slots, size, LANES), jnp.bfloat16),
        pltpu.VMEM((row_blocks + 1, size, LANES), jnp.bfloat16),
        pltpu.VMEM((2 * size, LANES), jnp.float32),
    ]
    if step == 0:
        out_shape.append(jax.ShapeDtypeStruct((row_blocks * slots, 2 * size, 2 * size), jnp.bfloat16))
    if step == ITERS - 1:
        scratch_shapes += [pltpu.VMEM(z, jnp.float32), pltpu.VMEM((parts, rows), jnp.float32)]
    return pl.pallas_call(
        functools.partial(step_kernel, step, plane, line, freqs),
        in_specs=in_specs,
        out_specs=[vmem] * len(out_shape),
        out_shape=out_shape,
        scratch_shapes=scratch_shapes,
        compiler_params=pltpu.CompilerParams(vmem_limit_bytes=VMEM_LIMIT),
        name=f"step_{step}",
    )(*lists, turn, info, *lines, *prev, *blocks)


def final_kernel(tiles_ref, own_ref, out_ref, residual_ref):
    devices, parts, _ = tiles_ref.shape
    fit = LANES // parts
    tiles = [tiles_ref[i] for i in range(devices)]
    sets = [jnp.transpose(jnp.concatenate(tiles[at : at + fit], axis=0)) for at in range(0, devices, fit)]
    sums = tiles
    while len(sums) > 1:
        sums = [x + y for x, y in zip(sums[::2], sums[1::2])] + sums[len(sums) // 2 * 2 :]
    total = sums[0] + pltpu.roll(sums[0], parts // 2, 0)
    lane = lax.broadcasted_iota(jnp.int32, total.shape, 1)
    info = jnp.transpose(jnp.concatenate([jnp.where(lane < SHARES, tiles[0], total)] * fit, axis=0))

    def all_devices(shares):
        total = sum(shares[1:], shares[0])
        step = parts // 2
        while step < LANES:
            total = total + pltpu.roll(total, step, 1)
            step *= 2
        return total

    def row(table, at):
        return jnp.broadcast_to(table[at : at + 1], (8, LANES))

    zero = jnp.zeros((8, LANES), jnp.float32)
    norm, h00, h10, h01, h11, h21 = [row(info, i) for i in range(6)]
    last = [row(info, SHARES + i) for i in range(ITERS)]
    shares = []
    for s in sets:
        off = [last[i] - row(s, SHARES + ITERS + i) for i in range(ITERS)]
        square = row(s, SHARES + 3 * ITERS)
        at = SHARES + 3 * ITERS + 1
        for i in range(ITERS):
            square = square - 2.0 * off[i] * row(s, SHARES + 2 * ITERS + i)
            for j in range(i + 1):
                square = square + (1.0 if i == j else 2.0) * off[i] * off[j] * row(s, at)
                at += 1
        shares.append(square)
    height = jnp.sqrt(jnp.maximum(all_devices(shares), 0.0))
    hessen = [[h00, h01, last[0]], [h10, h11, last[1]], [zero, h21, last[2]], [zero, zero, height]]
    normal = [[sum(h[m] * h[n] for h in hessen) for n in range(ITERS)] for m in range(ITERS)]
    low = [[None] * ITERS for _ in range(ITERS)]
    middle = []
    for m in range(ITERS):
        for n in range(m):
            rest = normal[m][n] - sum((low[m][k] * low[n][k] for k in range(n)), zero)
            low[m][n] = rest / low[n][n]
        low[m][m] = jnp.sqrt(normal[m][m] - sum((low[m][k] * low[m][k] for k in range(m)), zero))
        rest = norm * hessen[0][m] - sum((low[m][k] * middle[k] for k in range(m)), zero)
        middle.append(rest / low[m][m])
    coef_y = [None] * ITERS
    for m in reversed(range(ITERS)):
        rest = middle[m] - sum((low[k][m] * coef_y[k] for k in range(m + 1, ITERS)), zero)
        coef_y[m] = rest / low[m][m]
    total = zero
    for i, h in enumerate(hessen):
        misfit = (norm if i == 0 else zero) - sum(h[m] * coef_y[m] for m in range(ITERS))
        total = total + misfit * misfit
    residual_ref[...] = jnp.sqrt(total)[:1, : parts // 2]
    columns = jnp.transpose(
        jnp.concatenate([y for y in coef_y] + [jnp.zeros((LANES - 8 * ITERS, LANES), jnp.float32)], axis=0)
    )[:parts]
    rows = own_ref.shape[-1]
    x = sum(jnp.broadcast_to(columns[:, 8 * m : 8 * m + 1], (parts, rows)) * own_ref[m] for m in range(ITERS))
    out_ref[0] = x[: parts // 2]
    out_ref[1] = x[parts // 2 :]


def run_final(tiles, own):
    _, parts, rows = own.shape
    vmem = pl.BlockSpec(memory_space=pltpu.VMEM)
    return pl.pallas_call(
        final_kernel,
        in_specs=[vmem] * 2,
        out_specs=[vmem] * 2,
        out_shape=[
            jax.ShapeDtypeStruct((2, parts // 2, rows), jnp.float32),
            jax.ShapeDtypeStruct((1, parts // 2), jnp.float32),
        ],
        name="final",
    )(tiles, own)


def make_shards(line, plane, freqs):
    def shards(excitation, g_blocks, c_blocks, pattern, counts, freq_ids):
        row_blocks, own_slots, size, _ = g_blocks.shape
        freq_count = excitation.shape[1]
        parts = 2 * freq_count
        where = jnp.stack([lax.axis_index(name) for name in ("line", "place", "freq")])
        scalars = jnp.concatenate([where, counts, freq_ids, pattern.reshape(-1)]).astype(jnp.int32)
        stored = (row_blocks * own_slots, size, size)
        g_own, c_own = g_blocks.reshape(stored), c_blocks.reshape(stored)
        *lists, turn, g_near, c_near = run_setup(
            scalars, pattern.shape, freq_count, g_own, c_own, line, plane, freqs
        )
        g_parts, c_parts = [g_near], [c_near]
        for d in range(1, freqs):
            perm = [(i, (i + d) % freqs) for i in range(freqs)]
            g_parts.append(lax.ppermute(g_own, "freq", perm))
            c_parts.append(lax.ppermute(c_own, "freq", perm))
        info = jnp.zeros((parts, LANES), jnp.float32)
        krylov = []
        rows = excitation
        blocks = g_parts + c_parts
        for step in range(ITERS):
            lines = gather_rows(rows, line, plane)
            result = run_step(step, lists, turn, info, lines, krylov, blocks, freqs)
            if step == ITERS - 1:
                own, info = result
            elif step == 0:
                z, rows, info, tiles = result
                blocks = [tiles]
                krylov.append(z)
            else:
                z, rows, info = result
                krylov.append(z)
        answer, residual = run_final(jnp.concatenate(gather_rows(info, line, plane)), own)
        return answer, residual.reshape(freq_count)

    return shards


def solution(mesh):
    line, plane = split_nodes(mesh.shape["node"])
    freqs = mesh.shape["freq"]
    fine = Mesh(mesh.devices.reshape(line, plane, freqs), ("line", "place", "freq"))
    node = ("line", "place")
    in_specs = (
        P(None, "freq", node),
        P(node, "freq", None, None),
        P(node, "freq", None, None),
        P(node, None),
        P(node),
        P("freq"),
    )
    out_specs = (P(None, "freq", node), P("freq"))
    shards = make_shards(line, plane, freqs)
    return jax.shard_map(shards, mesh=fine, in_specs=in_specs, out_specs=out_specs, check_vma=False)
```

```python
import functools
import math

import jax
import jax.numpy as jnp
from jax import lax
from jax.experimental import pallas as pl
from jax.experimental.pallas import tpu as pltpu
from jax.sharding import Mesh
from jax.sharding import PartitionSpec as P

ITERS = 3
LANES = 128
GROUP = 4
FULL_GROUP = 4
SHARES = 16
VMEM_LIMIT = 16 * 1024 * 1024


def split_nodes(nodes):
    plane = 4 if nodes % 4 == 0 else 1
    return nodes // plane, plane


def partner_steps(size):
    if size & (size - 1) == 0:
        return [[(i, i ^ d) for i in range(size)] for d in range(1, size)]
    return [[(i, (i + d) % size) for i in range(size)] for d in range(1, size)]


def distance(me, other, size):
    if size & (size - 1) == 0:
        return me ^ other
    return lax.rem(me - other + size, size)


def gather_rows(rows, line, plane):
    parts = rows.size // rows.shape[-1]
    held = [rows] + [lax.ppermute(rows, "line", perm) for perm in partner_steps(line)]
    whole_line = jnp.stack(held).reshape(line, parts, rows.shape[-1])
    return [whole_line] + [lax.ppermute(whole_line, "place", perm) for perm in partner_steps(plane)]


def setup_kernel(
    line, plane, freqs, scalars_ref, g_ref, c_ref,
    items_ref, places_ref, turn_ref, g_out_ref, c_out_ref, sems,
):
    row_blocks, slots = places_ref.shape
    pattern_at = 3 + row_blocks + turn_ref.shape[0] // 2
    own_slots = slots // freqs
    pieces = sems.shape[1]
    part = g_ref.shape[0] // pieces
    copies = []
    for m, (source, target) in enumerate(((g_ref, g_out_ref), (c_ref, c_out_ref))):
        for i in range(pieces):
            at = pl.ds(i * part, part)
            copies.append(pltpu.make_async_copy(source.at[at], target.at[at], sems.at[m, i]))
            copies[-1].start()

    order = lax.broadcasted_iota(jnp.int32, (8, LANES), 1)
    freq = scalars_ref[2]
    for table, d in enumerate(list(range(freqs)) + [None]):
        first = 0 if d is None else lax.rem(freq + (freqs - d), freqs) * own_slots
        group = FULL_GROUP if d is None else GROUP
        layer = jnp.zeros((8, LANES), jnp.int32) + first
        block = jnp.full((8, LANES), row_blocks, jnp.int32)
        home = jnp.zeros((8, LANES), jnp.int32)
        used = jnp.int32(0)
        for b in range(row_blocks):
            here = scalars_ref[3 + b] if d is None else jnp.clip(scalars_ref[3 + b] - first, 0, own_slots)
            inside = order - used
            hit = (inside >= 0) & (inside < here)
            layer = jnp.where(hit, first + inside, layer)
            block = jnp.where(hit, b, block)
            home = jnp.where(hit, b, home)
            used = used + here
        away = freq - lax.div(layer, own_slots)
        away = jnp.where(away < 0, away + freqs, away)
        stored = (away * row_blocks + home) * own_slots + lax.rem(layer, own_slots)
        groups = jnp.zeros((8, LANES), jnp.int32) + lax.div(used + (group - 1), group)
        for i, values in enumerate((layer, block, stored, groups)):
            items_ref[4 * table + i : 4 * table + i + 1, :] = values[:1]

    b_at = lax.broadcasted_iota(jnp.int32, places_ref.shape, 0)
    k_at = lax.broadcasted_iota(jnp.int32, places_ref.shape, 1)
    pattern = jnp.zeros(places_ref.shape, jnp.int32)
    for i in range(row_blocks * slots):
        pattern = jnp.where(b_at * slots + k_at == i, scalars_ref[pattern_at + i], pattern)
    owner = lax.div(pattern, row_blocks)
    far = distance(scalars_ref[0], lax.div(owner, plane), line)
    place = distance(scalars_ref[1], lax.rem(owner, plane), plane) * line + far
    place = place * row_blocks + lax.rem(pattern, row_blocks)
    count = jnp.zeros(pattern.shape, jnp.int32)
    for b in range(row_blocks):
        count = jnp.where(b_at == b, scalars_ref[3 + b], count)
    places_ref[...] = jnp.where(k_at < count, place, line * plane * row_blocks)

    half = turn_ref.shape[0] // 2
    row_at = lax.broadcasted_iota(jnp.int32, turn_ref.shape, 0)
    ids = jnp.zeros(turn_ref.shape, jnp.int32)
    for f in range(half):
        ids = jnp.where(lax.rem(row_at, half) == f, scalars_ref[3 + row_blocks + f], ids)
    angular = 0.2 * jnp.exp(ids.astype(jnp.float32) * (math.log(8.0) / 1000.0))
    turn_ref[...] = jnp.where(row_at < half, -angular, angular)
    for copy in copies:
        copy.wait()


def run_setup(scalars, shape, freq_count, g_own, c_own, line, plane, freqs):
    smem, vmem = pl.BlockSpec(memory_space=pltpu.SMEM), pl.BlockSpec(memory_space=pltpu.VMEM)
    far = pl.BlockSpec(memory_space=pl.ANY)
    blocks = jax.ShapeDtypeStruct(g_own.shape, jnp.float32)
    pieces = math.gcd(g_own.shape[0], 8)
    return pl.pallas_call(
        functools.partial(setup_kernel, line, plane, freqs),
        in_specs=[smem, far, far],
        out_specs=[vmem] * 5,
        out_shape=[
            jax.ShapeDtypeStruct((4 * (freqs + 1), LANES), jnp.int32),
            jax.ShapeDtypeStruct(shape, jnp.int32),
            jax.ShapeDtypeStruct((2 * freq_count, LANES), jnp.float32),
            blocks,
            blocks,
        ],
        scratch_shapes=[pltpu.SemaphoreType.DMA((2, pieces))],
        compiler_params=pltpu.CompilerParams(vmem_limit_bytes=VMEM_LIMIT),
        cost_estimate=pl.CostEstimate(flops=0, bytes_accessed=16 * g_own.size, transcendentals=0),
        name="setup",
    )(scalars, g_own, c_own)


def lane_sum(x):
    return jnp.sum(x, axis=1, keepdims=True)


def with_other_part(column):
    wide = jnp.broadcast_to(column, (column.shape[0], LANES))
    return wide + pltpu.roll(wide, column.shape[0] // 2, 0)


def put_lane(tile, lane, column):
    at = lax.broadcasted_iota(jnp.int32, tile.shape, 1) == lane
    return jnp.where(at, column, tile)


def split(x):
    high = x.astype(jnp.bfloat16)
    return high, (x - high.astype(jnp.float32)).astype(jnp.bfloat16)


def step_kernel(step, plane, line, freqs, items_ref, places_ref, turn_ref, info_in_ref, *refs):
    lines, refs = refs[:plane], refs[plane:]
    prev, refs = refs[:step], refs[step:]
    row_blocks, slots = places_ref.shape
    nodes = plane * line
    if step == 0:
        g_refs, c_refs = refs[:freqs], list(refs[freqs : 2 * freqs])
        z_ref, local_ref, info_ref, split_ref, layer_ref, mask_ref, acc_ref, kept_ref, sems = refs[2 * freqs :]
        arrivals = []
        for d in range(1, freqs):
            arrivals.append(pltpu.make_async_copy(c_refs[d], kept_ref.at[d - 1], sems.at[d - 1]))
            arrivals[-1].start()
            c_refs[d] = kept_ref.at[d - 1]
    elif step < ITERS - 1:
        split_ref, z_ref, local_ref, info_ref, layer_ref, mask_ref, acc_ref = refs
    else:
        split_ref, own_ref, info_ref, layer_ref, mask_ref, acc_ref, z_ref, local_ref, zs_ref, sem = refs
    parts, rows = local_ref.shape
    size = rows // row_blocks

    lane = lax.broadcasted_iota(jnp.int32, (size, LANES), 1)
    for b in range(row_blocks):
        mask_ref[b] = jnp.where((lane // parts) % row_blocks == b, 1.0, 0.0).astype(jnp.bfloat16)
    mask_ref[row_blocks] = jnp.zeros((size, LANES), jnp.bfloat16)
    acc_ref[...] = jnp.zeros_like(acc_ref)
    z_ref[nodes * row_blocks] = jnp.zeros((parts, size), jnp.float32)

    def blocks(body, carry):
        for q in range(plane):

            def chunk(i, carry, q=q):
                x = lines[q][i]
                for b in range(row_blocks):
                    carry = body(b, x[:, b * size : (b + 1) * size], (q * line + i) * row_blocks + b, carry)
                return carry

            if line <= 4:
                for i in range(line):
                    carry = chunk(i, carry)
            else:
                carry = lax.fori_loop(0, line, chunk, carry)
        return carry

    def add(sums, b, term):
        return sums[:b] + (sums[b] + term,) + sums[b + 1 :]

    def whole(sums):
        while len(sums) > 1:
            sums = tuple(x + y for x, y in zip(sums[::2], sums[1::2])) + sums[len(sums) // 2 * 2 :]
        return with_other_part(lane_sum(sums[0]))

    none = (jnp.zeros((parts, size), jnp.float32),) * row_blocks
    info = info_in_ref[...]
    if step == 0:
        height = jnp.sqrt(whole(blocks(lambda b, x, at, sums: add(sums, b, x * x), none)))
        info = put_lane(info, 0, height)

        def normal(b, x, at, carry):
            z_ref[at] = x / height
            return carry
    else:
        first = 1 if step == 1 else 3

        def dot(b, x, at, sums):
            return tuple(add(s, b, p[at] * x) for s, p in zip(sums, prev))

        coeffs = [whole(s) for s in blocks(dot, (none,) * step)]
        for i, coeff in enumerate(coeffs):
            info = put_lane(info, first + i, coeff)

        def subtract(b, x, at, sums):
            for coeff, p in zip(coeffs, prev):
                x = x - coeff * p[at]
            z_ref[at] = x
            return add(sums, b, x * x)

        height = jnp.sqrt(whole(blocks(subtract, none)))
        info = put_lane(info, first + step, height)

        def normal(b, x, at, carry):
            z_ref[at] = z_ref[at] / height
            return carry

    blocks(normal, 0)
    if step == ITERS - 1:
        for i, p in enumerate((*prev, z_ref)):
            zs_ref[i] = jnp.concatenate([p[b] for b in range(row_blocks)], axis=1)
        leave = pltpu.make_async_copy(zs_ref, own_ref, sem)
        leave.start()

    for k in range(slots):
        chosen = jnp.concatenate([z_ref[places_ref[b, k]] for b in range(row_blocks)], axis=0)
        high = chosen.astype(jnp.bfloat16).astype(jnp.float32)
        layer_ref[k] = jnp.transpose(jnp.concatenate([high, chosen - high], axis=0)).astype(jnp.bfloat16)

    def vectors(table, t):
        right = layer_ref[items_ref[table, t]] * mask_ref[items_ref[table + 1, t]]
        return jnp.concatenate([right, right], axis=0)

    def add_group(lefts, rights):
        left, right = jnp.concatenate(lefts, axis=1), jnp.concatenate(rights, axis=0)
        acc_ref[...] += jnp.dot(left, right, preferred_element_type=jnp.float32)

    if step == 0:
        for d in range(freqs):
            if d:
                arrivals[d - 1].wait()

            @pl.loop(0, items_ref[4 * d + 3, 0])
            def _(group):
                lefts, rights = [], []
                for u in range(GROUP):
                    t = group * GROUP + u
                    stored = items_ref[4 * d + 2, t]
                    here = stored - d * g_refs[d].shape[0]
                    parts_of = split(jnp.concatenate([g_refs[d][here], c_refs[d][here]], axis=0))
                    left = jnp.concatenate(parts_of, axis=1)
                    split_ref[stored] = left
                    lefts.append(left)
                    rights.append(vectors(4 * d, t))
                add_group(lefts, rights)
    else:

        @pl.loop(0, items_ref[4 * freqs + 3, 0])
        def _(group):
            places = [group * FULL_GROUP + u for u in range(FULL_GROUP)]
            lefts = [split_ref[items_ref[4 * freqs + 2, t]] for t in places]
            add_group(lefts, [vectors(4 * freqs, t) for t in places])

    half = row_blocks * parts
    gsum, csum = jnp.transpose(acc_ref[:size]), jnp.transpose(acc_ref[size:])
    gsum, csum = gsum[:half] + gsum[half:], csum[:half] + csum[half:]
    turn = turn_ref[...]
    for b in range(row_blocks):
        at = slice(b * parts, (b + 1) * parts)
        other = pltpu.roll(csum[at], parts // 2, 0)
        local_ref[:, b * size : (b + 1) * size] = gsum[at] + turn * other

    if step == ITERS - 1:
        w = local_ref[...]
        zs = [zs_ref[i] for i in range(ITERS)]
        values = [lane_sum(z * w) for z in zs]
        gram = [[lane_sum(zs[i] * zs[j]) for j in range(i + 1)] for i in range(ITERS)]
        shares = []
        for i, z in enumerate(zs):
            along = lane_sum(z * w) if i else values[0]
            share = jnp.where(gram[i][i] > 0.0, along / gram[i][i], 0.0)
            shares.append(share)
            w = w - share * z
        values += shares + [lane_sum(z * w) for z in zs] + [lane_sum(w * w)]
        values += [gram[i][j] for i in range(ITERS) for j in range(i + 1)]
        for lane_at, value in enumerate(values):
            info = put_lane(info, SHARES + lane_at, value)
        leave.wait()
    info_ref[...] = info


def run_step(step, lists, turn, info, lines, prev, blocks, freqs):
    plane = len(lines)
    line, parts, rows = lines[0].shape
    row_blocks, slots = lists[1].shape
    size = rows // row_blocks
    vmem = pl.BlockSpec(memory_space=pltpu.VMEM)
    in_specs = [pl.BlockSpec(memory_space=pltpu.SMEM)] * 2 + [vmem] * (2 + plane + step + len(blocks))
    z = (plane * line * row_blocks + 1, parts, size)
    tile = jax.ShapeDtypeStruct((parts, LANES), jnp.float32)
    own = jax.ShapeDtypeStruct((parts, rows), jnp.float32)
    owns = jax.ShapeDtypeStruct((ITERS, parts, rows), jnp.float32)
    out_shape = [owns, tile] if step == ITERS - 1 else [jax.ShapeDtypeStruct(z, jnp.float32), own, tile]
    scratch_shapes = [
        pltpu.VMEM((slots, size, LANES), jnp.bfloat16),
        pltpu.VMEM((row_blocks + 1, size, LANES), jnp.bfloat16),
        pltpu.VMEM((2 * size, LANES), jnp.float32),
    ]
    out_specs = [vmem] * len(out_shape)
    far = pl.BlockSpec(memory_space=pl.ANY)
    if step == 0:
        received = len(in_specs) - freqs + 1
        in_specs[received:] = [far] * (freqs - 1)
        scratch_shapes += [
            pltpu.VMEM((freqs - 1,) + blocks[0].shape, jnp.float32),
            pltpu.SemaphoreType.DMA((freqs - 1,)),
        ]
        out_specs.append(vmem)
        out_shape.append(jax.ShapeDtypeStruct((row_blocks * slots, 2 * size, 2 * size), jnp.bfloat16))
    if step == ITERS - 1:
        out_specs[0] = far
        scratch_shapes += [
            pltpu.VMEM(z, jnp.float32),
            pltpu.VMEM((parts, rows), jnp.float32),
            pltpu.VMEM(owns.shape, jnp.float32),
            pltpu.SemaphoreType.DMA,
        ]
    return pl.pallas_call(
        functools.partial(step_kernel, step, plane, line, freqs),
        in_specs=in_specs,
        out_specs=out_specs,
        out_shape=out_shape,
        scratch_shapes=scratch_shapes,
        compiler_params=pltpu.CompilerParams(vmem_limit_bytes=VMEM_LIMIT),
        name=f"step_{step}",
    )(*lists, turn, info, *lines, *prev, *blocks)


def final_kernel(tiles_ref, far_ref, out_ref, residual_ref, own_ref, sem):
    arrive = pltpu.make_async_copy(far_ref, own_ref, sem)
    arrive.start()
    devices, parts, _ = tiles_ref.shape
    fit = LANES // parts
    tiles = [tiles_ref[i] for i in range(devices)]
    sets = [jnp.transpose(jnp.concatenate(tiles[at : at + fit], axis=0)) for at in range(0, devices, fit)]
    sums = tiles
    while len(sums) > 1:
        sums = [x + y for x, y in zip(sums[::2], sums[1::2])] + sums[len(sums) // 2 * 2 :]
    total = sums[0] + pltpu.roll(sums[0], parts // 2, 0)
    lane = lax.broadcasted_iota(jnp.int32, total.shape, 1)
    info = jnp.transpose(jnp.concatenate([jnp.where(lane < SHARES, tiles[0], total)] * fit, axis=0))

    def all_devices(shares):
        total = sum(shares[1:], shares[0])
        step = parts // 2
        while step < LANES:
            total = total + pltpu.roll(total, step, 1)
            step *= 2
        return total

    def row(table, at):
        return jnp.broadcast_to(table[at : at + 1], (8, LANES))

    zero = jnp.zeros((8, LANES), jnp.float32)
    norm, h00, h10, h01, h11, h21 = [row(info, i) for i in range(6)]
    last = [row(info, SHARES + i) for i in range(ITERS)]
    shares = []
    for s in sets:
        off = [last[i] - row(s, SHARES + ITERS + i) for i in range(ITERS)]
        square = row(s, SHARES + 3 * ITERS)
        at = SHARES + 3 * ITERS + 1
        for i in range(ITERS):
            square = square - 2.0 * off[i] * row(s, SHARES + 2 * ITERS + i)
            for j in range(i + 1):
                square = square + (1.0 if i == j else 2.0) * off[i] * off[j] * row(s, at)
                at += 1
        shares.append(square)
    height = jnp.sqrt(jnp.maximum(all_devices(shares), 0.0))
    hessen = [[h00, h01, last[0]], [h10, h11, last[1]], [zero, h21, last[2]], [zero, zero, height]]
    normal = [[sum(h[m] * h[n] for h in hessen) for n in range(ITERS)] for m in range(ITERS)]
    low = [[None] * ITERS for _ in range(ITERS)]
    middle = []
    for m in range(ITERS):
        for n in range(m):
            rest = normal[m][n] - sum((low[m][k] * low[n][k] for k in range(n)), zero)
            low[m][n] = rest / low[n][n]
        low[m][m] = jnp.sqrt(normal[m][m] - sum((low[m][k] * low[m][k] for k in range(m)), zero))
        rest = norm * hessen[0][m] - sum((low[m][k] * middle[k] for k in range(m)), zero)
        middle.append(rest / low[m][m])
    coef_y = [None] * ITERS
    for m in reversed(range(ITERS)):
        rest = middle[m] - sum((low[k][m] * coef_y[k] for k in range(m + 1, ITERS)), zero)
        coef_y[m] = rest / low[m][m]
    total = zero
    for i, h in enumerate(hessen):
        misfit = (norm if i == 0 else zero) - sum(h[m] * coef_y[m] for m in range(ITERS))
        total = total + misfit * misfit
    residual_ref[...] = jnp.sqrt(total)[:1, : parts // 2]
    columns = jnp.transpose(
        jnp.concatenate([y for y in coef_y] + [jnp.zeros((LANES - 8 * ITERS, LANES), jnp.float32)], axis=0)
    )[:parts]
    rows = own_ref.shape[-1]
    arrive.wait()
    x = sum(jnp.broadcast_to(columns[:, 8 * m : 8 * m + 1], (parts, rows)) * own_ref[m] for m in range(ITERS))
    out_ref[0] = x[: parts // 2]
    out_ref[1] = x[parts // 2 :]


def run_final(tiles, own):
    _, parts, rows = own.shape
    vmem = pl.BlockSpec(memory_space=pltpu.VMEM)
    return pl.pallas_call(
        final_kernel,
        in_specs=[vmem, pl.BlockSpec(memory_space=pl.ANY)],
        out_specs=[vmem] * 2,
        out_shape=[
            jax.ShapeDtypeStruct((2, parts // 2, rows), jnp.float32),
            jax.ShapeDtypeStruct((1, parts // 2), jnp.float32),
        ],
        scratch_shapes=[pltpu.VMEM(own.shape, jnp.float32), pltpu.SemaphoreType.DMA],
        name="final",
    )(tiles, own)


def make_shards(line, plane, freqs):
    def shards(excitation, g_blocks, c_blocks, pattern, counts, freq_ids):
        row_blocks, own_slots, size, _ = g_blocks.shape
        freq_count = excitation.shape[1]
        parts = 2 * freq_count
        where = jnp.stack([lax.axis_index(name) for name in ("line", "place", "freq")])
        scalars = jnp.concatenate([where, counts, freq_ids, pattern.reshape(-1)]).astype(jnp.int32)
        stored = (row_blocks * own_slots, size, size)
        g_own, c_own = g_blocks.reshape(stored), c_blocks.reshape(stored)
        *lists, turn, g_near, c_near = run_setup(
            scalars, pattern.shape, freq_count, g_own, c_own, line, plane, freqs
        )
        g_parts, c_parts = [g_near], [c_near]
        for d in range(1, freqs):
            perm = [(i, (i + d) % freqs) for i in range(freqs)]
            g_parts.append(lax.ppermute(g_own, "freq", perm))
            c_parts.append(lax.ppermute(c_own, "freq", perm))
        info = jnp.zeros((parts, LANES), jnp.float32)
        krylov = []
        rows = excitation
        blocks = g_parts + c_parts
        for step in range(ITERS):
            lines = gather_rows(rows, line, plane)
            result = run_step(step, lists, turn, info, lines, krylov, blocks, freqs)
            if step == ITERS - 1:
                own, info = result
            elif step == 0:
                z, rows, info, tiles = result
                blocks = [tiles]
                krylov.append(z)
            else:
                z, rows, info = result
                krylov.append(z)
        answer, residual = run_final(jnp.concatenate(gather_rows(info, line, plane)), own)
        return answer, residual.reshape(freq_count)

    return shards


def solution(mesh):
    line, plane = split_nodes(mesh.shape["node"])
    freqs = mesh.shape["freq"]
    fine = Mesh(mesh.devices.reshape(line, plane, freqs), ("line", "place", "freq"))
    node = ("line", "place")
    in_specs = (
        P(None, "freq", node),
        P(node, "freq", None, None),
        P(node, "freq", None, None),
        P(node, None),
        P(node),
        P("freq"),
    )
    out_specs = (P(None, "freq", node), P("freq"))
    shards = make_shards(line, plane, freqs)
    return jax.shard_map(shards, mesh=fine, in_specs=in_specs, out_specs=out_specs, check_vma=False)
```

```python
import functools
import math

import jax
import jax.numpy as jnp
from jax import lax
from jax.experimental import pallas as pl
from jax.experimental.pallas import tpu as pltpu
from jax.sharding import Mesh
from jax.sharding import PartitionSpec as P

ITERS = 3
LANES = 128
GROUP = 4
FULL_GROUP = 8
SHARES = 16
VMEM_LIMIT = 16 * 1024 * 1024


def split_nodes(nodes):
    plane = 4 if nodes % 4 == 0 else 1
    return nodes // plane, plane


def partner_steps(size):
    if size & (size - 1) == 0:
        return [[(i, i ^ d) for i in range(size)] for d in range(1, size)]
    return [[(i, (i + d) % size) for i in range(size)] for d in range(1, size)]


def distance(me, other, size):
    if size & (size - 1) == 0:
        return me ^ other
    return lax.rem(me - other + size, size)


def gather_rows(rows, line, plane):
    parts = rows.size // rows.shape[-1]
    held = [rows] + [lax.ppermute(rows, "line", perm) for perm in partner_steps(line)]
    whole_line = jnp.stack(held).reshape(line, parts, rows.shape[-1])
    return [whole_line] + [lax.ppermute(whole_line, "place", perm) for perm in partner_steps(plane)]


def setup_kernel(
    line, plane, freqs, scalars_ref, g_ref, c_ref,
    items_ref, places_ref, turn_ref, g_out_ref, c_out_ref, sems,
):
    row_blocks, slots = places_ref.shape
    pattern_at = 3 + row_blocks + turn_ref.shape[0] // 2
    own_slots = slots // freqs
    pieces = sems.shape[1]
    part = g_ref.shape[0] // pieces
    copies = []
    for m, (source, target) in enumerate(((g_ref, g_out_ref), (c_ref, c_out_ref))):
        for i in range(pieces):
            at = pl.ds(i * part, part)
            copies.append(pltpu.make_async_copy(source.at[at], target.at[at], sems.at[m, i]))
            copies[-1].start()

    order = lax.broadcasted_iota(jnp.int32, (8, LANES), 1)
    freq = scalars_ref[2]
    for table, d in enumerate(list(range(freqs)) + [None]):
        first = 0 if d is None else lax.rem(freq + (freqs - d), freqs) * own_slots
        group = FULL_GROUP if d is None else GROUP
        layer = jnp.zeros((8, LANES), jnp.int32) + first
        block = jnp.full((8, LANES), row_blocks, jnp.int32)
        home = jnp.zeros((8, LANES), jnp.int32)
        used = jnp.int32(0)
        for b in range(row_blocks):
            here = scalars_ref[3 + b] if d is None else jnp.clip(scalars_ref[3 + b] - first, 0, own_slots)
            inside = order - used
            hit = (inside >= 0) & (inside < here)
            layer = jnp.where(hit, first + inside, layer)
            block = jnp.where(hit, b, block)
            home = jnp.where(hit, b, home)
            used = used + here
        away = freq - lax.div(layer, own_slots)
        away = jnp.where(away < 0, away + freqs, away)
        stored = (away * row_blocks + home) * own_slots + lax.rem(layer, own_slots)
        groups = jnp.zeros((8, LANES), jnp.int32) + lax.div(used + (group - 1), group)
        for i, values in enumerate((layer, block, stored, groups)):
            items_ref[4 * table + i : 4 * table + i + 1, :] = values[:1]

    b_at = lax.broadcasted_iota(jnp.int32, places_ref.shape, 0)
    k_at = lax.broadcasted_iota(jnp.int32, places_ref.shape, 1)
    pattern = jnp.zeros(places_ref.shape, jnp.int32)
    for i in range(row_blocks * slots):
        pattern = jnp.where(b_at * slots + k_at == i, scalars_ref[pattern_at + i], pattern)
    owner = lax.div(pattern, row_blocks)
    far = distance(scalars_ref[0], lax.div(owner, plane), line)
    place = distance(scalars_ref[1], lax.rem(owner, plane), plane) * line + far
    place = place * row_blocks + lax.rem(pattern, row_blocks)
    count = jnp.zeros(pattern.shape, jnp.int32)
    for b in range(row_blocks):
        count = jnp.where(b_at == b, scalars_ref[3 + b], count)
    places_ref[...] = jnp.where(k_at < count, place, line * plane * row_blocks)

    half = turn_ref.shape[0] // 2
    row_at = lax.broadcasted_iota(jnp.int32, turn_ref.shape, 0)
    ids = jnp.zeros(turn_ref.shape, jnp.int32)
    for f in range(half):
        ids = jnp.where(lax.rem(row_at, half) == f, scalars_ref[3 + row_blocks + f], ids)
    angular = 0.2 * jnp.exp(ids.astype(jnp.float32) * (math.log(8.0) / 1000.0))
    turn_ref[...] = jnp.where(row_at < half, -angular, angular)
    for copy in copies:
        copy.wait()


def run_setup(scalars, shape, freq_count, g_own, c_own, line, plane, freqs):
    smem, vmem = pl.BlockSpec(memory_space=pltpu.SMEM), pl.BlockSpec(memory_space=pltpu.VMEM)
    far = pl.BlockSpec(memory_space=pl.ANY)
    blocks = jax.ShapeDtypeStruct(g_own.shape, jnp.float32)
    pieces = math.gcd(g_own.shape[0], 8)
    return pl.pallas_call(
        functools.partial(setup_kernel, line, plane, freqs),
        in_specs=[smem, far, far],
        out_specs=[vmem] * 5,
        out_shape=[
            jax.ShapeDtypeStruct((4 * (freqs + 1), LANES), jnp.int32),
            jax.ShapeDtypeStruct(shape, jnp.int32),
            jax.ShapeDtypeStruct((2 * freq_count, LANES), jnp.float32),
            blocks,
            blocks,
        ],
        scratch_shapes=[pltpu.SemaphoreType.DMA((2, pieces))],
        compiler_params=pltpu.CompilerParams(vmem_limit_bytes=VMEM_LIMIT),
        cost_estimate=pl.CostEstimate(flops=0, bytes_accessed=16 * g_own.size, transcendentals=0),
        name="setup",
    )(scalars, g_own, c_own)


def lane_sum(x):
    return jnp.sum(x, axis=1, keepdims=True)


def with_other_part(column):
    wide = jnp.broadcast_to(column, (column.shape[0], LANES))
    return wide + pltpu.roll(wide, column.shape[0] // 2, 0)


def put_lane(tile, lane, column):
    at = lax.broadcasted_iota(jnp.int32, tile.shape, 1) == lane
    return jnp.where(at, column, tile)


def split(x):
    high = x.astype(jnp.bfloat16)
    return high, (x - high.astype(jnp.float32)).astype(jnp.bfloat16)


def step_kernel(step, plane, line, freqs, items_ref, places_ref, turn_ref, info_in_ref, *refs):
    lines, refs = refs[:plane], refs[plane:]
    prev, refs = refs[:step], refs[step:]
    row_blocks, slots = places_ref.shape
    nodes = plane * line
    if step == 0:
        g_refs, c_refs = refs[:freqs], list(refs[freqs : 2 * freqs])
        z_ref, local_ref, info_ref, split_ref, layer_ref, mask_ref, acc_ref, kept_ref, sems = refs[2 * freqs :]
        arrivals = []
        for d in range(1, freqs):
            arrivals.append(pltpu.make_async_copy(c_refs[d], kept_ref.at[d - 1], sems.at[d - 1]))
            arrivals[-1].start()
            c_refs[d] = kept_ref.at[d - 1]
    elif step < ITERS - 1:
        split_ref, z_ref, local_ref, info_ref, layer_ref, mask_ref, acc_ref = refs
    else:
        split_ref, own_ref, info_ref, layer_ref, mask_ref, acc_ref, z_ref, local_ref = refs
    parts, rows = local_ref.shape
    size = rows // row_blocks

    lane = lax.broadcasted_iota(jnp.int32, (size, LANES), 1)
    for b in range(row_blocks):
        mask_ref[b] = jnp.where((lane // parts) % row_blocks == b, 1.0, 0.0).astype(jnp.bfloat16)
    mask_ref[row_blocks] = jnp.zeros((size, LANES), jnp.bfloat16)
    acc_ref[...] = jnp.zeros_like(acc_ref)
    z_ref[nodes * row_blocks] = jnp.zeros((parts, size), jnp.float32)

    def blocks(body, carry):
        for q in range(plane):

            def chunk(i, carry, q=q):
                x = lines[q][i]
                for b in range(row_blocks):
                    carry = body(b, x[:, b * size : (b + 1) * size], (q * line + i) * row_blocks + b, carry)
                return carry

            if line <= 4:
                for i in range(line):
                    carry = chunk(i, carry)
            else:
                carry = lax.fori_loop(0, line, chunk, carry)
        return carry

    def add(sums, b, term):
        return sums[:b] + (sums[b] + term,) + sums[b + 1 :]

    def whole(sums):
        while len(sums) > 1:
            sums = tuple(x + y for x, y in zip(sums[::2], sums[1::2])) + sums[len(sums) // 2 * 2 :]
        return with_other_part(lane_sum(sums[0]))

    none = (jnp.zeros((parts, size), jnp.float32),) * row_blocks
    info = info_in_ref[...]
    if step == 0:
        height = jnp.sqrt(whole(blocks(lambda b, x, at, sums: add(sums, b, x * x), none)))
        info = put_lane(info, 0, height)

        def normal(b, x, at, carry):
            z_ref[at] = x / height
            return carry
    else:
        first = 1 if step == 1 else 3

        def dot(b, x, at, sums):
            return tuple(add(s, b, p[at] * x) for s, p in zip(sums, prev))

        coeffs = [whole(s) for s in blocks(dot, (none,) * step)]
        for i, coeff in enumerate(coeffs):
            info = put_lane(info, first + i, coeff)

        def subtract(b, x, at, sums):
            for coeff, p in zip(coeffs, prev):
                x = x - coeff * p[at]
            z_ref[at] = x
            return add(sums, b, x * x)

        height = jnp.sqrt(whole(blocks(subtract, none)))
        info = put_lane(info, first + step, height)

        def normal(b, x, at, carry):
            z_ref[at] = z_ref[at] / height
            return carry

    blocks(normal, 0)

    for k in range(slots):
        chosen = jnp.concatenate([z_ref[places_ref[b, k]] for b in range(row_blocks)], axis=0)
        high = chosen.astype(jnp.bfloat16).astype(jnp.float32)
        layer_ref[k] = jnp.transpose(jnp.concatenate([high, chosen - high], axis=0)).astype(jnp.bfloat16)

    def vectors(table, t):
        right = layer_ref[items_ref[table, t]] * mask_ref[items_ref[table + 1, t]]
        return jnp.concatenate([right, right], axis=0)

    def add_group(lefts, rights):
        left, right = jnp.concatenate(lefts, axis=1), jnp.concatenate(rights, axis=0)
        acc_ref[...] += jnp.dot(left, right, preferred_element_type=jnp.float32)

    def work_off(table, sizes, slots_of):
        total = items_ref[4 * table + 3, 0] * sizes[-1]
        turns = lax.div(total, sizes[0])

        @pl.loop(0, turns)
        def _(turn):
            slots_of(turn * sizes[0], sizes[0])

        start = turns * sizes[0]
        for count in sizes[1:]:
            fits = total - start >= count
            pl.when(fits)(functools.partial(slots_of, start, count))
            start = start + jnp.where(fits, count, 0)

    if step == 0:
        for d in range(freqs):
            if d:
                arrivals[d - 1].wait()

            def split_slots(start, count, d=d):
                lefts, rights = [], []
                for u in range(count):
                    stored = items_ref[4 * d + 2, start + u]
                    here = stored - d * g_refs[d].shape[0]
                    parts_of = split(jnp.concatenate([g_refs[d][here], c_refs[d][here]], axis=0))
                    left = jnp.concatenate(parts_of, axis=1)
                    split_ref[stored] = left
                    lefts.append(left)
                    rights.append(vectors(4 * d, start + u))
                add_group(lefts, rights)

            work_off(d, (4 * GROUP, 2 * GROUP, GROUP), split_slots)
    else:

        def kept_slots(start, count):
            lefts = [split_ref[items_ref[4 * freqs + 2, start + u]] for u in range(count)]
            add_group(lefts, [vectors(4 * freqs, start + u) for u in range(count)])

        work_off(freqs, (4 * FULL_GROUP, 2 * FULL_GROUP, FULL_GROUP), kept_slots)

    half = row_blocks * parts
    gsum, csum = jnp.transpose(acc_ref[:size]), jnp.transpose(acc_ref[size:])
    gsum, csum = gsum[:half] + gsum[half:], csum[:half] + csum[half:]
    turn = turn_ref[...]
    for b in range(row_blocks):
        at = slice(b * parts, (b + 1) * parts)
        other = pltpu.roll(csum[at], parts // 2, 0)
        local_ref[:, b * size : (b + 1) * size] = gsum[at] + turn * other

    if step == ITERS - 1:
        w = local_ref[...]
        zs = [jnp.concatenate([p[b] for b in range(row_blocks)], axis=1) for p in (*prev, z_ref)]
        for i, z in enumerate(zs):
            own_ref[i] = z
        values = [lane_sum(z * w) for z in zs]
        gram = [[lane_sum(zs[i] * zs[j]) for j in range(i + 1)] for i in range(ITERS)]
        shares = []
        for i, z in enumerate(zs):
            along = lane_sum(z * w) if i else values[0]
            share = jnp.where(gram[i][i] > 0.0, along / gram[i][i], 0.0)
            shares.append(share)
            w = w - share * z
        values += shares + [lane_sum(z * w) for z in zs] + [lane_sum(w * w)]
        values += [gram[i][j] for i in range(ITERS) for j in range(i + 1)]
        for lane_at, value in enumerate(values):
            info = put_lane(info, SHARES + lane_at, value)
    info_ref[...] = info


def run_step(step, lists, turn, info, lines, prev, blocks, freqs):
    plane = len(lines)
    line, parts, rows = lines[0].shape
    row_blocks, slots = lists[1].shape
    size = rows // row_blocks
    vmem = pl.BlockSpec(memory_space=pltpu.VMEM)
    in_specs = [pl.BlockSpec(memory_space=pltpu.SMEM)] * 2 + [vmem] * (2 + plane + step + len(blocks))
    z = (plane * line * row_blocks + 1, parts, size)
    tile = jax.ShapeDtypeStruct((parts, LANES), jnp.float32)
    own = jax.ShapeDtypeStruct((parts, rows), jnp.float32)
    owns = jax.ShapeDtypeStruct((ITERS, parts, rows), jnp.float32)
    out_shape = [owns, tile] if step == ITERS - 1 else [jax.ShapeDtypeStruct(z, jnp.float32), own, tile]
    scratch_shapes = [
        pltpu.VMEM((slots, size, LANES), jnp.bfloat16),
        pltpu.VMEM((row_blocks + 1, size, LANES), jnp.bfloat16),
        pltpu.VMEM((2 * size, LANES), jnp.float32),
    ]
    if step == 0:
        received = len(in_specs) - freqs + 1
        in_specs[received:] = [pl.BlockSpec(memory_space=pl.ANY)] * (freqs - 1)
        scratch_shapes += [
            pltpu.VMEM((freqs - 1,) + blocks[0].shape, jnp.float32),
            pltpu.SemaphoreType.DMA((freqs - 1,)),
        ]
        out_shape.append(jax.ShapeDtypeStruct((row_blocks * slots, 2 * size, 2 * size), jnp.bfloat16))
    if step == ITERS - 1:
        scratch_shapes += [pltpu.VMEM(z, jnp.float32), pltpu.VMEM((parts, rows), jnp.float32)]
    return pl.pallas_call(
        functools.partial(step_kernel, step, plane, line, freqs),
        in_specs=in_specs,
        out_specs=[vmem] * len(out_shape),
        out_shape=out_shape,
        scratch_shapes=scratch_shapes,
        compiler_params=pltpu.CompilerParams(vmem_limit_bytes=VMEM_LIMIT),
        name=f"step_{step}",
    )(*lists, turn, info, *lines, *prev, *blocks)


def final_kernel(tiles_ref, own_ref, out_ref, residual_ref):
    devices, parts, _ = tiles_ref.shape
    fit = LANES // parts
    tiles = [tiles_ref[i] for i in range(devices)]
    sets = [jnp.transpose(jnp.concatenate(tiles[at : at + fit], axis=0)) for at in range(0, devices, fit)]
    sums = tiles
    while len(sums) > 1:
        sums = [x + y for x, y in zip(sums[::2], sums[1::2])] + sums[len(sums) // 2 * 2 :]
    total = sums[0] + pltpu.roll(sums[0], parts // 2, 0)
    lane = lax.broadcasted_iota(jnp.int32, total.shape, 1)
    info = jnp.transpose(jnp.concatenate([jnp.where(lane < SHARES, tiles[0], total)] * fit, axis=0))

    def all_devices(shares):
        total = sum(shares[1:], shares[0])
        step = parts // 2
        while step < LANES:
            total = total + pltpu.roll(total, step, 1)
            step *= 2
        return total

    def row(table, at):
        return jnp.broadcast_to(table[at : at + 1], (8, LANES))

    zero = jnp.zeros((8, LANES), jnp.float32)
    norm, h00, h10, h01, h11, h21 = [row(info, i) for i in range(6)]
    last = [row(info, SHARES + i) for i in range(ITERS)]
    shares = []
    for s in sets:
        off = [last[i] - row(s, SHARES + ITERS + i) for i in range(ITERS)]
        square = row(s, SHARES + 3 * ITERS)
        at = SHARES + 3 * ITERS + 1
        for i in range(ITERS):
            square = square - 2.0 * off[i] * row(s, SHARES + 2 * ITERS + i)
            for j in range(i + 1):
                square = square + (1.0 if i == j else 2.0) * off[i] * off[j] * row(s, at)
                at += 1
        shares.append(square)
    height = jnp.sqrt(jnp.maximum(all_devices(shares), 0.0))
    hessen = [[h00, h01, last[0]], [h10, h11, last[1]], [zero, h21, last[2]], [zero, zero, height]]
    normal = [[sum(h[m] * h[n] for h in hessen) for n in range(ITERS)] for m in range(ITERS)]
    low = [[None] * ITERS for _ in range(ITERS)]
    middle = []
    for m in range(ITERS):
        for n in range(m):
            rest = normal[m][n] - sum((low[m][k] * low[n][k] for k in range(n)), zero)
            low[m][n] = rest / low[n][n]
        low[m][m] = jnp.sqrt(normal[m][m] - sum((low[m][k] * low[m][k] for k in range(m)), zero))
        rest = norm * hessen[0][m] - sum((low[m][k] * middle[k] for k in range(m)), zero)
        middle.append(rest / low[m][m])
    coef_y = [None] * ITERS
    for m in reversed(range(ITERS)):
        rest = middle[m] - sum((low[k][m] * coef_y[k] for k in range(m + 1, ITERS)), zero)
        coef_y[m] = rest / low[m][m]
    total = zero
    for i, h in enumerate(hessen):
        misfit = (norm if i == 0 else zero) - sum(h[m] * coef_y[m] for m in range(ITERS))
        total = total + misfit * misfit
    residual_ref[...] = jnp.sqrt(total)[:1, : parts // 2]
    columns = jnp.transpose(
        jnp.concatenate([y for y in coef_y] + [jnp.zeros((LANES - 8 * ITERS, LANES), jnp.float32)], axis=0)
    )[:parts]
    rows = own_ref.shape[-1]
    x = sum(jnp.broadcast_to(columns[:, 8 * m : 8 * m + 1], (parts, rows)) * own_ref[m] for m in range(ITERS))
    out_ref[0] = x[: parts // 2]
    out_ref[1] = x[parts // 2 :]


def run_final(tiles, own):
    _, parts, rows = own.shape
    vmem = pl.BlockSpec(memory_space=pltpu.VMEM)
    return pl.pallas_call(
        final_kernel,
        in_specs=[vmem] * 2,
        out_specs=[vmem] * 2,
        out_shape=[
            jax.ShapeDtypeStruct((2, parts // 2, rows), jnp.float32),
            jax.ShapeDtypeStruct((1, parts // 2), jnp.float32),
        ],
        name="final",
    )(tiles, own)


def make_shards(line, plane, freqs):
    def shards(excitation, g_blocks, c_blocks, pattern, counts, freq_ids):
        row_blocks, own_slots, size, _ = g_blocks.shape
        freq_count = excitation.shape[1]
        parts = 2 * freq_count
        where = jnp.stack([lax.axis_index(name) for name in ("line", "place", "freq")])
        scalars = jnp.concatenate([where, counts, freq_ids, pattern.reshape(-1)]).astype(jnp.int32)
        stored = (row_blocks * own_slots, size, size)
        g_own, c_own = g_blocks.reshape(stored), c_blocks.reshape(stored)
        *lists, turn, g_near, c_near = run_setup(
            scalars, pattern.shape, freq_count, g_own, c_own, line, plane, freqs
        )
        g_parts, c_parts = [g_near], [c_near]
        for d in range(1, freqs):
            perm = [(i, (i + d) % freqs) for i in range(freqs)]
            g_parts.append(lax.ppermute(g_own, "freq", perm))
            c_parts.append(lax.ppermute(c_own, "freq", perm))
        info = jnp.zeros((parts, LANES), jnp.float32)
        krylov = []
        rows = excitation
        blocks = g_parts + c_parts
        for step in range(ITERS):
            lines = gather_rows(rows, line, plane)
            result = run_step(step, lists, turn, info, lines, krylov, blocks, freqs)
            if step == ITERS - 1:
                own, info = result
            elif step == 0:
                z, rows, info, tiles = result
                blocks = [tiles]
                krylov.append(z)
            else:
                z, rows, info = result
                krylov.append(z)
        answer, residual = run_final(jnp.concatenate(gather_rows(info, line, plane)), own)
        return answer, residual.reshape(freq_count)

    return shards


def solution(mesh):
    line, plane = split_nodes(mesh.shape["node"])
    freqs = mesh.shape["freq"]
    fine = Mesh(mesh.devices.reshape(line, plane, freqs), ("line", "place", "freq"))
    node = ("line", "place")
    in_specs = (
        P(None, "freq", node),
        P(node, "freq", None, None),
        P(node, "freq", None, None),
        P(node, None),
        P(node),
        P("freq"),
    )
    out_specs = (P(None, "freq", node), P("freq"))
    shards = make_shards(line, plane, freqs)
    return jax.shard_map(shards, mesh=fine, in_specs=in_specs, out_specs=out_specs, check_vma=False)
```

```python
import functools
import math

import jax
import jax.numpy as jnp
from jax import lax
from jax.experimental import pallas as pl
from jax.experimental.pallas import tpu as pltpu
from jax.sharding import Mesh
from jax.sharding import PartitionSpec as P

ITERS = 3
LANES = 128
GROUP = 4
FULL_GROUP = 8
SHARES = 16
VMEM_LIMIT = 16 * 1024 * 1024


def split_nodes(nodes):
    plane = 4 if nodes % 4 == 0 else 1
    return nodes // plane, plane


def partner_steps(size):
    if size & (size - 1) == 0:
        return [[(i, i ^ d) for i in range(size)] for d in range(1, size)]
    return [[(i, (i + d) % size) for i in range(size)] for d in range(1, size)]


def distance(me, other, size):
    if size & (size - 1) == 0:
        return me ^ other
    return lax.rem(me - other + size, size)


def gather_rows(rows, line, plane, between=None):
    parts = rows.size // rows.shape[-1]
    held = [rows] + [lax.ppermute(rows, "line", perm) for perm in partner_steps(line)]
    whole_line = jnp.stack(held).reshape(line, parts, rows.shape[-1])
    if between is not None:
        whole_line = whole_line + between[:1, :1]
    return [whole_line] + [lax.ppermute(whole_line, "place", perm) for perm in partner_steps(plane)]


def near_kernel(g_ref, c_ref, g_out_ref, c_out_ref, done_ref, sems):
    pieces = sems.shape[1]
    part = g_ref.shape[0] // pieces
    copies = []
    for m, (source, target) in enumerate(((g_ref, g_out_ref), (c_ref, c_out_ref))):
        for i in range(pieces):
            at = pl.ds(i * part, part)
            copies.append(pltpu.make_async_copy(source.at[at], target.at[at], sems.at[m, i]))
            copies[-1].start()
    for copy in copies:
        copy.wait()
    done_ref[...] = jnp.zeros_like(done_ref)


def bring_near(g_own, c_own):
    vmem, far = pl.BlockSpec(memory_space=pltpu.VMEM), pl.BlockSpec(memory_space=pl.ANY)
    blocks = jax.ShapeDtypeStruct(g_own.shape, jnp.float32)
    return pl.pallas_call(
        near_kernel,
        in_specs=[far] * 2,
        out_specs=[vmem] * 3,
        out_shape=[blocks] * 2 + [jax.ShapeDtypeStruct((8, LANES), jnp.float32)],
        scratch_shapes=[pltpu.SemaphoreType.DMA((2, math.gcd(g_own.shape[0], 8)))],
        compiler_params=pltpu.CompilerParams(vmem_limit_bytes=VMEM_LIMIT),
        cost_estimate=pl.CostEstimate(flops=0, bytes_accessed=16 * g_own.size, transcendentals=0),
        name="near",
    )(g_own, c_own)


def setup_kernel(line, plane, freqs, scalars_ref, items_ref, places_ref, turn_ref):
    row_blocks, slots = places_ref.shape
    pattern_at = 3 + row_blocks + turn_ref.shape[0] // 2
    own_slots = slots // freqs
    order = lax.broadcasted_iota(jnp.int32, (8, LANES), 1)
    freq = scalars_ref[2]
    for table, d in enumerate(list(range(freqs)) + [None]):
        first = 0 if d is None else lax.rem(freq + (freqs - d), freqs) * own_slots
        group = FULL_GROUP if d is None else GROUP
        layer = jnp.zeros((8, LANES), jnp.int32) + first
        block = jnp.full((8, LANES), row_blocks, jnp.int32)
        home = jnp.zeros((8, LANES), jnp.int32)
        used = jnp.int32(0)
        for b in range(row_blocks):
            here = scalars_ref[3 + b] if d is None else jnp.clip(scalars_ref[3 + b] - first, 0, own_slots)
            inside = order - used
            hit = (inside >= 0) & (inside < here)
            layer = jnp.where(hit, first + inside, layer)
            block = jnp.where(hit, b, block)
            home = jnp.where(hit, b, home)
            used = used + here
        away = freq - lax.div(layer, own_slots)
        away = jnp.where(away < 0, away + freqs, away)
        stored = (away * row_blocks + home) * own_slots + lax.rem(layer, own_slots)
        groups = jnp.zeros((8, LANES), jnp.int32) + lax.div(used + (group - 1), group)
        for i, values in enumerate((layer, block, stored, groups)):
            items_ref[4 * table + i : 4 * table + i + 1, :] = values[:1]

    b_at = lax.broadcasted_iota(jnp.int32, places_ref.shape, 0)
    k_at = lax.broadcasted_iota(jnp.int32, places_ref.shape, 1)
    pattern = jnp.zeros(places_ref.shape, jnp.int32)
    for i in range(row_blocks * slots):
        pattern = jnp.where(b_at * slots + k_at == i, scalars_ref[pattern_at + i], pattern)
    owner = lax.div(pattern, row_blocks)
    far = distance(scalars_ref[0], lax.div(owner, plane), line)
    place = distance(scalars_ref[1], lax.rem(owner, plane), plane) * line + far
    place = place * row_blocks + lax.rem(pattern, row_blocks)
    count = jnp.zeros(pattern.shape, jnp.int32)
    for b in range(row_blocks):
        count = jnp.where(b_at == b, scalars_ref[3 + b], count)
    places_ref[...] = jnp.where(k_at < count, place, line * plane * row_blocks)

    half = turn_ref.shape[0] // 2
    row_at = lax.broadcasted_iota(jnp.int32, turn_ref.shape, 0)
    ids = jnp.zeros(turn_ref.shape, jnp.int32)
    for f in range(half):
        ids = jnp.where(lax.rem(row_at, half) == f, scalars_ref[3 + row_blocks + f], ids)
    angular = 0.2 * jnp.exp(ids.astype(jnp.float32) * (math.log(8.0) / 1000.0))
    turn_ref[...] = jnp.where(row_at < half, -angular, angular)


def run_setup(scalars, shape, freq_count, line, plane, freqs):
    return pl.pallas_call(
        functools.partial(setup_kernel, line, plane, freqs),
        in_specs=[pl.BlockSpec(memory_space=pltpu.SMEM)],
        out_specs=[pl.BlockSpec(memory_space=pltpu.VMEM)] * 3,
        out_shape=[
            jax.ShapeDtypeStruct((4 * (freqs + 1), LANES), jnp.int32),
            jax.ShapeDtypeStruct(shape, jnp.int32),
            jax.ShapeDtypeStruct((2 * freq_count, LANES), jnp.float32),
        ],
        name="setup",
    )(scalars)


def lane_sum(x):
    return jnp.sum(x, axis=1, keepdims=True)


def with_other_part(column):
    wide = jnp.broadcast_to(column, (column.shape[0], LANES))
    return wide + pltpu.roll(wide, column.shape[0] // 2, 0)


def put_lane(tile, lane, column):
    at = lax.broadcasted_iota(jnp.int32, tile.shape, 1) == lane
    return jnp.where(at, column, tile)


def split(x):
    high = x.astype(jnp.bfloat16)
    return high, (x - high.astype(jnp.float32)).astype(jnp.bfloat16)


def step_kernel(step, plane, line, freqs, items_ref, places_ref, turn_ref, info_in_ref, *refs):
    lines, refs = refs[:plane], refs[plane:]
    prev, refs = refs[:step], refs[step:]
    row_blocks, slots = places_ref.shape
    nodes = plane * line
    if step == 0:
        g_refs, c_refs = refs[:freqs], list(refs[freqs : 2 * freqs])
        z_ref, local_ref, info_ref, split_ref, layer_ref, mask_ref, acc_ref, kept_ref, sems = refs[2 * freqs :]
        arrivals = []
        for d in range(1, freqs):
            arrivals.append(pltpu.make_async_copy(c_refs[d], kept_ref.at[d - 1], sems.at[d - 1]))
            arrivals[-1].start()
            c_refs[d] = kept_ref.at[d - 1]
    elif step < ITERS - 1:
        split_ref, z_ref, local_ref, info_ref, layer_ref, mask_ref, acc_ref = refs
    else:
        split_ref, own_ref, info_ref, layer_ref, mask_ref, acc_ref, z_ref, local_ref = refs
    parts, rows = local_ref.shape
    size = rows // row_blocks

    lane = lax.broadcasted_iota(jnp.int32, (size, LANES), 1)
    for b in range(row_blocks):
        mask_ref[b] = jnp.where((lane // parts) % row_blocks == b, 1.0, 0.0).astype(jnp.bfloat16)
    mask_ref[row_blocks] = jnp.zeros((size, LANES), jnp.bfloat16)
    acc_ref[...] = jnp.zeros_like(acc_ref)
    z_ref[nodes * row_blocks] = jnp.zeros((parts, size), jnp.float32)

    def blocks(body, carry):
        for q in range(plane):

            def chunk(i, carry, q=q):
                x = lines[q][i]
                for b in range(row_blocks):
                    carry = body(b, x[:, b * size : (b + 1) * size], (q * line + i) * row_blocks + b, carry)
                return carry

            if line <= 4:
                for i in range(line):
                    carry = chunk(i, carry)
            else:
                carry = lax.fori_loop(0, line, chunk, carry)
        return carry

    def add(sums, b, term):
        return sums[:b] + (sums[b] + term,) + sums[b + 1 :]

    def whole(sums):
        while len(sums) > 1:
            sums = tuple(x + y for x, y in zip(sums[::2], sums[1::2])) + sums[len(sums) // 2 * 2 :]
        return with_other_part(lane_sum(sums[0]))

    none = (jnp.zeros((parts, size), jnp.float32),) * row_blocks
    info = info_in_ref[...]
    if step == 0:
        height = jnp.sqrt(whole(blocks(lambda b, x, at, sums: add(sums, b, x * x), none)))
        info = put_lane(info, 0, height)

        def normal(b, x, at, carry):
            z_ref[at] = x / height
            return carry
    else:
        first = 1 if step == 1 else 3

        def dot(b, x, at, sums):
            return tuple(add(s, b, p[at] * x) for s, p in zip(sums, prev))

        coeffs = [whole(s) for s in blocks(dot, (none,) * step)]
        for i, coeff in enumerate(coeffs):
            info = put_lane(info, first + i, coeff)

        def subtract(b, x, at, sums):
            for coeff, p in zip(coeffs, prev):
                x = x - coeff * p[at]
            z_ref[at] = x
            return add(sums, b, x * x)

        height = jnp.sqrt(whole(blocks(subtract, none)))
        info = put_lane(info, first + step, height)

        def normal(b, x, at, carry):
            z_ref[at] = z_ref[at] / height
            return carry

    blocks(normal, 0)

    for k in range(slots):
        chosen = jnp.concatenate([z_ref[places_ref[b, k]] for b in range(row_blocks)], axis=0)
        high = chosen.astype(jnp.bfloat16).astype(jnp.float32)
        layer_ref[k] = jnp.transpose(jnp.concatenate([high, chosen - high], axis=0)).astype(jnp.bfloat16)

    def vectors(table, t):
        right = layer_ref[items_ref[table, t]] * mask_ref[items_ref[table + 1, t]]
        return jnp.concatenate([right, right], axis=0)

    def add_group(lefts, rights):
        left, right = jnp.concatenate(lefts, axis=1), jnp.concatenate(rights, axis=0)
        acc_ref[...] += jnp.dot(left, right, preferred_element_type=jnp.float32)

    def work_off(table, sizes, slots_of):
        total = items_ref[4 * table + 3, 0] * sizes[-1]
        turns = lax.div(total, sizes[0])

        @pl.loop(0, turns)
        def _(turn):
            slots_of(turn * sizes[0], sizes[0])

        start = turns * sizes[0]
        for count in sizes[1:]:
            fits = total - start >= count
            pl.when(fits)(functools.partial(slots_of, start, count))
            start = start + jnp.where(fits, count, 0)

    if step == 0:
        for d in range(freqs):
            if d:
                arrivals[d - 1].wait()

            def split_slots(start, count, d=d):
                lefts, rights = [], []
                for u in range(count):
                    stored = items_ref[4 * d + 2, start + u]
                    here = stored - d * g_refs[d].shape[0]
                    parts_of = split(jnp.concatenate([g_refs[d][here], c_refs[d][here]], axis=0))
                    left = jnp.concatenate(parts_of, axis=1)
                    split_ref[stored] = left
                    lefts.append(left)
                    rights.append(vectors(4 * d, start + u))
                add_group(lefts, rights)

            work_off(d, (4 * GROUP, 2 * GROUP, GROUP), split_slots)
    else:

        def kept_slots(start, count):
            lefts = [split_ref[items_ref[4 * freqs + 2, start + u]] for u in range(count)]
            add_group(lefts, [vectors(4 * freqs, start + u) for u in range(count)])

        work_off(freqs, (4 * FULL_GROUP, 2 * FULL_GROUP, FULL_GROUP), kept_slots)

    half = row_blocks * parts
    gsum, csum = jnp.transpose(acc_ref[:size]), jnp.transpose(acc_ref[size:])
    gsum, csum = gsum[:half] + gsum[half:], csum[:half] + csum[half:]
    turn = turn_ref[...]
    for b in range(row_blocks):
        at = slice(b * parts, (b + 1) * parts)
        other = pltpu.roll(csum[at], parts // 2, 0)
        local_ref[:, b * size : (b + 1) * size] = gsum[at] + turn * other

    if step == ITERS - 1:
        w = local_ref[...]
        zs = [jnp.concatenate([p[b] for b in range(row_blocks)], axis=1) for p in (*prev, z_ref)]
        for i, z in enumerate(zs):
            own_ref[i] = z
        values = [lane_sum(z * w) for z in zs]
        gram = [[lane_sum(zs[i] * zs[j]) for j in range(i + 1)] for i in range(ITERS)]
        shares = []
        for i, z in enumerate(zs):
            along = lane_sum(z * w) if i else values[0]
            share = jnp.where(gram[i][i] > 0.0, along / gram[i][i], 0.0)
            shares.append(share)
            w = w - share * z
        values += shares + [lane_sum(z * w) for z in zs] + [lane_sum(w * w)]
        values += [gram[i][j] for i in range(ITERS) for j in range(i + 1)]
        for lane_at, value in enumerate(values):
            info = put_lane(info, SHARES + lane_at, value)
    info_ref[...] = info


def run_step(step, lists, turn, info, lines, prev, blocks, freqs):
    plane = len(lines)
    line, parts, rows = lines[0].shape
    row_blocks, slots = lists[1].shape
    size = rows // row_blocks
    vmem = pl.BlockSpec(memory_space=pltpu.VMEM)
    in_specs = [pl.BlockSpec(memory_space=pltpu.SMEM)] * 2 + [vmem] * (2 + plane + step + len(blocks))
    z = (plane * line * row_blocks + 1, parts, size)
    tile = jax.ShapeDtypeStruct((parts, LANES), jnp.float32)
    own = jax.ShapeDtypeStruct((parts, rows), jnp.float32)
    owns = jax.ShapeDtypeStruct((ITERS, parts, rows), jnp.float32)
    out_shape = [owns, tile] if step == ITERS - 1 else [jax.ShapeDtypeStruct(z, jnp.float32), own, tile]
    scratch_shapes = [
        pltpu.VMEM((slots, size, LANES), jnp.bfloat16),
        pltpu.VMEM((row_blocks + 1, size, LANES), jnp.bfloat16),
        pltpu.VMEM((2 * size, LANES), jnp.float32),
    ]
    if step == 0:
        received = len(in_specs) - freqs + 1
        in_specs[received:] = [pl.BlockSpec(memory_space=pl.ANY)] * (freqs - 1)
        scratch_shapes += [
            pltpu.VMEM((freqs - 1,) + blocks[0].shape, jnp.float32),
            pltpu.SemaphoreType.DMA((freqs - 1,)),
        ]
        out_shape.append(jax.ShapeDtypeStruct((row_blocks * slots, 2 * size, 2 * size), jnp.bfloat16))
    if step == ITERS - 1:
        scratch_shapes += [pltpu.VMEM(z, jnp.float32), pltpu.VMEM((parts, rows), jnp.float32)]
    return pl.pallas_call(
        functools.partial(step_kernel, step, plane, line, freqs),
        in_specs=in_specs,
        out_specs=[vmem] * len(out_shape),
        out_shape=out_shape,
        scratch_shapes=scratch_shapes,
        compiler_params=pltpu.CompilerParams(vmem_limit_bytes=VMEM_LIMIT),
        name=f"step_{step}",
    )(*lists, turn, info, *lines, *prev, *blocks)


def final_kernel(tiles_ref, own_ref, out_ref, residual_ref):
    devices, parts, _ = tiles_ref.shape
    fit = LANES // parts
    tiles = [tiles_ref[i] for i in range(devices)]
    sets = [jnp.transpose(jnp.concatenate(tiles[at : at + fit], axis=0)) for at in range(0, devices, fit)]
    sums = tiles
    while len(sums) > 1:
        sums = [x + y for x, y in zip(sums[::2], sums[1::2])] + sums[len(sums) // 2 * 2 :]
    total = sums[0] + pltpu.roll(sums[0], parts // 2, 0)
    lane = lax.broadcasted_iota(jnp.int32, total.shape, 1)
    info = jnp.transpose(jnp.concatenate([jnp.where(lane < SHARES, tiles[0], total)] * fit, axis=0))

    def all_devices(shares):
        total = sum(shares[1:], shares[0])
        step = parts // 2
        while step < LANES:
            total = total + pltpu.roll(total, step, 1)
            step *= 2
        return total

    def row(table, at):
        return jnp.broadcast_to(table[at : at + 1], (8, LANES))

    zero = jnp.zeros((8, LANES), jnp.float32)
    norm, h00, h10, h01, h11, h21 = [row(info, i) for i in range(6)]
    last = [row(info, SHARES + i) for i in range(ITERS)]
    shares = []
    for s in sets:
        off = [last[i] - row(s, SHARES + ITERS + i) for i in range(ITERS)]
        square = row(s, SHARES + 3 * ITERS)
        at = SHARES + 3 * ITERS + 1
        for i in range(ITERS):
            square = square - 2.0 * off[i] * row(s, SHARES + 2 * ITERS + i)
            for j in range(i + 1):
                square = square + (1.0 if i == j else 2.0) * off[i] * off[j] * row(s, at)
                at += 1
        shares.append(square)
    height = jnp.sqrt(jnp.maximum(all_devices(shares), 0.0))
    hessen = [[h00, h01, last[0]], [h10, h11, last[1]], [zero, h21, last[2]], [zero, zero, height]]
    normal = [[sum(h[m] * h[n] for h in hessen) for n in range(ITERS)] for m in range(ITERS)]
    low = [[None] * ITERS for _ in range(ITERS)]
    middle = []
    for m in range(ITERS):
        for n in range(m):
            rest = normal[m][n] - sum((low[m][k] * low[n][k] for k in range(n)), zero)
            low[m][n] = rest / low[n][n]
        low[m][m] = jnp.sqrt(normal[m][m] - sum((low[m][k] * low[m][k] for k in range(m)), zero))
        rest = norm * hessen[0][m] - sum((low[m][k] * middle[k] for k in range(m)), zero)
        middle.append(rest / low[m][m])
    coef_y = [None] * ITERS
    for m in reversed(range(ITERS)):
        rest = middle[m] - sum((low[k][m] * coef_y[k] for k in range(m + 1, ITERS)), zero)
        coef_y[m] = rest / low[m][m]
    total = zero
    for i, h in enumerate(hessen):
        misfit = (norm if i == 0 else zero) - sum(h[m] * coef_y[m] for m in range(ITERS))
        total = total + misfit * misfit
    residual_ref[...] = jnp.sqrt(total)[:1, : parts // 2]
    columns = jnp.transpose(
        jnp.concatenate([y for y in coef_y] + [jnp.zeros((LANES - 8 * ITERS, LANES), jnp.float32)], axis=0)
    )[:parts]
    rows = own_ref.shape[-1]
    x = sum(jnp.broadcast_to(columns[:, 8 * m : 8 * m + 1], (parts, rows)) * own_ref[m] for m in range(ITERS))
    out_ref[0] = x[: parts // 2]
    out_ref[1] = x[parts // 2 :]


def run_final(tiles, own):
    _, parts, rows = own.shape
    vmem = pl.BlockSpec(memory_space=pltpu.VMEM)
    return pl.pallas_call(
        final_kernel,
        in_specs=[vmem] * 2,
        out_specs=[vmem] * 2,
        out_shape=[
            jax.ShapeDtypeStruct((2, parts // 2, rows), jnp.float32),
            jax.ShapeDtypeStruct((1, parts // 2), jnp.float32),
        ],
        name="final",
    )(tiles, own)


def make_shards(line, plane, freqs):
    def shards(excitation, g_blocks, c_blocks, pattern, counts, freq_ids):
        row_blocks, own_slots, size, _ = g_blocks.shape
        freq_count = excitation.shape[1]
        parts = 2 * freq_count
        where = jnp.stack([lax.axis_index(name) for name in ("line", "place", "freq")])
        scalars = jnp.concatenate([where, counts, freq_ids, pattern.reshape(-1)]).astype(jnp.int32)
        stored = (row_blocks * own_slots, size, size)
        g_own, c_own = g_blocks.reshape(stored), c_blocks.reshape(stored)
        *lists, turn = run_setup(scalars, pattern.shape, freq_count, line, plane, freqs)
        g_near, c_near, near = bring_near(g_own, c_own)
        g_parts, c_parts = [g_near], [c_near]
        for d in range(1, freqs):
            perm = [(i, (i + d) % freqs) for i in range(freqs)]
            g_parts.append(lax.ppermute(g_own, "freq", perm))
            c_parts.append(lax.ppermute(c_own, "freq", perm))
        info = jnp.zeros((parts, LANES), jnp.float32)
        krylov = []
        rows = excitation
        blocks = g_parts + c_parts
        for step in range(ITERS):
            lines = gather_rows(rows, line, plane, None if step else near)
            result = run_step(step, lists, turn, info, lines, krylov, blocks, freqs)
            if step == ITERS - 1:
                own, info = result
            elif step == 0:
                z, rows, info, tiles = result
                blocks = [tiles]
                krylov.append(z)
            else:
                z, rows, info = result
                krylov.append(z)
        answer, residual = run_final(jnp.concatenate(gather_rows(info, line, plane)), own)
        return answer, residual.reshape(freq_count)

    return shards


def solution(mesh):
    line, plane = split_nodes(mesh.shape["node"])
    freqs = mesh.shape["freq"]
    fine = Mesh(mesh.devices.reshape(line, plane, freqs), ("line", "place", "freq"))
    node = ("line", "place")
    in_specs = (
        P(None, "freq", node),
        P(node, "freq", None, None),
        P(node, "freq", None, None),
        P(node, None),
        P(node),
        P("freq"),
    )
    out_specs = (P(None, "freq", node), P("freq"))
    shards = make_shards(line, plane, freqs)
    return jax.shard_map(shards, mesh=fine, in_specs=in_specs, out_specs=out_specs, check_vma=False)
```

```python
import functools
import math

import jax
import jax.numpy as jnp
from jax import lax
from jax.experimental import pallas as pl
from jax.experimental.pallas import tpu as pltpu
from jax.sharding import Mesh
from jax.sharding import PartitionSpec as P

ITERS = 3
LANES = 128
GROUP = 4
FULL_GROUP = 8
SHARES = 16
VMEM_LIMIT = 16 * 1024 * 1024


def split_nodes(nodes):
    plane = 4 if nodes % 4 == 0 else 1
    return nodes // plane, plane


def partner_steps(size):
    if size & (size - 1) == 0:
        return [[(i, i ^ d) for i in range(size)] for d in range(1, size)]
    return [[(i, (i + d) % size) for i in range(size)] for d in range(1, size)]


def distance(me, other, size):
    if size & (size - 1) == 0:
        return me ^ other
    return lax.rem(me - other + size, size)


def gather_rows(rows, line, plane):
    parts = rows.size // rows.shape[-1]
    held = [rows] + [lax.ppermute(rows, "line", perm) for perm in partner_steps(line)]
    whole_line = jnp.stack(held).reshape(line, parts, rows.shape[-1])
    return [whole_line] + [lax.ppermute(whole_line, "place", perm) for perm in partner_steps(plane)]


def setup_kernel(
    line, plane, freqs, scalars_ref, g_ref, c_ref,
    items_ref, places_ref, turn_ref, g_out_ref, c_out_ref, sems,
):
    row_blocks, slots = places_ref.shape
    own_slots = slots // freqs
    pieces = sems.shape[1]
    part = g_ref.shape[0] // pieces
    copies = []
    for m, (source, target) in enumerate(((g_ref, g_out_ref), (c_ref, c_out_ref))):
        for i in range(pieces):
            at = pl.ds(i * part, part)
            copies.append(pltpu.make_async_copy(source.at[at], target.at[at], sems.at[m, i]))
            copies[-1].start()

    order = lax.broadcasted_iota(jnp.int32, (8, LANES), 1)
    freq = scalars_ref[row_blocks, 2]
    for table, d in enumerate(list(range(freqs)) + [None]):
        first = 0 if d is None else lax.rem(freq + (freqs - d), freqs) * own_slots
        group = FULL_GROUP if d is None else GROUP
        layer = jnp.zeros((8, LANES), jnp.int32) + first
        block = jnp.full((8, LANES), row_blocks, jnp.int32)
        home = jnp.zeros((8, LANES), jnp.int32)
        used = jnp.int32(0)
        for b in range(row_blocks):
            here = scalars_ref[row_blocks, 3 + b] if d is None else jnp.clip(scalars_ref[row_blocks, 3 + b] - first, 0, own_slots)
            inside = order - used
            hit = (inside >= 0) & (inside < here)
            layer = jnp.where(hit, first + inside, layer)
            block = jnp.where(hit, b, block)
            home = jnp.where(hit, b, home)
            used = used + here
        away = freq - lax.div(layer, own_slots)
        away = jnp.where(away < 0, away + freqs, away)
        stored = (away * row_blocks + home) * own_slots + lax.rem(layer, own_slots)
        groups = jnp.zeros((8, LANES), jnp.int32) + lax.div(used + (group - 1), group)
        for i, values in enumerate((layer, block, stored, groups)):
            items_ref[4 * table + i : 4 * table + i + 1, :] = values[:1]

    b_at = lax.broadcasted_iota(jnp.int32, places_ref.shape, 0)
    k_at = lax.broadcasted_iota(jnp.int32, places_ref.shape, 1)
    pattern = jnp.zeros(places_ref.shape, jnp.int32)
    for i in range(row_blocks * slots):
        pattern = jnp.where(b_at * slots + k_at == i, scalars_ref[i // slots, i % slots], pattern)
    owner = lax.div(pattern, row_blocks)
    far = distance(scalars_ref[row_blocks, 0], lax.div(owner, plane), line)
    place = distance(scalars_ref[row_blocks, 1], lax.rem(owner, plane), plane) * line + far
    place = place * row_blocks + lax.rem(pattern, row_blocks)
    count = jnp.zeros(pattern.shape, jnp.int32)
    for b in range(row_blocks):
        count = jnp.where(b_at == b, scalars_ref[row_blocks, 3 + b], count)
    places_ref[...] = jnp.where(k_at < count, place, line * plane * row_blocks)

    half = turn_ref.shape[0] // 2
    row_at = lax.broadcasted_iota(jnp.int32, turn_ref.shape, 0)
    ids = jnp.zeros(turn_ref.shape, jnp.int32)
    for f in range(half):
        ids = jnp.where(lax.rem(row_at, half) == f, scalars_ref[row_blocks, 3 + row_blocks + f], ids)
    angular = 0.2 * jnp.exp(ids.astype(jnp.float32) * (math.log(8.0) / 1000.0))
    turn_ref[...] = jnp.where(row_at < half, -angular, angular)
    for copy in copies:
        copy.wait()


def run_setup(scalars, shape, freq_count, g_own, c_own, line, plane, freqs):
    smem, vmem = pl.BlockSpec(memory_space=pltpu.SMEM), pl.BlockSpec(memory_space=pltpu.VMEM)
    far = pl.BlockSpec(memory_space=pl.ANY)
    blocks = jax.ShapeDtypeStruct(g_own.shape, jnp.float32)
    pieces = math.gcd(g_own.shape[0], 8)
    return pl.pallas_call(
        functools.partial(setup_kernel, line, plane, freqs),
        in_specs=[smem, far, far],
        out_specs=[vmem] * 5,
        out_shape=[
            jax.ShapeDtypeStruct((4 * (freqs + 1), LANES), jnp.int32),
            jax.ShapeDtypeStruct(shape, jnp.int32),
            jax.ShapeDtypeStruct((2 * freq_count, LANES), jnp.float32),
            blocks,
            blocks,
        ],
        scratch_shapes=[pltpu.SemaphoreType.DMA((2, pieces))],
        compiler_params=pltpu.CompilerParams(vmem_limit_bytes=VMEM_LIMIT),
        cost_estimate=pl.CostEstimate(flops=0, bytes_accessed=16 * g_own.size, transcendentals=0),
        name="setup",
    )(scalars, g_own, c_own)


def lane_sum(x):
    return jnp.sum(x, axis=1, keepdims=True)


def with_other_part(column):
    wide = jnp.broadcast_to(column, (column.shape[0], LANES))
    return wide + pltpu.roll(wide, column.shape[0] // 2, 0)


def put_lane(tile, lane, column):
    at = lax.broadcasted_iota(jnp.int32, tile.shape, 1) == lane
    return jnp.where(at, column, tile)


def split(x):
    high = x.astype(jnp.bfloat16)
    return high, (x - high.astype(jnp.float32)).astype(jnp.bfloat16)


def step_kernel(step, plane, line, freqs, items_ref, places_ref, turn_ref, info_in_ref, *refs):
    lines, refs = refs[:plane], refs[plane:]
    prev, refs = refs[:step], refs[step:]
    row_blocks, slots = places_ref.shape
    nodes = plane * line
    if step == 0:
        g_refs, c_refs = refs[:freqs], list(refs[freqs : 2 * freqs])
        z_ref, local_ref, info_ref, split_ref, layer_ref, mask_ref, acc_ref, kept_ref, sems = refs[2 * freqs :]
        arrivals = []
        for d in range(1, freqs):
            arrivals.append(pltpu.make_async_copy(c_refs[d], kept_ref.at[d - 1], sems.at[d - 1]))
            arrivals[-1].start()
            c_refs[d] = kept_ref.at[d - 1]
    elif step < ITERS - 1:
        split_ref, z_ref, local_ref, info_ref, layer_ref, mask_ref, acc_ref = refs
    else:
        split_ref, own_ref, info_ref, layer_ref, mask_ref, acc_ref, z_ref, local_ref = refs
    parts, rows = local_ref.shape
    size = rows // row_blocks

    lane = lax.broadcasted_iota(jnp.int32, (size, LANES), 1)
    for b in range(row_blocks):
        mask_ref[b] = jnp.where((lane // parts) % row_blocks == b, 1.0, 0.0).astype(jnp.bfloat16)
    mask_ref[row_blocks] = jnp.zeros((size, LANES), jnp.bfloat16)
    acc_ref[...] = jnp.zeros_like(acc_ref)
    z_ref[nodes * row_blocks] = jnp.zeros((parts, size), jnp.float32)

    def blocks(body, carry):
        for q in range(plane):

            def chunk(i, carry, q=q):
                x = lines[q][i]
                for b in range(row_blocks):
                    carry = body(b, x[:, b * size : (b + 1) * size], (q * line + i) * row_blocks + b, carry)
                return carry

            if line <= 4:
                for i in range(line):
                    carry = chunk(i, carry)
            else:
                carry = lax.fori_loop(0, line, chunk, carry)
        return carry

    def add(sums, b, term):
        return sums[:b] + (sums[b] + term,) + sums[b + 1 :]

    def whole(sums):
        while len(sums) > 1:
            sums = tuple(x + y for x, y in zip(sums[::2], sums[1::2])) + sums[len(sums) // 2 * 2 :]
        return with_other_part(lane_sum(sums[0]))

    none = (jnp.zeros((parts, size), jnp.float32),) * row_blocks
    info = info_in_ref[...]
    if step == 0:
        height = jnp.sqrt(whole(blocks(lambda b, x, at, sums: add(sums, b, x * x), none)))
        info = put_lane(info, 0, height)

        def normal(b, x, at, carry):
            z_ref[at] = x / height
            return carry
    else:
        first = 1 if step == 1 else 3

        def dot(b, x, at, sums):
            return tuple(add(s, b, p[at] * x) for s, p in zip(sums, prev))

        coeffs = [whole(s) for s in blocks(dot, (none,) * step)]
        for i, coeff in enumerate(coeffs):
            info = put_lane(info, first + i, coeff)

        def subtract(b, x, at, sums):
            for coeff, p in zip(coeffs, prev):
                x = x - coeff * p[at]
            z_ref[at] = x
            return add(sums, b, x * x)

        height = jnp.sqrt(whole(blocks(subtract, none)))
        info = put_lane(info, first + step, height)

        def normal(b, x, at, carry):
            z_ref[at] = z_ref[at] / height
            return carry

    blocks(normal, 0)

    for k in range(slots):
        chosen = jnp.concatenate([z_ref[places_ref[b, k]] for b in range(row_blocks)], axis=0)
        high = chosen.astype(jnp.bfloat16).astype(jnp.float32)
        layer_ref[k] = jnp.transpose(jnp.concatenate([high, chosen - high], axis=0)).astype(jnp.bfloat16)

    def vectors(table, t):
        right = layer_ref[items_ref[table, t]] * mask_ref[items_ref[table + 1, t]]
        return jnp.concatenate([right, right], axis=0)

    def add_group(lefts, rights):
        left, right = jnp.concatenate(lefts, axis=1), jnp.concatenate(rights, axis=0)
        acc_ref[...] += jnp.dot(left, right, preferred_element_type=jnp.float32)

    def work_off(table, sizes, slots_of):
        total = items_ref[4 * table + 3, 0] * sizes[-1]
        turns = lax.div(total, sizes[0])

        @pl.loop(0, turns)
        def _(turn):
            slots_of(turn * sizes[0], sizes[0])

        start = turns * sizes[0]
        for count in sizes[1:]:
            fits = total - start >= count
            pl.when(fits)(functools.partial(slots_of, start, count))
            start = start + jnp.where(fits, count, 0)

    if step == 0:
        for d in range(freqs):
            if d:
                arrivals[d - 1].wait()

            def split_slots(start, count, d=d):
                lefts, rights = [], []
                for u in range(count):
                    stored = items_ref[4 * d + 2, start + u]
                    here = stored - d * g_refs[d].shape[0]
                    parts_of = split(jnp.concatenate([g_refs[d][here], c_refs[d][here]], axis=0))
                    left = jnp.concatenate(parts_of, axis=1)
                    split_ref[stored] = left
                    lefts.append(left)
                    rights.append(vectors(4 * d, start + u))
                add_group(lefts, rights)

            work_off(d, (4 * GROUP, 2 * GROUP, GROUP), split_slots)
    else:

        def kept_slots(start, count):
            lefts = [split_ref[items_ref[4 * freqs + 2, start + u]] for u in range(count)]
            add_group(lefts, [vectors(4 * freqs, start + u) for u in range(count)])

        work_off(freqs, (4 * FULL_GROUP, 2 * FULL_GROUP, FULL_GROUP), kept_slots)

    half = row_blocks * parts
    gsum, csum = jnp.transpose(acc_ref[:size]), jnp.transpose(acc_ref[size:])
    gsum, csum = gsum[:half] + gsum[half:], csum[:half] + csum[half:]
    turn = turn_ref[...]
    for b in range(row_blocks):
        at = slice(b * parts, (b + 1) * parts)
        other = pltpu.roll(csum[at], parts // 2, 0)
        local_ref[:, b * size : (b + 1) * size] = gsum[at] + turn * other

    if step == ITERS - 1:
        w = local_ref[...]
        zs = [jnp.concatenate([p[b] for b in range(row_blocks)], axis=1) for p in (*prev, z_ref)]
        for i, z in enumerate(zs):
            own_ref[i] = z
        values = [lane_sum(z * w) for z in zs]
        gram = [[lane_sum(zs[i] * zs[j]) for j in range(i + 1)] for i in range(ITERS)]
        shares = []
        for i, z in enumerate(zs):
            along = lane_sum(z * w) if i else values[0]
            share = jnp.where(gram[i][i] > 0.0, along / gram[i][i], 0.0)
            shares.append(share)
            w = w - share * z
        values += shares + [lane_sum(z * w) for z in zs] + [lane_sum(w * w)]
        values += [gram[i][j] for i in range(ITERS) for j in range(i + 1)]
        for lane_at, value in enumerate(values):
            info = put_lane(info, SHARES + lane_at, value)
    info_ref[...] = info


def run_step(step, lists, turn, info, lines, prev, blocks, freqs):
    plane = len(lines)
    line, parts, rows = lines[0].shape
    row_blocks, slots = lists[1].shape
    size = rows // row_blocks
    vmem = pl.BlockSpec(memory_space=pltpu.VMEM)
    in_specs = [pl.BlockSpec(memory_space=pltpu.SMEM)] * 2 + [vmem] * (2 + plane + step + len(blocks))
    z = (plane * line * row_blocks + 1, parts, size)
    tile = jax.ShapeDtypeStruct((parts, LANES), jnp.float32)
    own = jax.ShapeDtypeStruct((parts, rows), jnp.float32)
    owns = jax.ShapeDtypeStruct((ITERS, parts, rows), jnp.float32)
    out_shape = [owns, tile] if step == ITERS - 1 else [jax.ShapeDtypeStruct(z, jnp.float32), own, tile]
    scratch_shapes = [
        pltpu.VMEM((slots, size, LANES), jnp.bfloat16),
        pltpu.VMEM((row_blocks + 1, size, LANES), jnp.bfloat16),
        pltpu.VMEM((2 * size, LANES), jnp.float32),
    ]
    if step == 0:
        received = len(in_specs) - freqs + 1
        in_specs[received:] = [pl.BlockSpec(memory_space=pl.ANY)] * (freqs - 1)
        scratch_shapes += [
            pltpu.VMEM((freqs - 1,) + blocks[0].shape, jnp.float32),
            pltpu.SemaphoreType.DMA((freqs - 1,)),
        ]
        out_shape.append(jax.ShapeDtypeStruct((row_blocks * slots, 2 * size, 2 * size), jnp.bfloat16))
    if step == ITERS - 1:
        scratch_shapes += [pltpu.VMEM(z, jnp.float32), pltpu.VMEM((parts, rows), jnp.float32)]
    return pl.pallas_call(
        functools.partial(step_kernel, step, plane, line, freqs),
        in_specs=in_specs,
        out_specs=[vmem] * len(out_shape),
        out_shape=out_shape,
        scratch_shapes=scratch_shapes,
        compiler_params=pltpu.CompilerParams(vmem_limit_bytes=VMEM_LIMIT),
        name=f"step_{step}",
    )(*lists, turn, info, *lines, *prev, *blocks)


def final_kernel(tiles_ref, own_ref, out_ref, residual_ref):
    devices, parts, _ = tiles_ref.shape
    fit = LANES // parts
    tiles = [tiles_ref[i] for i in range(devices)]
    sets = [jnp.transpose(jnp.concatenate(tiles[at : at + fit], axis=0)) for at in range(0, devices, fit)]
    sums = tiles
    while len(sums) > 1:
        sums = [x + y for x, y in zip(sums[::2], sums[1::2])] + sums[len(sums) // 2 * 2 :]
    total = sums[0] + pltpu.roll(sums[0], parts // 2, 0)
    lane = lax.broadcasted_iota(jnp.int32, total.shape, 1)
    info = jnp.transpose(jnp.concatenate([jnp.where(lane < SHARES, tiles[0], total)] * fit, axis=0))

    def all_devices(shares):
        total = sum(shares[1:], shares[0])
        step = parts // 2
        while step < LANES:
            total = total + pltpu.roll(total, step, 1)
            step *= 2
        return total

    def row(table, at):
        return jnp.broadcast_to(table[at : at + 1], (8, LANES))

    zero = jnp.zeros((8, LANES), jnp.float32)
    norm, h00, h10, h01, h11, h21 = [row(info, i) for i in range(6)]
    last = [row(info, SHARES + i) for i in range(ITERS)]
    shares = []
    for s in sets:
        off = [last[i] - row(s, SHARES + ITERS + i) for i in range(ITERS)]
        square = row(s, SHARES + 3 * ITERS)
        at = SHARES + 3 * ITERS + 1
        for i in range(ITERS):
            square = square - 2.0 * off[i] * row(s, SHARES + 2 * ITERS + i)
            for j in range(i + 1):
                square = square + (1.0 if i == j else 2.0) * off[i] * off[j] * row(s, at)
                at += 1
        shares.append(square)
    height = jnp.sqrt(jnp.maximum(all_devices(shares), 0.0))
    hessen = [[h00, h01, last[0]], [h10, h11, last[1]], [zero, h21, last[2]], [zero, zero, height]]
    normal = [[sum(h[m] * h[n] for h in hessen) for n in range(ITERS)] for m in range(ITERS)]
    low = [[None] * ITERS for _ in range(ITERS)]
    middle = []
    for m in range(ITERS):
        for n in range(m):
            rest = normal[m][n] - sum((low[m][k] * low[n][k] for k in range(n)), zero)
            low[m][n] = rest / low[n][n]
        low[m][m] = jnp.sqrt(normal[m][m] - sum((low[m][k] * low[m][k] for k in range(m)), zero))
        rest = norm * hessen[0][m] - sum((low[m][k] * middle[k] for k in range(m)), zero)
        middle.append(rest / low[m][m])
    coef_y = [None] * ITERS
    for m in reversed(range(ITERS)):
        rest = middle[m] - sum((low[k][m] * coef_y[k] for k in range(m + 1, ITERS)), zero)
        coef_y[m] = rest / low[m][m]
    total = zero
    for i, h in enumerate(hessen):
        misfit = (norm if i == 0 else zero) - sum(h[m] * coef_y[m] for m in range(ITERS))
        total = total + misfit * misfit
    residual_ref[...] = jnp.sqrt(total)[:1, : parts // 2]
    columns = jnp.transpose(
        jnp.concatenate([y for y in coef_y] + [jnp.zeros((LANES - 8 * ITERS, LANES), jnp.float32)], axis=0)
    )[:parts]
    rows = own_ref.shape[-1]
    x = sum(jnp.broadcast_to(columns[:, 8 * m : 8 * m + 1], (parts, rows)) * own_ref[m] for m in range(ITERS))
    out_ref[0] = x[: parts // 2]
    out_ref[1] = x[parts // 2 :]


def run_final(tiles, own):
    _, parts, rows = own.shape
    vmem = pl.BlockSpec(memory_space=pltpu.VMEM)
    return pl.pallas_call(
        final_kernel,
        in_specs=[vmem] * 2,
        out_specs=[vmem] * 2,
        out_shape=[
            jax.ShapeDtypeStruct((2, parts // 2, rows), jnp.float32),
            jax.ShapeDtypeStruct((1, parts // 2), jnp.float32),
        ],
        name="final",
    )(tiles, own)


def make_shards(line, plane, freqs):
    def shards(excitation, g_blocks, c_blocks, pattern, counts, freq_ids):
        row_blocks, own_slots, size, _ = g_blocks.shape
        freq_count = excitation.shape[1]
        parts = 2 * freq_count
        where = jnp.stack([lax.axis_index(name) for name in ("line", "place", "freq")])
        last_row = jnp.concatenate([where, counts, freq_ids])
        scalars = jnp.concatenate(
            [
                jnp.pad(pattern, ((0, 0), (0, LANES - pattern.shape[1]))),
                jnp.pad(last_row, (0, LANES - last_row.size))[None],
            ]
        ).astype(jnp.int32)
        stored = (row_blocks * own_slots, size, size)
        g_own, c_own = g_blocks.reshape(stored), c_blocks.reshape(stored)
        *lists, turn, g_near, c_near = run_setup(
            scalars, pattern.shape, freq_count, g_own, c_own, line, plane, freqs
        )
        g_parts, c_parts = [g_near], [c_near]
        for d in range(1, freqs):
            perm = [(i, (i + d) % freqs) for i in range(freqs)]
            g_parts.append(lax.ppermute(g_own, "freq", perm))
            c_parts.append(lax.ppermute(c_own, "freq", perm))
        info = jnp.zeros((parts, LANES), jnp.float32)
        krylov = []
        rows = excitation
        blocks = g_parts + c_parts
        for step in range(ITERS):
            lines = gather_rows(rows, line, plane)
            result = run_step(step, lists, turn, info, lines, krylov, blocks, freqs)
            if step == ITERS - 1:
                own, info = result
            elif step == 0:
                z, rows, info, tiles = result
                blocks = [tiles]
                krylov.append(z)
            else:
                z, rows, info = result
                krylov.append(z)
        answer, residual = run_final(jnp.concatenate(gather_rows(info, line, plane)), own)
        return answer, residual.reshape(freq_count)

    return shards


def solution(mesh):
    line, plane = split_nodes(mesh.shape["node"])
    freqs = mesh.shape["freq"]
    fine = Mesh(mesh.devices.reshape(line, plane, freqs), ("line", "place", "freq"))
    node = ("line", "place")
    in_specs = (
        P(None, "freq", node),
        P(node, "freq", None, None),
        P(node, "freq", None, None),
        P(node, None),
        P(node),
        P("freq"),
    )
    out_specs = (P(None, "freq", node), P("freq"))
    shards = make_shards(line, plane, freqs)
    return jax.shard_map(shards, mesh=fine, in_specs=in_specs, out_specs=out_specs, check_vma=False)
```

```python
import functools
import math

import jax
import jax.numpy as jnp
from jax import lax
from jax.experimental import pallas as pl
from jax.experimental.pallas import tpu as pltpu
from jax.sharding import Mesh
from jax.sharding import PartitionSpec as P

ITERS = 3
LANES = 128
GROUP = 4
FULL_GROUP = 8
SHARES = 16
VMEM_LIMIT = 16 * 1024 * 1024


def split_nodes(nodes):
    plane = 4 if nodes % 4 == 0 else 1
    return nodes // plane, plane


def partner_steps(size):
    if size & (size - 1) == 0:
        return [[(i, i ^ d) for i in range(size)] for d in range(1, size)]
    return [[(i, (i + d) % size) for i in range(size)] for d in range(1, size)]


def distance(me, other, size):
    if size & (size - 1) == 0:
        return me ^ other
    return lax.rem(me - other + size, size)


def gather_rows(rows, line, plane):
    parts = rows.size // rows.shape[-1]
    held = [rows] + [lax.ppermute(rows, "line", perm) for perm in partner_steps(line)]
    whole_line = jnp.stack(held).reshape(line, parts, rows.shape[-1])
    return [whole_line] + [lax.ppermute(whole_line, "place", perm) for perm in partner_steps(plane)]


def setup_kernel(line, plane, freqs, scalars_ref, items_ref, places_ref, turn_ref):
    row_blocks, slots = places_ref.shape
    own_slots = slots // freqs
    order = lax.broadcasted_iota(jnp.int32, (8, LANES), 1)
    freq = scalars_ref[row_blocks, 2]
    for table, d in enumerate(list(range(freqs)) + [None]):
        first = 0 if d is None else lax.rem(freq + (freqs - d), freqs) * own_slots
        group = FULL_GROUP if d is None else GROUP
        layer = jnp.zeros((8, LANES), jnp.int32) + first
        block = jnp.full((8, LANES), row_blocks, jnp.int32)
        home = jnp.zeros((8, LANES), jnp.int32)
        used = jnp.int32(0)
        for b in range(row_blocks):
            here = scalars_ref[row_blocks, 3 + b] if d is None else jnp.clip(scalars_ref[row_blocks, 3 + b] - first, 0, own_slots)
            inside = order - used
            hit = (inside >= 0) & (inside < here)
            layer = jnp.where(hit, first + inside, layer)
            block = jnp.where(hit, b, block)
            home = jnp.where(hit, b, home)
            used = used + here
        away = freq - lax.div(layer, own_slots)
        away = jnp.where(away < 0, away + freqs, away)
        stored = (away * row_blocks + home) * own_slots + lax.rem(layer, own_slots)
        groups = jnp.zeros((8, LANES), jnp.int32) + lax.div(used + (group - 1), group)
        for i, values in enumerate((layer, block, stored, groups)):
            items_ref[4 * table + i : 4 * table + i + 1, :] = values[:1]

    b_at = lax.broadcasted_iota(jnp.int32, places_ref.shape, 0)
    k_at = lax.broadcasted_iota(jnp.int32, places_ref.shape, 1)
    pattern = jnp.zeros(places_ref.shape, jnp.int32)
    for i in range(row_blocks * slots):
        pattern = jnp.where(b_at * slots + k_at == i, scalars_ref[i // slots, i % slots], pattern)
    owner = lax.div(pattern, row_blocks)
    far = distance(scalars_ref[row_blocks, 0], lax.div(owner, plane), line)
    place = distance(scalars_ref[row_blocks, 1], lax.rem(owner, plane), plane) * line + far
    place = place * row_blocks + lax.rem(pattern, row_blocks)
    count = jnp.zeros(pattern.shape, jnp.int32)
    for b in range(row_blocks):
        count = jnp.where(b_at == b, scalars_ref[row_blocks, 3 + b], count)
    places_ref[...] = jnp.where(k_at < count, place, line * plane * row_blocks)

    half = turn_ref.shape[0] // 2
    row_at = lax.broadcasted_iota(jnp.int32, turn_ref.shape, 0)
    ids = jnp.zeros(turn_ref.shape, jnp.int32)
    for f in range(half):
        ids = jnp.where(lax.rem(row_at, half) == f, scalars_ref[row_blocks, 3 + row_blocks + f], ids)
    angular = 0.2 * jnp.exp(ids.astype(jnp.float32) * (math.log(8.0) / 1000.0))
    turn_ref[...] = jnp.where(row_at < half, -angular, angular)


def run_setup(scalars, shape, freq_count, line, plane, freqs):
    return pl.pallas_call(
        functools.partial(setup_kernel, line, plane, freqs),
        in_specs=[pl.BlockSpec(memory_space=pltpu.SMEM)],
        out_specs=[pl.BlockSpec(memory_space=pltpu.VMEM)] * 3,
        out_shape=[
            jax.ShapeDtypeStruct((4 * (freqs + 1), LANES), jnp.int32),
            jax.ShapeDtypeStruct(shape, jnp.int32),
            jax.ShapeDtypeStruct((2 * freq_count, LANES), jnp.float32),
        ],
        name="setup",
    )(scalars)


def lane_sum(x):
    return jnp.sum(x, axis=1, keepdims=True)


def with_other_part(column):
    wide = jnp.broadcast_to(column, (column.shape[0], LANES))
    return wide + pltpu.roll(wide, column.shape[0] // 2, 0)


def put_lane(tile, lane, column):
    at = lax.broadcasted_iota(jnp.int32, tile.shape, 1) == lane
    return jnp.where(at, column, tile)


def split(x):
    high = x.astype(jnp.bfloat16)
    return high, (x - high.astype(jnp.float32)).astype(jnp.bfloat16)


def step_kernel(step, plane, line, freqs, items_ref, places_ref, turn_ref, info_in_ref, *refs):
    lines, refs = refs[:plane], refs[plane:]
    prev, refs = refs[:step], refs[step:]
    row_blocks, slots = places_ref.shape
    nodes = plane * line
    if step == 0:
        g_refs, c_refs = list(refs[:freqs]), list(refs[freqs : 2 * freqs])
        z_ref, local_ref, info_ref, split_ref, layer_ref, mask_ref, acc_ref, kept_ref, sems = refs[2 * freqs :]
        arrivals = []
        for at, (held, d) in enumerate([(c_refs, d) for d in range(1, freqs)] + [(g_refs, 0), (c_refs, 0)]):
            arrivals.append(pltpu.make_async_copy(held[d], kept_ref.at[at], sems.at[at]))
            arrivals[-1].start()
            held[d] = kept_ref.at[at]
    elif step < ITERS - 1:
        split_ref, z_ref, local_ref, info_ref, layer_ref, mask_ref, acc_ref = refs
    else:
        split_ref, own_ref, info_ref, layer_ref, mask_ref, acc_ref, z_ref, local_ref = refs
    parts, rows = local_ref.shape
    size = rows // row_blocks

    lane = lax.broadcasted_iota(jnp.int32, (size, LANES), 1)
    for b in range(row_blocks):
        mask_ref[b] = jnp.where((lane // parts) % row_blocks == b, 1.0, 0.0).astype(jnp.bfloat16)
    mask_ref[row_blocks] = jnp.zeros((size, LANES), jnp.bfloat16)
    acc_ref[...] = jnp.zeros_like(acc_ref)
    z_ref[nodes * row_blocks] = jnp.zeros((parts, size), jnp.float32)

    def blocks(body, carry):
        for q in range(plane):

            def chunk(i, carry, q=q):
                x = lines[q][i]
                for b in range(row_blocks):
                    carry = body(b, x[:, b * size : (b + 1) * size], (q * line + i) * row_blocks + b, carry)
                return carry

            if line <= 4:
                for i in range(line):
                    carry = chunk(i, carry)
            else:
                carry = lax.fori_loop(0, line, chunk, carry)
        return carry

    def add(sums, b, term):
        return sums[:b] + (sums[b] + term,) + sums[b + 1 :]

    def whole(sums):
        while len(sums) > 1:
            sums = tuple(x + y for x, y in zip(sums[::2], sums[1::2])) + sums[len(sums) // 2 * 2 :]
        return with_other_part(lane_sum(sums[0]))

    none = (jnp.zeros((parts, size), jnp.float32),) * row_blocks
    info = info_in_ref[...]
    if step == 0:
        height = jnp.sqrt(whole(blocks(lambda b, x, at, sums: add(sums, b, x * x), none)))
        info = put_lane(info, 0, height)

        def normal(b, x, at, carry):
            z_ref[at] = x / height
            return carry
    else:
        first = 1 if step == 1 else 3

        def dot(b, x, at, sums):
            return tuple(add(s, b, p[at] * x) for s, p in zip(sums, prev))

        coeffs = [whole(s) for s in blocks(dot, (none,) * step)]
        for i, coeff in enumerate(coeffs):
            info = put_lane(info, first + i, coeff)

        def subtract(b, x, at, sums):
            for coeff, p in zip(coeffs, prev):
                x = x - coeff * p[at]
            z_ref[at] = x
            return add(sums, b, x * x)

        height = jnp.sqrt(whole(blocks(subtract, none)))
        info = put_lane(info, first + step, height)

        def normal(b, x, at, carry):
            z_ref[at] = z_ref[at] / height
            return carry

    blocks(normal, 0)

    for k in range(slots):
        chosen = jnp.concatenate([z_ref[places_ref[b, k]] for b in range(row_blocks)], axis=0)
        high = chosen.astype(jnp.bfloat16).astype(jnp.float32)
        layer_ref[k] = jnp.transpose(jnp.concatenate([high, chosen - high], axis=0)).astype(jnp.bfloat16)

    def vectors(table, t):
        right = layer_ref[items_ref[table, t]] * mask_ref[items_ref[table + 1, t]]
        return jnp.concatenate([right, right], axis=0)

    def add_group(lefts, rights):
        left, right = jnp.concatenate(lefts, axis=1), jnp.concatenate(rights, axis=0)
        acc_ref[...] += jnp.dot(left, right, preferred_element_type=jnp.float32)

    def work_off(table, sizes, slots_of):
        total = items_ref[4 * table + 3, 0] * sizes[-1]
        turns = lax.div(total, sizes[0])

        @pl.loop(0, turns)
        def _(turn):
            slots_of(turn * sizes[0], sizes[0])

        start = turns * sizes[0]
        for count in sizes[1:]:
            fits = total - start >= count
            pl.when(fits)(functools.partial(slots_of, start, count))
            start = start + jnp.where(fits, count, 0)

    if step == 0:
        for d in (*range(1, freqs), 0):
            for arrival in [arrivals[d - 1]] if d else arrivals[freqs - 1 :]:
                arrival.wait()

            def split_slots(start, count, d=d):
                lefts, rights = [], []
                for u in range(count):
                    stored = items_ref[4 * d + 2, start + u]
                    here = stored - d * g_refs[d].shape[0]
                    parts_of = split(jnp.concatenate([g_refs[d][here], c_refs[d][here]], axis=0))
                    left = jnp.concatenate(parts_of, axis=1)
                    split_ref[stored] = left
                    lefts.append(left)
                    rights.append(vectors(4 * d, start + u))
                add_group(lefts, rights)

            work_off(d, (4 * GROUP, 2 * GROUP, GROUP), split_slots)
    else:

        def kept_slots(start, count):
            lefts = [split_ref[items_ref[4 * freqs + 2, start + u]] for u in range(count)]
            add_group(lefts, [vectors(4 * freqs, start + u) for u in range(count)])

        work_off(freqs, (4 * FULL_GROUP, 2 * FULL_GROUP, FULL_GROUP), kept_slots)

    half = row_blocks * parts
    gsum, csum = jnp.transpose(acc_ref[:size]), jnp.transpose(acc_ref[size:])
    gsum, csum = gsum[:half] + gsum[half:], csum[:half] + csum[half:]
    turn = turn_ref[...]
    for b in range(row_blocks):
        at = slice(b * parts, (b + 1) * parts)
        other = pltpu.roll(csum[at], parts // 2, 0)
        local_ref[:, b * size : (b + 1) * size] = gsum[at] + turn * other

    if step == ITERS - 1:
        w = local_ref[...]
        zs = [jnp.concatenate([p[b] for b in range(row_blocks)], axis=1) for p in (*prev, z_ref)]
        for i, z in enumerate(zs):
            own_ref[i] = z
        values = [lane_sum(z * w) for z in zs]
        gram = [[lane_sum(zs[i] * zs[j]) for j in range(i + 1)] for i in range(ITERS)]
        shares = []
        for i, z in enumerate(zs):
            along = lane_sum(z * w) if i else values[0]
            share = jnp.where(gram[i][i] > 0.0, along / gram[i][i], 0.0)
            shares.append(share)
            w = w - share * z
        values += shares + [lane_sum(z * w) for z in zs] + [lane_sum(w * w)]
        values += [gram[i][j] for i in range(ITERS) for j in range(i + 1)]
        for lane_at, value in enumerate(values):
            info = put_lane(info, SHARES + lane_at, value)
    info_ref[...] = info


def run_step(step, lists, turn, info, lines, prev, blocks, freqs):
    plane = len(lines)
    line, parts, rows = lines[0].shape
    row_blocks, slots = lists[1].shape
    size = rows // row_blocks
    vmem = pl.BlockSpec(memory_space=pltpu.VMEM)
    in_specs = [pl.BlockSpec(memory_space=pltpu.SMEM)] * 2 + [vmem] * (2 + plane + step + len(blocks))
    z = (plane * line * row_blocks + 1, parts, size)
    tile = jax.ShapeDtypeStruct((parts, LANES), jnp.float32)
    own = jax.ShapeDtypeStruct((parts, rows), jnp.float32)
    owns = jax.ShapeDtypeStruct((ITERS, parts, rows), jnp.float32)
    out_shape = [owns, tile] if step == ITERS - 1 else [jax.ShapeDtypeStruct(z, jnp.float32), own, tile]
    scratch_shapes = [
        pltpu.VMEM((slots, size, LANES), jnp.bfloat16),
        pltpu.VMEM((row_blocks + 1, size, LANES), jnp.bfloat16),
        pltpu.VMEM((2 * size, LANES), jnp.float32),
    ]
    if step == 0:
        received = len(in_specs) - freqs + 1
        far = pl.BlockSpec(memory_space=pl.ANY)
        in_specs[received - 1 :] = [far] * freqs
        in_specs[received - 1 - freqs] = far
        scratch_shapes += [
            pltpu.VMEM((freqs + 1,) + blocks[0].shape, jnp.float32),
            pltpu.SemaphoreType.DMA((freqs + 1,)),
        ]
        out_shape.append(jax.ShapeDtypeStruct((row_blocks * slots, 2 * size, 2 * size), jnp.bfloat16))
    if step == ITERS - 1:
        scratch_shapes += [pltpu.VMEM(z, jnp.float32), pltpu.VMEM((parts, rows), jnp.float32)]
    return pl.pallas_call(
        functools.partial(step_kernel, step, plane, line, freqs),
        in_specs=in_specs,
        out_specs=[vmem] * len(out_shape),
        out_shape=out_shape,
        scratch_shapes=scratch_shapes,
        compiler_params=pltpu.CompilerParams(vmem_limit_bytes=VMEM_LIMIT),
        name=f"step_{step}",
    )(*lists, turn, info, *lines, *prev, *blocks)


def final_kernel(tiles_ref, own_ref, out_ref, residual_ref):
    devices, parts, _ = tiles_ref.shape
    fit = LANES // parts
    tiles = [tiles_ref[i] for i in range(devices)]
    sets = [jnp.transpose(jnp.concatenate(tiles[at : at + fit], axis=0)) for at in range(0, devices, fit)]
    sums = tiles
    while len(sums) > 1:
        sums = [x + y for x, y in zip(sums[::2], sums[1::2])] + sums[len(sums) // 2 * 2 :]
    total = sums[0] + pltpu.roll(sums[0], parts // 2, 0)
    lane = lax.broadcasted_iota(jnp.int32, total.shape, 1)
    info = jnp.transpose(jnp.concatenate([jnp.where(lane < SHARES, tiles[0], total)] * fit, axis=0))

    def all_devices(shares):
        total = sum(shares[1:], shares[0])
        step = parts // 2
        while step < LANES:
            total = total + pltpu.roll(total, step, 1)
            step *= 2
        return total

    def row(table, at):
        return jnp.broadcast_to(table[at : at + 1], (8, LANES))

    zero = jnp.zeros((8, LANES), jnp.float32)
    norm, h00, h10, h01, h11, h21 = [row(info, i) for i in range(6)]
    last = [row(info, SHARES + i) for i in range(ITERS)]
    shares = []
    for s in sets:
        off = [last[i] - row(s, SHARES + ITERS + i) for i in range(ITERS)]
        square = row(s, SHARES + 3 * ITERS)
        at = SHARES + 3 * ITERS + 1
        for i in range(ITERS):
            square = square - 2.0 * off[i] * row(s, SHARES + 2 * ITERS + i)
            for j in range(i + 1):
                square = square + (1.0 if i == j else 2.0) * off[i] * off[j] * row(s, at)
                at += 1
        shares.append(square)
    height = jnp.sqrt(jnp.maximum(all_devices(shares), 0.0))
    hessen = [[h00, h01, last[0]], [h10, h11, last[1]], [zero, h21, last[2]], [zero, zero, height]]
    normal = [[sum(h[m] * h[n] for h in hessen) for n in range(ITERS)] for m in range(ITERS)]
    low = [[None] * ITERS for _ in range(ITERS)]
    middle = []
    for m in range(ITERS):
        for n in range(m):
            rest = normal[m][n] - sum((low[m][k] * low[n][k] for k in range(n)), zero)
            low[m][n] = rest / low[n][n]
        low[m][m] = jnp.sqrt(normal[m][m] - sum((low[m][k] * low[m][k] for k in range(m)), zero))
        rest = norm * hessen[0][m] - sum((low[m][k] * middle[k] for k in range(m)), zero)
        middle.append(rest / low[m][m])
    coef_y = [None] * ITERS
    for m in reversed(range(ITERS)):
        rest = middle[m] - sum((low[k][m] * coef_y[k] for k in range(m + 1, ITERS)), zero)
        coef_y[m] = rest / low[m][m]
    total = zero
    for i, h in enumerate(hessen):
        misfit = (norm if i == 0 else zero) - sum(h[m] * coef_y[m] for m in range(ITERS))
        total = total + misfit * misfit
    residual_ref[...] = jnp.sqrt(total)[:1, : parts // 2]
    columns = jnp.transpose(
        jnp.concatenate([y for y in coef_y] + [jnp.zeros((LANES - 8 * ITERS, LANES), jnp.float32)], axis=0)
    )[:parts]
    rows = own_ref.shape[-1]
    x = sum(jnp.broadcast_to(columns[:, 8 * m : 8 * m + 1], (parts, rows)) * own_ref[m] for m in range(ITERS))
    out_ref[0] = x[: parts // 2]
    out_ref[1] = x[parts // 2 :]


def run_final(tiles, own):
    _, parts, rows = own.shape
    vmem = pl.BlockSpec(memory_space=pltpu.VMEM)
    return pl.pallas_call(
        final_kernel,
        in_specs=[vmem] * 2,
        out_specs=[vmem] * 2,
        out_shape=[
            jax.ShapeDtypeStruct((2, parts // 2, rows), jnp.float32),
            jax.ShapeDtypeStruct((1, parts // 2), jnp.float32),
        ],
        name="final",
    )(tiles, own)


def make_shards(line, plane, freqs):
    def shards(excitation, g_blocks, c_blocks, pattern, counts, freq_ids):
        row_blocks, own_slots, size, _ = g_blocks.shape
        freq_count = excitation.shape[1]
        parts = 2 * freq_count
        where = jnp.stack([lax.axis_index(name) for name in ("line", "place", "freq")])
        last_row = jnp.concatenate([where, counts, freq_ids])
        scalars = jnp.concatenate(
            [
                jnp.pad(pattern, ((0, 0), (0, LANES - pattern.shape[1]))),
                jnp.pad(last_row, (0, LANES - last_row.size))[None],
            ]
        ).astype(jnp.int32)
        stored = (row_blocks * own_slots, size, size)
        g_own, c_own = g_blocks.reshape(stored), c_blocks.reshape(stored)
        *lists, turn = run_setup(scalars, pattern.shape, freq_count, line, plane, freqs)
        g_parts, c_parts = [g_own], [c_own]
        for d in range(1, freqs):
            perm = [(i, (i + d) % freqs) for i in range(freqs)]
            g_parts.append(lax.ppermute(g_own, "freq", perm))
            c_parts.append(lax.ppermute(c_own, "freq", perm))
        info = jnp.zeros((parts, LANES), jnp.float32)
        krylov = []
        rows = excitation
        blocks = g_parts + c_parts
        for step in range(ITERS):
            lines = gather_rows(rows, line, plane)
            result = run_step(step, lists, turn, info, lines, krylov, blocks, freqs)
            if step == ITERS - 1:
                own, info = result
            elif step == 0:
                z, rows, info, tiles = result
                blocks = [tiles]
                krylov.append(z)
            else:
                z, rows, info = result
                krylov.append(z)
        answer, residual = run_final(jnp.concatenate(gather_rows(info, line, plane)), own)
        return answer, residual.reshape(freq_count)

    return shards


def solution(mesh):
    line, plane = split_nodes(mesh.shape["node"])
    freqs = mesh.shape["freq"]
    fine = Mesh(mesh.devices.reshape(line, plane, freqs), ("line", "place", "freq"))
    node = ("line", "place")
    in_specs = (
        P(None, "freq", node),
        P(node, "freq", None, None),
        P(node, "freq", None, None),
        P(node, None),
        P(node),
        P("freq"),
    )
    out_specs = (P(None, "freq", node), P("freq"))
    shards = make_shards(line, plane, freqs)
    return jax.shard_map(shards, mesh=fine, in_specs=in_specs, out_specs=out_specs, check_vma=False)
```

```python
import functools
import math

import jax
import jax.numpy as jnp
from jax import lax
from jax.experimental import pallas as pl
from jax.experimental.pallas import tpu as pltpu
from jax.sharding import Mesh
from jax.sharding import PartitionSpec as P

ITERS = 3
LANES = 128
GROUP = 4
FULL_GROUP = 8
SHARES = 16
VMEM_LIMIT = 8 * 1024 * 1024


def split_nodes(nodes):
    plane = 4 if nodes % 4 == 0 else 1
    return nodes // plane, plane


def partner_steps(size):
    if size & (size - 1) == 0:
        return [[(i, i ^ d) for i in range(size)] for d in range(1, size)]
    return [[(i, (i + d) % size) for i in range(size)] for d in range(1, size)]


def distance(me, other, size):
    if size & (size - 1) == 0:
        return me ^ other
    return lax.rem(me - other + size, size)


def gather_rows(rows, line, plane):
    parts = rows.size // rows.shape[-1]
    held = [rows] + [lax.ppermute(rows, "line", perm) for perm in partner_steps(line)]
    whole_line = jnp.stack(held).reshape(line, parts, rows.shape[-1])
    return [whole_line] + [lax.ppermute(whole_line, "place", perm) for perm in partner_steps(plane)]


def setup_kernel(
    line, plane, freqs, scalars_ref, g_ref, c_ref,
    items_ref, places_ref, turn_ref, g_out_ref, c_out_ref, sems,
):
    row_blocks, slots = places_ref.shape
    own_slots = slots // freqs
    pieces = sems.shape[1]
    part = g_ref.shape[0] // pieces
    copies = []
    for m, (source, target) in enumerate(((g_ref, g_out_ref), (c_ref, c_out_ref))):
        for i in range(pieces):
            at = pl.ds(i * part, part)
            copies.append(pltpu.make_async_copy(source.at[at], target.at[at], sems.at[m, i]))
            copies[-1].start()

    order = lax.broadcasted_iota(jnp.int32, (8, LANES), 1)
    freq = scalars_ref[row_blocks, 2]
    for table, d in enumerate(list(range(freqs)) + [None]):
        first = 0 if d is None else lax.rem(freq + (freqs - d), freqs) * own_slots
        group = FULL_GROUP if d is None else GROUP
        layer = jnp.zeros((8, LANES), jnp.int32) + first
        block = jnp.full((8, LANES), row_blocks, jnp.int32)
        home = jnp.zeros((8, LANES), jnp.int32)
        used = jnp.int32(0)
        for b in range(row_blocks):
            here = scalars_ref[row_blocks, 3 + b] if d is None else jnp.clip(scalars_ref[row_blocks, 3 + b] - first, 0, own_slots)
            inside = order - used
            hit = (inside >= 0) & (inside < here)
            layer = jnp.where(hit, first + inside, layer)
            block = jnp.where(hit, b, block)
            home = jnp.where(hit, b, home)
            used = used + here
        away = freq - lax.div(layer, own_slots)
        away = jnp.where(away < 0, away + freqs, away)
        stored = (away * row_blocks + home) * own_slots + lax.rem(layer, own_slots)
        groups = jnp.zeros((8, LANES), jnp.int32) + lax.div(used + (group - 1), group)
        for i, values in enumerate((layer, block, stored, groups)):
            items_ref[4 * table + i : 4 * table + i + 1, :] = values[:1]

    b_at = lax.broadcasted_iota(jnp.int32, places_ref.shape, 0)
    k_at = lax.broadcasted_iota(jnp.int32, places_ref.shape, 1)
    pattern = jnp.zeros(places_ref.shape, jnp.int32)
    for i in range(row_blocks * slots):
        pattern = jnp.where(b_at * slots + k_at == i, scalars_ref[i // slots, i % slots], pattern)
    owner = lax.div(pattern, row_blocks)
    far = distance(scalars_ref[row_blocks, 0], lax.div(owner, plane), line)
    place = distance(scalars_ref[row_blocks, 1], lax.rem(owner, plane), plane) * line + far
    place = place * row_blocks + lax.rem(pattern, row_blocks)
    count = jnp.zeros(pattern.shape, jnp.int32)
    for b in range(row_blocks):
        count = jnp.where(b_at == b, scalars_ref[row_blocks, 3 + b], count)
    places_ref[...] = jnp.where(k_at < count, place, line * plane * row_blocks)

    half = turn_ref.shape[0] // 2
    row_at = lax.broadcasted_iota(jnp.int32, turn_ref.shape, 0)
    ids = jnp.zeros(turn_ref.shape, jnp.int32)
    for f in range(half):
        ids = jnp.where(lax.rem(row_at, half) == f, scalars_ref[row_blocks, 3 + row_blocks + f], ids)
    angular = 0.2 * jnp.exp(ids.astype(jnp.float32) * (math.log(8.0) / 1000.0))
    turn_ref[...] = jnp.where(row_at < half, -angular, angular)
    for copy in copies:
        copy.wait()


def run_setup(scalars, shape, freq_count, g_own, c_own, line, plane, freqs):
    smem, vmem = pl.BlockSpec(memory_space=pltpu.SMEM), pl.BlockSpec(memory_space=pltpu.VMEM)
    far = pl.BlockSpec(memory_space=pl.ANY)
    blocks = jax.ShapeDtypeStruct(g_own.shape, jnp.float32)
    pieces = math.gcd(g_own.shape[0], 8)
    return pl.pallas_call(
        functools.partial(setup_kernel, line, plane, freqs),
        in_specs=[smem, far, far],
        out_specs=[vmem] * 5,
        out_shape=[
            jax.ShapeDtypeStruct((4 * (freqs + 1), LANES), jnp.int32),
            jax.ShapeDtypeStruct(shape, jnp.int32),
            jax.ShapeDtypeStruct((2 * freq_count, LANES), jnp.float32),
            blocks,
            blocks,
        ],
        scratch_shapes=[pltpu.SemaphoreType.DMA((2, pieces))],
        compiler_params=pltpu.CompilerParams(vmem_limit_bytes=VMEM_LIMIT),
        cost_estimate=pl.CostEstimate(flops=0, bytes_accessed=16 * g_own.size, transcendentals=0),
        name="setup",
    )(scalars, g_own, c_own)


def lane_sum(x):
    return jnp.sum(x, axis=1, keepdims=True)


def with_other_part(column):
    wide = jnp.broadcast_to(column, (column.shape[0], LANES))
    return wide + pltpu.roll(wide, column.shape[0] // 2, 0)


def put_lane(tile, lane, column):
    at = lax.broadcasted_iota(jnp.int32, tile.shape, 1) == lane
    return jnp.where(at, column, tile)


def split(x):
    high = x.astype(jnp.bfloat16)
    return high, (x - high.astype(jnp.float32)).astype(jnp.bfloat16)


def step_kernel(step, plane, line, freqs, items_ref, places_ref, turn_ref, info_in_ref, *refs):
    lines, refs = refs[:plane], refs[plane:]
    prev, refs = refs[:step], refs[step:]
    row_blocks, slots = places_ref.shape
    nodes = plane * line
    if step == 0:
        g_refs, c_refs = refs[:freqs], list(refs[freqs : 2 * freqs])
        z_ref, local_ref, info_ref, split_ref, layer_ref, mask_ref, acc_ref, kept_ref, sems = refs[2 * freqs :]
        arrivals = []
        for d in range(1, freqs):
            arrivals.append(pltpu.make_async_copy(c_refs[d], kept_ref.at[d - 1], sems.at[d - 1]))
            arrivals[-1].start()
            c_refs[d] = kept_ref.at[d - 1]
    elif step < ITERS - 1:
        split_ref, z_ref, local_ref, info_ref, layer_ref, mask_ref, acc_ref = refs
    else:
        split_ref, own_ref, info_ref, layer_ref, mask_ref, acc_ref, z_ref, local_ref = refs
    parts, rows = local_ref.shape
    size = rows // row_blocks

    lane = lax.broadcasted_iota(jnp.int32, (size, LANES), 1)
    for b in range(row_blocks):
        mask_ref[b] = jnp.where((lane // parts) % row_blocks == b, 1.0, 0.0).astype(jnp.bfloat16)
    mask_ref[row_blocks] = jnp.zeros((size, LANES), jnp.bfloat16)
    acc_ref[...] = jnp.zeros_like(acc_ref)
    z_ref[nodes * row_blocks] = jnp.zeros((parts, size), jnp.float32)

    def blocks(body, carry):
        for q in range(plane):

            def chunk(i, carry, q=q):
                x = lines[q][i]
                for b in range(row_blocks):
                    carry = body(b, x[:, b * size : (b + 1) * size], (q * line + i) * row_blocks + b, carry)
                return carry

            if line <= 4:
                for i in range(line):
                    carry = chunk(i, carry)
            else:
                carry = lax.fori_loop(0, line, chunk, carry)
        return carry

    def add(sums, b, term):
        return sums[:b] + (sums[b] + term,) + sums[b + 1 :]

    def whole(sums):
        while len(sums) > 1:
            sums = tuple(x + y for x, y in zip(sums[::2], sums[1::2])) + sums[len(sums) // 2 * 2 :]
        return with_other_part(lane_sum(sums[0]))

    none = (jnp.zeros((parts, size), jnp.float32),) * row_blocks
    info = info_in_ref[...]
    if step == 0:
        height = jnp.sqrt(whole(blocks(lambda b, x, at, sums: add(sums, b, x * x), none)))
        info = put_lane(info, 0, height)

        def normal(b, x, at, carry):
            z_ref[at] = x / height
            return carry
    else:
        first = 1 if step == 1 else 3

        def dot(b, x, at, sums):
            return tuple(add(s, b, p[at] * x) for s, p in zip(sums, prev))

        coeffs = [whole(s) for s in blocks(dot, (none,) * step)]
        for i, coeff in enumerate(coeffs):
            info = put_lane(info, first + i, coeff)

        def subtract(b, x, at, sums):
            for coeff, p in zip(coeffs, prev):
                x = x - coeff * p[at]
            z_ref[at] = x
            return add(sums, b, x * x)

        height = jnp.sqrt(whole(blocks(subtract, none)))
        info = put_lane(info, first + step, height)

        def normal(b, x, at, carry):
            z_ref[at] = z_ref[at] / height
            return carry

    blocks(normal, 0)

    for k in range(slots):
        chosen = jnp.concatenate([z_ref[places_ref[b, k]] for b in range(row_blocks)], axis=0)
        high = chosen.astype(jnp.bfloat16).astype(jnp.float32)
        layer_ref[k] = jnp.transpose(jnp.concatenate([high, chosen - high], axis=0)).astype(jnp.bfloat16)

    def vectors(table, t):
        right = layer_ref[items_ref[table, t]] * mask_ref[items_ref[table + 1, t]]
        return jnp.concatenate([right, right], axis=0)

    def add_group(lefts, rights):
        left, right = jnp.concatenate(lefts, axis=1), jnp.concatenate(rights, axis=0)
        acc_ref[...] += jnp.dot(left, right, preferred_element_type=jnp.float32)

    def work_off(table, sizes, slots_of):
        total = items_ref[4 * table + 3, 0] * sizes[-1]
        turns = lax.div(total, sizes[0])

        @pl.loop(0, turns)
        def _(turn):
            slots_of(turn * sizes[0], sizes[0])

        start = turns * sizes[0]
        for count in sizes[1:]:
            fits = total - start >= count
            pl.when(fits)(functools.partial(slots_of, start, count))
            start = start + jnp.where(fits, count, 0)

    if step == 0:
        for d in range(freqs):
            if d:
                arrivals[d - 1].wait()

            def split_slots(start, count, d=d):
                lefts, rights = [], []
                for u in range(count):
                    stored = items_ref[4 * d + 2, start + u]
                    here = stored - d * g_refs[d].shape[0]
                    parts_of = split(jnp.concatenate([g_refs[d][here], c_refs[d][here]], axis=0))
                    left = jnp.concatenate(parts_of, axis=1)
                    split_ref[stored] = left
                    lefts.append(left)
                    rights.append(vectors(4 * d, start + u))
                add_group(lefts, rights)

            work_off(d, (4 * GROUP, 2 * GROUP, GROUP), split_slots)
    else:

        def kept_slots(start, count):
            lefts = [split_ref[items_ref[4 * freqs + 2, start + u]] for u in range(count)]
            add_group(lefts, [vectors(4 * freqs, start + u) for u in range(count)])

        work_off(freqs, (4 * FULL_GROUP, 2 * FULL_GROUP, FULL_GROUP), kept_slots)

    half = row_blocks * parts
    gsum, csum = jnp.transpose(acc_ref[:size]), jnp.transpose(acc_ref[size:])
    gsum, csum = gsum[:half] + gsum[half:], csum[:half] + csum[half:]
    turn = turn_ref[...]
    for b in range(row_blocks):
        at = slice(b * parts, (b + 1) * parts)
        other = pltpu.roll(csum[at], parts // 2, 0)
        local_ref[:, b * size : (b + 1) * size] = gsum[at] + turn * other

    if step == ITERS - 1:
        w = local_ref[...]
        zs = [jnp.concatenate([p[b] for b in range(row_blocks)], axis=1) for p in (*prev, z_ref)]
        for i, z in enumerate(zs):
            own_ref[i] = z
        values = [lane_sum(z * w) for z in zs]
        gram = [[lane_sum(zs[i] * zs[j]) for j in range(i + 1)] for i in range(ITERS)]
        shares = []
        for i, z in enumerate(zs):
            along = lane_sum(z * w) if i else values[0]
            share = jnp.where(gram[i][i] > 0.0, along / gram[i][i], 0.0)
            shares.append(share)
            w = w - share * z
        values += shares + [lane_sum(z * w) for z in zs] + [lane_sum(w * w)]
        values += [gram[i][j] for i in range(ITERS) for j in range(i + 1)]
        for lane_at, value in enumerate(values):
            info = put_lane(info, SHARES + lane_at, value)
    info_ref[...] = info


def run_step(step, lists, turn, info, lines, prev, blocks, freqs):
    plane = len(lines)
    line, parts, rows = lines[0].shape
    row_blocks, slots = lists[1].shape
    size = rows // row_blocks
    vmem = pl.BlockSpec(memory_space=pltpu.VMEM)
    in_specs = [pl.BlockSpec(memory_space=pltpu.SMEM)] * 2 + [vmem] * (2 + plane + step + len(blocks))
    z = (plane * line * row_blocks + 1, parts, size)
    tile = jax.ShapeDtypeStruct((parts, LANES), jnp.float32)
    own = jax.ShapeDtypeStruct((parts, rows), jnp.float32)
    owns = jax.ShapeDtypeStruct((ITERS, parts, rows), jnp.float32)
    out_shape = [owns, tile] if step == ITERS - 1 else [jax.ShapeDtypeStruct(z, jnp.float32), own, tile]
    scratch_shapes = [
        pltpu.VMEM((slots, size, LANES), jnp.bfloat16),
        pltpu.VMEM((row_blocks + 1, size, LANES), jnp.bfloat16),
        pltpu.VMEM((2 * size, LANES), jnp.float32),
    ]
    if step == 0:
        received = len(in_specs) - freqs + 1
        in_specs[received:] = [pl.BlockSpec(memory_space=pl.ANY)] * (freqs - 1)
        scratch_shapes += [
            pltpu.VMEM((freqs - 1,) + blocks[0].shape, jnp.float32),
            pltpu.SemaphoreType.DMA((freqs - 1,)),
        ]
        out_shape.append(jax.ShapeDtypeStruct((row_blocks * slots, 2 * size, 2 * size), jnp.bfloat16))
    if step == ITERS - 1:
        scratch_shapes += [pltpu.VMEM(z, jnp.float32), pltpu.VMEM((parts, rows), jnp.float32)]
    return pl.pallas_call(
        functools.partial(step_kernel, step, plane, line, freqs),
        in_specs=in_specs,
        out_specs=[vmem] * len(out_shape),
        out_shape=out_shape,
        scratch_shapes=scratch_shapes,
        compiler_params=pltpu.CompilerParams(vmem_limit_bytes=VMEM_LIMIT),
        name=f"step_{step}",
    )(*lists, turn, info, *lines, *prev, *blocks)


def final_kernel(tiles_ref, own_ref, out_ref, residual_ref):
    devices, parts, _ = tiles_ref.shape
    fit = LANES // parts
    tiles = [tiles_ref[i] for i in range(devices)]
    sets = [jnp.transpose(jnp.concatenate(tiles[at : at + fit], axis=0)) for at in range(0, devices, fit)]
    sums = tiles
    while len(sums) > 1:
        sums = [x + y for x, y in zip(sums[::2], sums[1::2])] + sums[len(sums) // 2 * 2 :]
    total = sums[0] + pltpu.roll(sums[0], parts // 2, 0)
    lane = lax.broadcasted_iota(jnp.int32, total.shape, 1)
    info = jnp.transpose(jnp.concatenate([jnp.where(lane < SHARES, tiles[0], total)] * fit, axis=0))

    def all_devices(shares):
        total = sum(shares[1:], shares[0])
        step = parts // 2
        while step < LANES:
            total = total + pltpu.roll(total, step, 1)
            step *= 2
        return total

    def row(table, at):
        return jnp.broadcast_to(table[at : at + 1], (8, LANES))

    zero = jnp.zeros((8, LANES), jnp.float32)
    norm, h00, h10, h01, h11, h21 = [row(info, i) for i in range(6)]
    last = [row(info, SHARES + i) for i in range(ITERS)]
    shares = []
    for s in sets:
        off = [last[i] - row(s, SHARES + ITERS + i) for i in range(ITERS)]
        square = row(s, SHARES + 3 * ITERS)
        at = SHARES + 3 * ITERS + 1
        for i in range(ITERS):
            square = square - 2.0 * off[i] * row(s, SHARES + 2 * ITERS + i)
            for j in range(i + 1):
                square = square + (1.0 if i == j else 2.0) * off[i] * off[j] * row(s, at)
                at += 1
        shares.append(square)
    height = jnp.sqrt(jnp.maximum(all_devices(shares), 0.0))
    hessen = [[h00, h01, last[0]], [h10, h11, last[1]], [zero, h21, last[2]], [zero, zero, height]]
    normal = [[sum(h[m] * h[n] for h in hessen) for n in range(ITERS)] for m in range(ITERS)]
    low = [[None] * ITERS for _ in range(ITERS)]
    middle = []
    for m in range(ITERS):
        for n in range(m):
            rest = normal[m][n] - sum((low[m][k] * low[n][k] for k in range(n)), zero)
            low[m][n] = rest / low[n][n]
        low[m][m] = jnp.sqrt(normal[m][m] - sum((low[m][k] * low[m][k] for k in range(m)), zero))
        rest = norm * hessen[0][m] - sum((low[m][k] * middle[k] for k in range(m)), zero)
        middle.append(rest / low[m][m])
    coef_y = [None] * ITERS
    for m in reversed(range(ITERS)):
        rest = middle[m] - sum((low[k][m] * coef_y[k] for k in range(m + 1, ITERS)), zero)
        coef_y[m] = rest / low[m][m]
    total = zero
    for i, h in enumerate(hessen):
        misfit = (norm if i == 0 else zero) - sum(h[m] * coef_y[m] for m in range(ITERS))
        total = total + misfit * misfit
    residual_ref[...] = jnp.sqrt(total)[:1, : parts // 2]
    columns = jnp.transpose(
        jnp.concatenate([y for y in coef_y] + [jnp.zeros((LANES - 8 * ITERS, LANES), jnp.float32)], axis=0)
    )[:parts]
    rows = own_ref.shape[-1]
    x = sum(jnp.broadcast_to(columns[:, 8 * m : 8 * m + 1], (parts, rows)) * own_ref[m] for m in range(ITERS))
    out_ref[0] = x[: parts // 2]
    out_ref[1] = x[parts // 2 :]


def run_final(tiles, own):
    _, parts, rows = own.shape
    vmem = pl.BlockSpec(memory_space=pltpu.VMEM)
    return pl.pallas_call(
        final_kernel,
        in_specs=[vmem] * 2,
        out_specs=[vmem] * 2,
        out_shape=[
            jax.ShapeDtypeStruct((2, parts // 2, rows), jnp.float32),
            jax.ShapeDtypeStruct((1, parts // 2), jnp.float32),
        ],
        name="final",
    )(tiles, own)


def make_shards(line, plane, freqs):
    def shards(excitation, g_blocks, c_blocks, pattern, counts, freq_ids):
        row_blocks, own_slots, size, _ = g_blocks.shape
        freq_count = excitation.shape[1]
        parts = 2 * freq_count
        where = jnp.stack([lax.axis_index(name) for name in ("line", "place", "freq")])
        last_row = jnp.concatenate([where, counts, freq_ids])
        scalars = jnp.concatenate(
            [
                jnp.pad(pattern, ((0, 0), (0, LANES - pattern.shape[1]))),
                jnp.pad(last_row, (0, LANES - last_row.size))[None],
            ]
        ).astype(jnp.int32)
        stored = (row_blocks * own_slots, size, size)
        g_own, c_own = g_blocks.reshape(stored), c_blocks.reshape(stored)
        *lists, turn, g_near, c_near = run_setup(
            scalars, pattern.shape, freq_count, g_own, c_own, line, plane, freqs
        )
        g_parts, c_parts = [g_near], [c_near]
        for d in range(1, freqs):
            perm = [(i, (i + d) % freqs) for i in range(freqs)]
            g_parts.append(lax.ppermute(g_own, "freq", perm))
            c_parts.append(lax.ppermute(c_own, "freq", perm))
        info = jnp.zeros((parts, LANES), jnp.float32)
        krylov = []
        rows = excitation
        blocks = g_parts + c_parts
        for step in range(ITERS):
            lines = gather_rows(rows, line, plane)
            result = run_step(step, lists, turn, info, lines, krylov, blocks, freqs)
            if step == ITERS - 1:
                own, info = result
            elif step == 0:
                z, rows, info, tiles = result
                blocks = [tiles]
                krylov.append(z)
            else:
                z, rows, info = result
                krylov.append(z)
        answer, residual = run_final(jnp.concatenate(gather_rows(info, line, plane)), own)
        return answer, residual.reshape(freq_count)

    return shards


def solution(mesh):
    line, plane = split_nodes(mesh.shape["node"])
    freqs = mesh.shape["freq"]
    fine = Mesh(mesh.devices.reshape(line, plane, freqs), ("line", "place", "freq"))
    node = ("line", "place")
    in_specs = (
        P(None, "freq", node),
        P(node, "freq", None, None),
        P(node, "freq", None, None),
        P(node, None),
        P(node),
        P("freq"),
    )
    out_specs = (P(None, "freq", node), P("freq"))
    shards = make_shards(line, plane, freqs)
    return jax.shard_map(shards, mesh=fine, in_specs=in_specs, out_specs=out_specs, check_vma=False)
```
